32 devices in a mesh: grp: 2 (over x), seq: 8 (over z, y), ten: 2 (over core).
Axes of the slice: x: 2, y: 2, z: 4, core: 2. Of those that a mesh axis runs over, the one named last changes fastest.
Arguments:
- queries: bfloat16 [1024, 4096], P(('grp', 'seq'), 'ten'), parts along dimension 0, may hold values from -128 to 128
- keys: bfloat16 [1024, 512], P(('grp', 'seq'), 'ten'), parts along dimension 0, may hold values from -6 to 6
- values: bfloat16 [1024, 512], P(('grp', 'seq'), 'ten'), parts along dimension 0, may hold values from -6 to 6
- hidden: bfloat16 [1024, 8192], P(('grp', 'seq')), parts along dimension 0, may hold values from -6 to 6
- norm_gain: float32 [8192], replicated, may hold values from 0.1 to 1.9
- retained_lists: int32 [1024], P(('grp', 'seq')), parts along dimension 0, may hold values from -1 to 63, as said below
- counts: int32 [16], P('grp'), parts along dimension 0, may hold values from 0 to 64, as said below
- affine_matrix: bfloat16 [8192, 5120], P('seq', 'ten'), may hold values from -0.0625 to 0.0625
- affine_offset_vector: float32 [5120], P('ten'), may hold values from -3 to 3
Outputs:
- context: float32 [1024, 4096], P(('grp', 'seq'), 'ten'), parts along dimension 0
- col_scores: float32 [1024], P(('grp', 'seq')), parts along dimension 0
- tier_third_mapped_triples: float32 [512, 5120], P(('grp', 'seq'), 'ten'), parts along dimension 0
The draws below stay inside these ranges and needn't reach their ends.
There are 2 independent parts, one for each index of `grp`. The reference program is written for one: setup_inputs(seed, part) draws one part's arguments, and reference() takes and returns one part's arrays. A program takes and returns all parts, laid end to end along the dimension named above; an argument that names none is the same for every part. Nothing has to cross between parts.
Inputs may be any that keep to these rules, and one draw needn't show every extreme that they name: `retained_lists`: entries s*64 to (s+1)*64 - 1 hold, in their first counts[s] places, the kept local rows of shard s in rising order, and -1 after them. counts sum to 256; some shard keeps all its 64 rows.
All inputs are finite; a program needn't handle non-finite values.
Results may differ from the reference program's by a relative error of at most 0.0027.
Values may be sent and summed in bfloat16 or wider, within the bound.
No kernel may reach another device: no remote copies, remote signals or barrier semaphores. Data moves between devices by JAX's collectives and lax.ppermute only.
A program may use at most 64 MiB of HBM per device.

```python
import math
import jax
import jax.numpy as jnp
from jax import lax

D = 8192
HEAD_SIZE = 128
QUERY_HEADS = 32
KEY_VALUE_HEADS = 4
QD = 64
QUERY_BLOCK_ROWS = 512
QKVW = 5120


def paired_draw(key):
    queries = jnp.clip(jax.random.normal(jax.random.fold_in(key, 101), (QUERY_BLOCK_ROWS, QUERY_HEADS * HEAD_SIZE), jnp.float32), -6.0, 6.0)
    keys = jnp.clip(jax.random.normal(jax.random.fold_in(key, 202), (QUERY_BLOCK_ROWS, KEY_VALUE_HEADS * HEAD_SIZE), jnp.float32), -6.0, 6.0)
    head_place = jnp.arange(QUERY_HEADS, dtype=jnp.float32) / max(QUERY_HEADS - 1, 1)
    jitter = jax.random.uniform(jax.random.fold_in(key, 505), (QUERY_HEADS,), jnp.float32, 0.85, 1.15)
    head_scale = 0.6 * jnp.exp(head_place * math.log(6.0)) * jitter
    queries = queries * jnp.repeat(head_scale, HEAD_SIZE)[None, :]
    queries = jnp.clip(queries, -128.0, 128.0)
    return (queries, keys)


def draw_queries(key, part):
    return paired_draw(key)[0].astype(jnp.bfloat16)


def draw_keys(key, part):
    return paired_draw(key)[1].astype(jnp.bfloat16)


def retained_sequence_pick(key):
    base = jax.random.fold_in(key, 404)
    shard_count = QUERY_BLOCK_ROWS // QD
    levels = jax.random.randint(jax.random.fold_in(base, 1), (shard_count,), 0, 4)
    full_shard = jax.random.randint(jax.random.fold_in(base, 2), (), 0, shard_count)
    levels = jnp.where(jnp.arange(shard_count, dtype=jnp.int32) == full_shard, 5, levels)
    noise = jax.random.randint(jax.random.fold_in(base, 3), (QUERY_BLOCK_ROWS,), 0, 1024)
    position = jnp.arange(QUERY_BLOCK_ROWS, dtype=jnp.int32)
    ranking = (jnp.repeat(levels, QD) * 1024 + noise) * QUERY_BLOCK_ROWS + position
    unused, picked = lax.top_k(ranking, QUERY_BLOCK_ROWS // 2)
    marked = jnp.zeros((QUERY_BLOCK_ROWS,), jnp.int32).at[picked].set(1).reshape(shard_count, QD)
    counts = jnp.sum(marked, axis=1).astype(jnp.int32)
    partition_inner_position = jnp.arange(QD, dtype=jnp.int32)
    order_key = (1 - marked) * QD + partition_inner_position[None, :]
    ordered = jnp.argsort(order_key, axis=1, stable=True).astype(jnp.int32)
    retained_lists = jnp.where(partition_inner_position[None, :] < counts[:, None], ordered, -1).reshape(QUERY_BLOCK_ROWS)
    return (retained_lists, counts)


def draw_retained_lists(key, part):
    return retained_sequence_pick(key)[0]


def draw_counts(key, part):
    return retained_sequence_pick(key)[1]


def shard_levels(stream_key, dims, split, smallest, largest):
    level, own = 1.0, jax.random.fold_in(stream_key, 6)
    for axis_at, blocks in split:
        heights = jnp.exp(jax.random.uniform(jax.random.fold_in(own, axis_at), (blocks,), jnp.float32, smallest / len(split), largest / len(split)))
        level = level * jnp.repeat(heights, dims[axis_at] // blocks).reshape([-1 if axis == axis_at else 1 for axis in range(len(dims))])
    return level


def gaussian(rng, extent, width, limit, pieces=(), kind=jnp.bfloat16):
    entries = jax.random.normal(rng, extent, jnp.float32) * width
    if len(pieces) > 0:
        entries = shard_levels(rng, extent, pieces, -0.22, 0.18) * entries
    return jnp.clip(entries, min=-limit, max=limit).astype(kind)


def setup_inputs(seed: int = 0, part: int = 0) -> dict:
    arg_keys = jax.random.split(jax.random.key(seed), 10)
    part_keys = jax.random.split(jax.random.fold_in(arg_keys[9], part), 10)
    return {
        "queries": draw_queries(jax.random.fold_in(jax.random.fold_in(arg_keys[9], part), 71), part),
        "keys": draw_keys(jax.random.fold_in(jax.random.fold_in(arg_keys[9], part), 71), part),
        "values": gaussian(part_keys[2], (QUERY_BLOCK_ROWS, KEY_VALUE_HEADS * HEAD_SIZE), 1.0, 6.0, ((0, 8), (1, 2))),
        "hidden": gaussian(part_keys[3], (QUERY_BLOCK_ROWS, D), 1.0, 6.0, ((0, 8),)),
        "norm_gain": jnp.clip(1.0 + 0.18 * jax.random.normal(arg_keys[4], (D,), jnp.float32), 0.1, 1.9),
        "retained_lists": draw_retained_lists(jax.random.fold_in(jax.random.fold_in(arg_keys[9], part), 71), part),
        "counts": draw_counts(jax.random.fold_in(jax.random.fold_in(arg_keys[9], part), 71), part),
        "affine_matrix": gaussian(arg_keys[7], (D, QKVW), D ** -0.5, 0.0625, ((0, 8), (1, 2))),
        "affine_offset_vector": gaussian(arg_keys[8], (QKVW,), 0.5, 3.0, ((0, 2),), jnp.float32),
    }


def reference(queries, keys, values, hidden, norm_gain, retained_lists, counts, affine_matrix, affine_offset_vector):
    asker_line_tile = queries.shape[0]
    group_width = QUERY_HEADS // KEY_VALUE_HEADS
    positions = jnp.arange(asker_line_tile, dtype=jnp.int32)
    allowed = positions[None, :] <= positions[:, None]
    query_heads = queries.reshape(asker_line_tile, QUERY_HEADS, HEAD_SIZE).transpose(1, 0, 2)
    key_head_rows = keys.reshape(asker_line_tile, KEY_VALUE_HEADS, HEAD_SIZE).transpose(1, 0, 2)
    value_head_rows = values.reshape(asker_line_tile, KEY_VALUE_HEADS, HEAD_SIZE).transpose(1, 0, 2)

    def one_head(head):
        kv_index = head // group_width
        query_one = lax.dynamic_index_in_dim(query_heads, head, 0, keepdims=False)
        key_one = lax.dynamic_index_in_dim(key_head_rows, kv_index, 0, keepdims=False)
        value_one = lax.dynamic_index_in_dim(value_head_rows, kv_index, 0, keepdims=False)
        scores = jnp.dot(query_one, key_one.T, preferred_element_type=jnp.float32) * HEAD_SIZE ** (-0.5)
        row_max = lax.optimization_barrier(jnp.max(jnp.where(allowed, scores, -1e+30), axis=1))
        weights = jnp.where(allowed, jnp.exp(scores - row_max[:, None]), 0.0)
        row_sum = lax.optimization_barrier(jnp.sum(weights, axis=1))
        mixed = jnp.dot(weights.astype(jnp.bfloat16), value_one, preferred_element_type=jnp.float32) / row_sum[:, None]
        column = lax.optimization_barrier(jnp.sum(weights / row_sum[:, None], axis=0))
        return (mixed, column)
    mixed_all, columns = lax.map(one_head, jnp.arange(QUERY_HEADS, dtype=jnp.int32))
    context = mixed_all.transpose(1, 0, 2).reshape(asker_line_tile, QUERY_HEADS * HEAD_SIZE)
    col_scores = lax.optimization_barrier(jnp.sum(columns, axis=0)) / QUERY_HEADS
    hidden_f = hidden.astype(jnp.float32)
    rescaled_activations = (hidden_f * lax.rsqrt(lax.optimization_barrier(jnp.mean(hidden_f * hidden_f, axis=1, keepdims=True)) + 1e-06) * norm_gain).astype(jnp.bfloat16)
    shard_count = counts.shape[0]
    partition_inner_lines = asker_line_tile // shard_count
    retained_total = asker_line_tile // 2
    retained_element = jnp.arange(retained_total, dtype=jnp.int32)
    partition_finish_marks = jnp.cumsum(counts).astype(jnp.int32)
    holder_partition = lax.optimization_barrier(jnp.sum((partition_finish_marks[None, :] <= retained_element[:, None]).astype(jnp.int32), axis=1))
    starts = partition_finish_marks - counts
    opening_marks = lax.optimization_barrier(jnp.sum(jnp.where(jnp.arange(shard_count, dtype=jnp.int32)[None, :] == holder_partition[:, None], starts[None, :], 0), axis=1))
    retained_place_number = retained_element - opening_marks
    partition_inner_position = retained_lists[holder_partition * partition_inner_lines + retained_place_number]
    retained_elements = rescaled_activations[holder_partition * partition_inner_lines + partition_inner_position]
    tier_third_mapped_triples = jnp.dot(retained_elements, affine_matrix, preferred_element_type=jnp.float32) + affine_offset_vector
    return (context, col_scores, tier_third_mapped_triples)
```

```python
import functools

import jax
import jax.numpy as jnp
from jax import lax
from jax.experimental import pallas as pl
from jax.experimental.pallas import tpu as pltpu
from jax.sharding import PartitionSpec as P

HEAD_SIZE = 128
QUERY_HEADS = 32
VMEM = pl.BlockSpec(memory_space=pltpu.VMEM)
SMEM = pl.BlockSpec(memory_space=pltpu.SMEM)
PARAMS = pltpu.CompilerParams(vmem_limit_bytes=48 * 1024 * 1024)


def norm_select_kernel(n, place, hidden, gain, kept, *outs):
    rows, width = hidden.shape
    block = width // n
    half = block // 2
    s, t = place[0], place[1]
    total = jnp.zeros((rows, block), jnp.float32)
    for i in range(n):
        part = hidden[:, i * block : (i + 1) * block].astype(jnp.float32)
        total += part * part
    scale = lax.rsqrt(jnp.sum(total, axis=1, keepdims=True) / width + 1e-06)
    selector = (kept[...] == lax.broadcasted_iota(jnp.int32, (rows, rows), 0)).astype(jnp.bfloat16)
    for k in range(n):
        start = pl.multiple_of(lax.rem(s + k, n) * block + t * half, half)
        columns = pl.ds(start, half)
        normed = (hidden[:, columns].astype(jnp.float32) * scale * gain[:, columns]).astype(jnp.bfloat16)
        outs[k][...] = lax.dot_general(
            selector, normed, (((0,), (0,)), ((), ())), preferred_element_type=jnp.float32
        ).astype(jnp.bfloat16)


def attention_kernel(n, kv_heads, place, queries, *refs):
    blocks, (context, columns) = refs[:n], refs[n:]
    rows = queries.shape[0]
    group = queries.shape[1] // (HEAD_SIZE * kv_heads)
    s = place[0]
    keys_total = n * rows
    row = lax.broadcasted_iota(jnp.int32, (rows, keys_total), 0)
    column = lax.broadcasted_iota(jnp.int32, (rows, keys_total), 1)
    diagonal = (column <= row) & (column < rows)
    earlier = (column >= rows) & (column < (s + 1) * rows)
    allowed = diagonal | earlier
    sums = jnp.zeros((1, keys_total), jnp.float32)
    for g in range(kv_heads):
        key = jnp.concatenate([b[:, g * HEAD_SIZE : (g + 1) * HEAD_SIZE] for b in blocks], axis=0)
        first = (kv_heads + g) * HEAD_SIZE
        value = jnp.concatenate([b[:, first : first + HEAD_SIZE] for b in blocks], axis=0)
        for h in range(g * group, (g + 1) * group):
            lanes = slice(h * HEAD_SIZE, (h + 1) * HEAD_SIZE)
            scores = lax.dot_general(
                queries[:, lanes], key, (((1,), (1,)), ((), ())), preferred_element_type=jnp.float32
            ) * HEAD_SIZE ** (-0.5)
            scores = jnp.where(allowed, scores, -1e30)
            row_max = jnp.max(scores, axis=1, keepdims=True)
            weights = jnp.where(allowed, jnp.exp(scores - row_max), 0.0)
            inverse = 1.0 / jnp.sum(weights, axis=1, keepdims=True)
            mixed = jnp.dot(weights.astype(jnp.bfloat16), value, preferred_element_type=jnp.float32)
            context[:, lanes] = mixed * inverse
            sums += jnp.sum(weights * inverse, axis=0, keepdims=True)
    columns[...] = sums


def compact_kernel(n, place, counts, *refs):
    blocks, out = refs[:n], refs[n]
    rows = blocks[0].shape[0]
    survivors = out.shape[0]
    s = place[0]
    slot_all = lax.broadcasted_iota(jnp.int32, (1, n * rows), 1)
    target = jnp.full((1, n * rows), -1, jnp.int32)
    for k in range(n):
        source = lax.rem(s - k + n, n)
        begin = jnp.int32(0)
        for i in range(n):
            begin += jnp.where(i < source, counts[i], 0)
        slot = slot_all - k * rows
        inside = (slot >= 0) & (slot < counts[source])
        target = jnp.where(inside, begin + slot, target)
    survivor = lax.broadcasted_iota(jnp.int32, (survivors, n * rows), 0) + s * (survivors // n)
    survivor = jnp.where(survivor >= survivors, survivor - survivors, survivor)
    pick = (survivor == target).astype(jnp.float32).astype(jnp.bfloat16)
    received = jnp.concatenate([b[...] for b in blocks], axis=0)
    out[...] = jnp.dot(pick, received, preferred_element_type=jnp.float32).astype(jnp.bfloat16)


def project_kernel(n, place, own, other, matrix, columns, columns_other, own_part, own_columns, *sent):
    outs = (None,) + sent
    t = place[1]
    survivors, half = own.shape
    width = matrix.shape[1]
    lines = survivors // n
    rows = columns.shape[1] // n
    first = t == 0
    low = jnp.where(first, own[...], other[...])
    high = jnp.where(first, other[...], own[...])
    features = jnp.concatenate([low, high], axis=1)
    tile = width // 5 if width % 640 == 0 else width
    for c in range(width // tile):
        lanes = slice(c * tile, (c + 1) * tile)
        part = jnp.dot(features, matrix[:, lanes], preferred_element_type=jnp.float32)
        own_part[:, lanes] = part[:lines]
        for k in range(1, n):
            outs[k][:, lanes] = part[k * lines : (k + 1) * lines].astype(jnp.bfloat16)
    total = columns[...] + columns_other[...]
    own_columns[...] = total[:, :rows]
    for k in range(1, n):
        j = n - k
        piece = total[:, j * rows : (j + 1) * rows]
        head = piece.astype(jnp.bfloat16)
        tail = (piece - head.astype(jnp.float32)).astype(jnp.bfloat16)
        outs[k][:, width : width + rows] = jnp.broadcast_to(head, (lines, rows))
        outs[k][:, width + rows :] = jnp.broadcast_to(tail, (lines, rows))


def finish_kernel(n, own, own_columns, bias, *refs):
    received, (out, scores) = refs[: n - 1], refs[n - 1 :]
    width = own.shape[1]
    rows = own_columns.shape[1]
    total = own[...]
    sums = own_columns[...]
    for r in received:
        total += r[:, :width].astype(jnp.float32)
        extra = r[:16, width:].astype(jnp.float32)
        sums += extra[:1, :rows] + extra[:1, rows:]
    out[...] = total + bias[...]
    scores[...] = sums / QUERY_HEADS


def shards(queries, keys, values, hidden, norm_gain, retained_lists, counts, affine_matrix, affine_offset_vector):
    n = lax.axis_size("seq")
    rows, model = hidden.shape
    kv_heads = keys.shape[1] // HEAD_SIZE
    half = affine_matrix.shape[0] // 2
    width = affine_matrix.shape[1]
    survivors = n * rows // 2
    lines = survivors // n
    s, t = lax.axis_index("seq"), lax.axis_index("ten")
    place = jnp.stack([s, t]).astype(jnp.int32)
    f32, bf16 = jnp.float32, jnp.bfloat16
    shape = jax.ShapeDtypeStruct

    def shift(x, k):
        return lax.ppermute(x, "seq", [(i, (i + k) % n) for i in range(n)])

    def swap(x):
        return lax.ppermute(x, "ten", [(0, 1), (1, 0)])

    pair = jnp.concatenate([keys, values], axis=1)
    pairs = [pair] + [shift(pair, k) for k in range(1, n)]

    chosen = pl.pallas_call(
        functools.partial(norm_select_kernel, n),
        out_shape=[shape((rows, half), bf16)] * n,
        in_specs=[SMEM, VMEM, VMEM, VMEM],
        out_specs=[VMEM] * n,
        compiler_params=PARAMS,
        cost_estimate=pl.CostEstimate(flops=4 * rows * model, bytes_accessed=3 * rows * model, transcendentals=0),
        name="norm_select",
    )(place, hidden, norm_gain.reshape(1, model), retained_lists.reshape(1, rows))
    received = [chosen[0]] + [shift(chosen[k], k) for k in range(1, n)]

    context, columns = pl.pallas_call(
        functools.partial(attention_kernel, n, kv_heads),
        out_shape=[shape(queries.shape, f32), shape((1, n * rows), f32)],
        in_specs=[SMEM, VMEM] + [VMEM] * n,
        out_specs=[VMEM] * 2,
        compiler_params=PARAMS,
        cost_estimate=pl.CostEstimate(
            flops=4 * rows * n * rows * queries.shape[1], bytes_accessed=6 * rows * queries.shape[1], transcendentals=0
        ),
        name="attention",
    )(place, queries, *pairs)
    columns_other = swap(columns)

    own = pl.pallas_call(
        functools.partial(compact_kernel, n),
        out_shape=shape((survivors, half), bf16),
        in_specs=[SMEM, SMEM] + [VMEM] * n,
        out_specs=VMEM,
        compiler_params=PARAMS,
        cost_estimate=pl.CostEstimate(flops=2 * survivors * n * rows * half, bytes_accessed=4 * n * rows * half, transcendentals=0),
        name="compact",
    )(place, counts, *received)
    other = swap(own)

    own_part, own_columns, *partial_sums = pl.pallas_call(
        functools.partial(project_kernel, n),
        out_shape=[shape((lines, width), f32), shape((1, rows), f32)]
        + [shape((lines, width + 2 * rows), bf16)] * (n - 1),
        in_specs=[SMEM] + [VMEM] * 5,
        out_specs=[VMEM] * (n + 1),
        compiler_params=PARAMS,
        cost_estimate=pl.CostEstimate(
            flops=4 * survivors * half * width, bytes_accessed=4 * half * width + 2 * survivors * width, transcendentals=0
        ),
        name="project",
    )(place, own, other, affine_matrix, columns, columns_other)
    arrived = [shift(partial_sums[k - 1], k) for k in range(1, n)]

    triples, scores = pl.pallas_call(
        functools.partial(finish_kernel, n),
        out_shape=[shape((lines, width), f32), shape((1, rows), f32)],
        in_specs=[VMEM] * (n + 2),
        out_specs=[VMEM] * 2,
        compiler_params=PARAMS,
        cost_estimate=pl.CostEstimate(flops=n * lines * width, bytes_accessed=2 * n * lines * width, transcendentals=0),
        name="finish",
    )(own_part, own_columns, affine_offset_vector.reshape(1, width), *arrived)
    return (context, scores.reshape(rows), triples)


def solution(mesh):
    in_specs = (
        P(("grp", "seq"), "ten"),
        P(("grp", "seq"), "ten"),
        P(("grp", "seq"), "ten"),
        P(("grp", "seq"), None),
        P(),
        P(("grp", "seq")),
        P("grp"),
        P("seq", "ten"),
        P("ten"),
    )
    out_specs = (P(("grp", "seq"), "ten"), P(("grp", "seq")), P(("grp", "seq"), "ten"))
    return jax.shard_map(shards, mesh=mesh, in_specs=in_specs, out_specs=out_specs, check_vma=False)
```

```python
import functools

import jax
import jax.numpy as jnp
from jax import lax
from jax.experimental import pallas as pl
from jax.experimental.pallas import tpu as pltpu
from jax.sharding import PartitionSpec as P

HEAD_SIZE = 128
QUERY_HEADS = 32
CHUNKS = 2
VMEM = pl.BlockSpec(memory_space=pltpu.VMEM)
SMEM = pl.BlockSpec(memory_space=pltpu.SMEM)
ANY = pl.BlockSpec(memory_space=pl.ANY)
PARAMS = pltpu.CompilerParams(vmem_limit_bytes=16 * 1024 * 1024)


def norm_select_kernel(n, place, hidden_in, gain_in, kept_in, keys_in, values_in, pair, *refs):
    outs, (hidden, gain, kept, sems) = refs[:n], refs[n:]
    rows, width = hidden.shape
    block = width // n
    half = block // 2
    pieces = 4
    piece = width // pieces
    loads = [
        pltpu.make_async_copy(
            hidden_in.at[:, i * piece : (i + 1) * piece], hidden.at[:, i * piece : (i + 1) * piece], sems.at[i]
        )
        for i in range(pieces)
    ]
    key_width = keys_in.shape[1]
    loads += [
        pltpu.make_async_copy(gain_in, gain, sems.at[pieces]),
        pltpu.make_async_copy(kept_in, kept, sems.at[pieces + 1]),
        pltpu.make_async_copy(keys_in, pair.at[:, :key_width], sems.at[pieces + 2]),
        pltpu.make_async_copy(values_in, pair.at[:, key_width:], sems.at[pieces + 3]),
    ]
    for load in loads:
        load.start()
    s, t = place[0], place[1]
    step = min(piece, 1024)
    total = jnp.zeros((rows, step), jnp.float32)
    for i in range(pieces):
        loads[i].wait()
        for j in range(i * piece, (i + 1) * piece, step):
            part = hidden[:, j : j + step].astype(jnp.float32)
            total += part * part
    scale = lax.rsqrt(jnp.sum(total, axis=1, keepdims=True) / width + 1e-06)
    for load in loads[pieces:]:
        load.wait()
    selector = (kept[...] == lax.broadcasted_iota(jnp.int32, (rows, rows), 0)).astype(jnp.bfloat16)
    for k in range(n):
        start = pl.multiple_of(lax.bitwise_xor(s, k) * block + t * half, half)
        columns = pl.ds(start, half)
        normed = (hidden[:, columns].astype(jnp.float32) * scale * gain[:, columns]).astype(jnp.bfloat16)
        outs[k][...] = lax.dot_general(
            selector, normed, (((0,), (0,)), ((), ())), preferred_element_type=jnp.float32
        ).astype(jnp.bfloat16)


def attention_kernel(n, kv_heads, order, place, queries, held, context, columns):
    rows = queries.shape[0]
    group = queries.shape[1] // (HEAD_SIZE * kv_heads)
    s = place[0]
    keys_total = n * rows
    column = lax.broadcasted_iota(jnp.int32, (1, keys_total), 1)
    position = column
    for at, k in enumerate(order):
        inside = (column >= at * rows) & (column < (at + 1) * rows)
        position = jnp.where(inside, column + (lax.bitwise_xor(s, k) - s - at) * rows, position)
    allowed = position <= lax.broadcasted_iota(jnp.int32, (rows, keys_total), 0)
    sums = jnp.zeros((1, keys_total), jnp.float32)
    for g in range(kv_heads):
        key = held[:, g * HEAD_SIZE : (g + 1) * HEAD_SIZE]
        value = held[:, (kv_heads + g) * HEAD_SIZE : (kv_heads + g + 1) * HEAD_SIZE]
        for h in range(g * group, (g + 1) * group):
            lanes = slice(h * HEAD_SIZE, (h + 1) * HEAD_SIZE)
            scores = lax.dot_general(
                queries[:, lanes], key, (((1,), (1,)), ((), ())), preferred_element_type=jnp.float32
            ) * HEAD_SIZE ** (-0.5)
            scores = jnp.where(allowed, scores, -1e30)
            row_max = jnp.max(scores, axis=1, keepdims=True)
            weights = jnp.where(allowed, jnp.exp(scores - row_max), 0.0)
            inverse = 1.0 / jnp.sum(weights, axis=1, keepdims=True)
            mixed = jnp.dot(weights.astype(jnp.bfloat16), value, preferred_element_type=jnp.float32)
            context[:, lanes] = mixed * inverse
            sums += jnp.sum(weights * inverse, axis=0, keepdims=True)
    for at, k in enumerate(order):
        columns[k : k + 1, :] = sums[:, at * rows : (at + 1) * rows]


def compact_kernel(n, owners, place, counts, *refs):
    blocks, out = refs[:n], refs[n]
    rows = blocks[0].shape[0]
    survivors = out.shape[0]
    lines = survivors // n
    s = place[0]
    slot_all = lax.broadcasted_iota(jnp.int32, (1, n * rows), 1)
    target = jnp.full((1, n * rows), -1, jnp.int32)
    for k in range(n):
        source = lax.bitwise_xor(s, k)
        begin = jnp.int32(0)
        for i in range(n):
            begin += jnp.where(i < source, counts[i], 0)
        slot = slot_all - k * rows
        inside = (slot >= 0) & (slot < counts[source])
        target = jnp.where(inside, begin + slot, target)
    line = lax.broadcasted_iota(jnp.int32, (lines, n * rows), 0)
    received = jnp.concatenate([b[...] for b in blocks], axis=0)
    pick = jnp.concatenate(
        [(line + lax.bitwise_xor(s, k) * lines == target).astype(jnp.float32) for k in owners], axis=0
    ).astype(jnp.bfloat16)
    out[...] = jnp.dot(pick, received, preferred_element_type=jnp.float32).astype(jnp.bfloat16)


def project_kernel(place, own, other, matrix, *outs):
    survivors, half = own.shape
    near = survivors // 2
    first = place[1] == 0
    low = jnp.where(first, own[...], other[...])
    high = jnp.where(first, other[...], own[...])
    features = jnp.concatenate([low, high], axis=1)
    for c in range(CHUNKS):
        width = outs[2 * c].shape[1]
        tile = width // 2 if width % 256 == 0 else width
        for j in range(0, width, tile):
            lanes = slice(c * width + j, c * width + j + tile)
            part = jnp.dot(features, matrix[:, lanes], preferred_element_type=jnp.float32)
            outs[2 * c][:, j : j + tile] = part[:near]
            outs[2 * c + 1][:, j : j + tile] = part[near:].astype(jnp.bfloat16)


def pair_kernel(kept, received, own, *outs):
    lines = own.shape[0]
    own[...] = kept[:lines] + received[:lines].astype(jnp.float32)
    for i, out in enumerate(outs):
        at = slice((i + 1) * lines, (i + 2) * lines)
        out[...] = (kept[at] + received[at].astype(jnp.float32)).astype(jnp.bfloat16)


def finish_kernel(bias, *refs):
    *parts, out = refs
    per_chunk = len(parts) // CHUNKS
    width = parts[0].shape[1]
    for c in range(CHUNKS):
        own, *received = parts[c * per_chunk : (c + 1) * per_chunk]
        total = own[...]
        for r in received:
            total += r[...].astype(jnp.float32)
        lanes = slice(c * width, (c + 1) * width)
        out[:, lanes] = total + bias[:, lanes]


def shards(queries, keys, values, hidden, norm_gain, retained_lists, counts, affine_matrix, affine_offset_vector):
    n = lax.axis_size("seq")
    rows, model = hidden.shape
    kv_heads = keys.shape[1] // HEAD_SIZE
    half = affine_matrix.shape[0] // 2
    width = affine_matrix.shape[1]
    survivors = n * rows // 2
    lines = survivors // n
    chunk = width // CHUNKS
    s, t = lax.axis_index("seq"), lax.axis_index("ten")
    place = jnp.stack([s, t]).astype(jnp.int32)
    f32, bf16 = jnp.float32, jnp.bfloat16
    shape = jax.ShapeDtypeStruct

    def trade(x, k):
        return lax.ppermute(x, "seq", [(i, i ^ k) for i in range(n)])

    def swap(x):
        return lax.ppermute(x, "ten", [(0, 1), (1, 0)])

    def cost(flops, size):
        return pl.CostEstimate(flops=flops, bytes_accessed=size, transcendentals=0)

    pair, *chosen = pl.pallas_call(
        functools.partial(norm_select_kernel, n),
        out_shape=[shape((rows, 2 * keys.shape[1]), bf16)] + [shape((rows, half), bf16)] * n,
        in_specs=[SMEM] + [ANY] * 5,
        out_specs=[VMEM] * (n + 1),
        scratch_shapes=[
            pltpu.VMEM((rows, model), bf16),
            pltpu.VMEM((1, model), f32),
            pltpu.VMEM((1, rows), jnp.int32),
            pltpu.SemaphoreType.DMA((8,)),
        ],
        compiler_params=PARAMS,
        cost_estimate=cost(4 * rows * model, 3 * rows * model),
        name="norm_select",
    )(place, hidden, norm_gain.reshape(1, model), retained_lists.reshape(1, rows), keys, values)
    received = [chosen[0]] + [trade(chosen[k], k) for k in range(1, n)]

    masks = [1 << i for i in range(1, n.bit_length() - 1)] + [1]
    held, order = pair, [0]
    for mask in masks:
        held = jnp.concatenate([held, trade(held, mask)], axis=0)
        order = order + [k ^ mask for k in order]
    context, columns = pl.pallas_call(
        functools.partial(attention_kernel, n, kv_heads, order),
        out_shape=[shape(queries.shape, f32), shape((n, rows), f32)],
        in_specs=[SMEM, VMEM, VMEM],
        out_specs=[VMEM] * 2,
        compiler_params=PARAMS,
        cost_estimate=cost(4 * rows * n * rows * queries.shape[1], 6 * rows * queries.shape[1]),
        name="attention",
    )(place, queries, held)
    mask = n // 2
    while mask:
        columns = columns[:mask] + trade(columns[mask:], mask)
        mask //= 2
    scores = (columns + swap(columns)).reshape(rows) / QUERY_HEADS

    owners = list(range(0, n, 2)) + list(range(1, n, 2))
    own = pl.pallas_call(
        functools.partial(compact_kernel, n, owners),
        out_shape=shape((survivors, half), bf16),
        in_specs=[SMEM, SMEM] + [VMEM] * n,
        out_specs=VMEM,
        compiler_params=PARAMS,
        cost_estimate=cost(2 * survivors * n * rows * half, 4 * n * rows * half),
        name="compact",
    )(place, counts, *received)
    other = swap(own)

    partial_sums = pl.pallas_call(
        project_kernel,
        out_shape=[shape((survivors // 2, chunk), f32), shape((survivors // 2, chunk), bf16)] * CHUNKS,
        in_specs=[SMEM] + [VMEM] * 3,
        out_specs=[VMEM] * (2 * CHUNKS),
        compiler_params=PARAMS,
        cost_estimate=cost(4 * survivors * half * width, 4 * half * width + 6 * survivors * width),
        name="project",
    )(place, own, other, affine_matrix)

    parts = []
    for c in range(CHUNKS):
        mine, *sent = pl.pallas_call(
            pair_kernel,
            out_shape=[shape((lines, chunk), f32)] + [shape((lines, chunk), bf16)] * (n // 2 - 1),
            in_specs=[VMEM] * 2,
            out_specs=[VMEM] * (n // 2),
            compiler_params=PARAMS,
            cost_estimate=cost(survivors * chunk, 3 * survivors * chunk),
            name="pair_sum",
        )(partial_sums[2 * c], trade(partial_sums[2 * c + 1], 1))
        parts += [mine] + [trade(sent[i], 2 * (i + 1)) for i in range(n // 2 - 1)]

    triples = pl.pallas_call(
        finish_kernel,
        out_shape=shape((lines, width), f32),
        in_specs=[VMEM] * (len(parts) + 1),
        out_specs=VMEM,
        compiler_params=PARAMS,
        cost_estimate=cost(n * lines * width, 2 * n * lines * width),
        name="finish",
    )(affine_offset_vector.reshape(1, width), *parts)
    return (context, scores, triples)


def solution(mesh):
    in_specs = (
        P(("grp", "seq"), "ten"),
        P(("grp", "seq"), "ten"),
        P(("grp", "seq"), "ten"),
        P(("grp", "seq"), None),
        P(),
        P(("grp", "seq")),
        P("grp"),
        P("seq", "ten"),
        P("ten"),
    )
    out_specs = (P(("grp", "seq"), "ten"), P(("grp", "seq")), P(("grp", "seq"), "ten"))
    return jax.shard_map(shards, mesh=mesh, in_specs=in_specs, out_specs=out_specs, check_vma=False)
```

```python
import functools
import math

import jax
import jax.numpy as jnp
from jax import lax
from jax.experimental import pallas as pl
from jax.experimental.pallas import tpu as pltpu
from jax.sharding import PartitionSpec as P

HEAD_SIZE = 128
QUERY_HEADS = 32
VMEM = pl.BlockSpec(memory_space=pltpu.VMEM)
ANY = pl.BlockSpec(memory_space=pl.ANY)
MIB = 1024 * 1024


def call(body, name, inputs, outputs, flops, limit=16, in_specs=None, scratch=(), remote=0):
    inputs = [pltpu.with_memory_space_constraint(x, pltpu.HBM) if i < remote else x for i, x in enumerate(inputs)]
    size = sum(math.prod(x.shape) * x.dtype.itemsize for x in list(inputs) + list(outputs))
    return pl.pallas_call(
        body,
        out_shape=list(outputs),
        in_specs=in_specs or [VMEM] * len(inputs),
        out_specs=[VMEM] * len(outputs),
        scratch_shapes=list(scratch),
        compiler_params=pltpu.CompilerParams(vmem_limit_bytes=limit * MIB),
        cost_estimate=pl.CostEstimate(flops=flops, bytes_accessed=size, transcendentals=0),
        name=name,
    )(*inputs)


def norm_select_kernel(n, hidden_in, gain_in, kept_in, keys_in, values_in, pair, *refs):
    outs, (hidden, gain, kept, sems) = refs[:n], refs[n:]
    rows, width = hidden.shape
    block = width // n
    half = block // 2
    pieces = 4
    piece = width // pieces
    key_width = keys_in.shape[1]
    loads = [
        pltpu.make_async_copy(
            hidden_in.at[:, i * piece : (i + 1) * piece], hidden.at[:, i * piece : (i + 1) * piece], sems.at[i]
        )
        for i in range(pieces)
    ]
    loads += [
        pltpu.make_async_copy(gain_in, gain, sems.at[pieces]),
        pltpu.make_async_copy(kept_in, kept, sems.at[pieces + 1]),
        pltpu.make_async_copy(keys_in, pair.at[:, :key_width], sems.at[pieces + 2]),
        pltpu.make_async_copy(values_in, pair.at[:, key_width:], sems.at[pieces + 3]),
    ]
    for load in loads:
        load.start()
    s, t = lax.axis_index("seq"), lax.axis_index("ten")
    step = min(piece, 1024)
    total = jnp.zeros((rows, step), jnp.float32)
    for i in range(pieces):
        loads[i].wait()
        for j in range(i * piece, (i + 1) * piece, step):
            part = hidden[:, j : j + step].astype(jnp.float32)
            total += part * part
    scale = lax.rsqrt(jnp.sum(total, axis=1, keepdims=True) / width + 1e-06)
    for load in loads[pieces:]:
        load.wait()
    selector = (kept[...] == lax.broadcasted_iota(jnp.int32, (rows, rows), 0)).astype(jnp.bfloat16)
    for k in range(n):
        start = pl.multiple_of(lax.bitwise_xor(s, k) * block + t * half, half)
        columns = pl.ds(start, half)
        normed = (hidden[:, columns].astype(jnp.float32) * scale * gain[:, columns]).astype(jnp.bfloat16)
        outs[k][...] = lax.dot_general(
            selector, normed, (((0,), (0,)), ((), ())), preferred_element_type=jnp.float32
        ).astype(jnp.bfloat16)


def stage_kernel(n, counts_in, matrix_in, queries_in, pair, pair_other, *refs):
    matrix, queries, held, target, counts, sems = refs[n // 2 :]
    loads = [
        pltpu.make_async_copy(counts_in, counts, sems.at[0]),
        pltpu.make_async_copy(matrix_in, matrix, sems.at[1]),
        pltpu.make_async_copy(queries_in, queries, sems.at[2]),
    ]
    for load in loads:
        load.start()
    rows = pair.shape[0]
    held[:rows] = pair[...]
    held[rows:] = pair_other[...]
    s = lax.axis_index("seq")
    loads[0].wait()
    slot_all = lax.broadcasted_iota(jnp.int32, (1, n * rows), 1)
    found = jnp.full((1, n * rows), -1, jnp.int32)
    for k in range(n):
        source = lax.bitwise_xor(s, k)
        begin = jnp.int32(0)
        for i in range(n):
            begin += jnp.where(i < source, counts[i], 0)
        slot = slot_all - k * rows
        inside = (slot >= 0) & (slot < counts[source])
        found = jnp.where(inside, begin + slot, found)
    target[...] = found
    for load in loads[1:]:
        load.wait()


def compact_kernel(n, owners, target, *refs):
    blocks, out = refs[:n], refs[n]
    lines = out.shape[0] // n
    s = lax.axis_index("seq")
    received = jnp.concatenate([b[...] for b in blocks], axis=0)
    line = lax.broadcasted_iota(jnp.int32, (lines, received.shape[0]), 0)
    pick = jnp.concatenate(
        [(line + lax.bitwise_xor(s, k) * lines == target[...]).astype(jnp.float32) for k in owners], axis=0
    ).astype(jnp.bfloat16)
    out[...] = jnp.dot(pick, received, preferred_element_type=jnp.float32).astype(jnp.bfloat16)


def project_kernel(first, own, other, matrix, near, far):
    survivors, half = own.shape
    lines = survivors // 2
    width = near.shape[1]
    t = lax.axis_index("ten")
    mine = pl.ds(pl.multiple_of(t * half, half), half)
    others = pl.ds(pl.multiple_of((1 - t) * half, half), half)
    tile = width // 2 if width % 256 == 0 else width
    for j in range(0, width, tile):
        lanes = slice(first + j, first + j + tile)
        part = jnp.dot(own[...], matrix[mine, lanes], preferred_element_type=jnp.float32)
        part += jnp.dot(other[...], matrix[others, lanes], preferred_element_type=jnp.float32)
        near[:, j : j + tile] = part[:lines]
        far[:, j : j + tile] = part[lines:].astype(jnp.bfloat16)


def pair_sum_kernel(kept, received, next_in, after, own, next_out, *outs):
    lines = own.shape[0]
    own[...] = kept[:lines] + received[:lines].astype(jnp.float32)
    for i, out in enumerate(outs):
        at = slice((i + 1) * lines, (i + 2) * lines)
        out[...] = (kept[at] + received[at].astype(jnp.float32)).astype(jnp.bfloat16)
    next_out[...] = next_in[...]


def total_of(own, received):
    total = own[...]
    for r in received:
        total += r[...].astype(jnp.float32)
    return total


def pair_sum_last_kernel(n, kept, received, columns, columns_other, *refs):
    chunk_parts, (done, own, own_columns, *outs) = refs[: n // 2], refs[n // 2 :]
    lines, width = own.shape
    done[...] = total_of(chunk_parts[0], chunk_parts[1:])
    rows = columns.shape[1]
    own[...] = kept[:lines] + received[:lines].astype(jnp.float32)
    own_columns[...] = columns[:1] + columns_other[:1]
    for i, out in enumerate(outs):
        at = slice((i + 1) * lines, (i + 2) * lines)
        out[:, :width] = (kept[at] + received[at].astype(jnp.float32)).astype(jnp.bfloat16)
        total = columns[i + 1 : i + 2] + columns_other[i + 1 : i + 2]
        head = total.astype(jnp.bfloat16).astype(jnp.float32)
        extra = jnp.concatenate([head, total - head], axis=1).astype(jnp.bfloat16)
        out[:, width:] = jnp.broadcast_to(extra, (lines, 2 * rows))


def attention_kernel(n, kv_heads, order, owners, queries, held_a, held_b, after, context, columns):
    rows = queries.shape[0]
    group = queries.shape[1] // (HEAD_SIZE * kv_heads)
    s = lax.axis_index("seq")
    keys_total = n * rows
    column = lax.broadcasted_iota(jnp.int32, (1, keys_total), 1)
    position = column
    for at, k in enumerate(order):
        inside = (column >= at * rows) & (column < (at + 1) * rows)
        position = jnp.where(inside, column + (lax.bitwise_xor(s, k) - s - at) * rows, position)
    row = lax.rem(lax.broadcasted_iota(jnp.int32, (group * rows, keys_total), 0), rows)
    allowed = position <= row
    sums = jnp.zeros((1, keys_total), jnp.float32)
    for g in range(kv_heads):
        key_lanes = slice(g * HEAD_SIZE, (g + 1) * HEAD_SIZE)
        value_lanes = slice((kv_heads + g) * HEAD_SIZE, (kv_heads + g + 1) * HEAD_SIZE)
        key = jnp.concatenate([held_a[:, key_lanes], held_b[:, key_lanes]], axis=0)
        value = jnp.concatenate([held_a[:, value_lanes], held_b[:, value_lanes]], axis=0)
        heads = range(g * group, (g + 1) * group)
        stacked = jnp.concatenate([queries[:, h * HEAD_SIZE : (h + 1) * HEAD_SIZE] for h in heads], axis=0)
        scores = lax.dot_general(
            stacked, key, (((1,), (1,)), ((), ())), preferred_element_type=jnp.float32
        ) * HEAD_SIZE ** (-0.5)
        scores = jnp.where(allowed, scores, -1e30)
        weights = jnp.exp(scores - jnp.max(scores, axis=1, keepdims=True))
        inverse = 1.0 / jnp.sum(weights, axis=1, keepdims=True)
        mixed = jnp.dot(weights.astype(jnp.bfloat16), value, preferred_element_type=jnp.float32) * inverse
        for i, h in enumerate(heads):
            context[:, h * HEAD_SIZE : (h + 1) * HEAD_SIZE] = mixed[i * rows : (i + 1) * rows]
        sums += jnp.sum(weights * inverse, axis=0, keepdims=True)
    for at, k in enumerate(order):
        i = owners.index(k)
        columns[i : i + 1, :] = sums[:, at * rows : (at + 1) * rows]


def finish_kernel(bias, done, own_columns, own, *refs):
    *received, out, scores = refs
    width = own.shape[1]
    rows = own_columns.shape[1]
    out[:, :width] = done[...] + bias[:, :width]
    out[:, width:] = total_of(own, [r.at[:, :width] for r in received]) + bias[:, width:]
    sums = own_columns[...]
    for r in received:
        extra = r[:16, width:].astype(jnp.float32)
        sums += extra[:1, :rows] + extra[:1, rows:]
    scores[...] = sums / QUERY_HEADS


def shards(queries, keys, values, hidden, norm_gain, retained_lists, counts, affine_matrix, affine_offset_vector):
    n = lax.axis_size("seq")
    rows, model = hidden.shape
    kv_heads = keys.shape[1] // HEAD_SIZE
    half = affine_matrix.shape[0] // 2
    width = affine_matrix.shape[1]
    survivors = n * rows // 2
    lines = survivors // n
    chunk = width // 2
    near = survivors // 2
    owners = list(range(0, n, 2)) + list(range(1, n, 2))
    f32, bf16, i32 = jnp.float32, jnp.bfloat16, jnp.int32
    shape = jax.ShapeDtypeStruct
    dma = pltpu.SemaphoreType.DMA

    def trade(x, k):
        return lax.ppermute(x, "seq", [(i, i ^ k) for i in range(n)])

    def swap(x):
        return lax.ppermute(x, "ten", [(0, 1), (1, 0)])

    pair, *chosen = call(
        functools.partial(norm_select_kernel, n),
        "norm_select",
        (hidden, norm_gain.reshape(1, model), retained_lists.reshape(1, rows), keys, values),
        [shape((rows, 2 * keys.shape[1]), bf16)] + [shape((rows, half), bf16)] * n,
        4 * rows * model,
        limit=16,
        in_specs=[ANY] * 5,
        remote=5,
        scratch=[pltpu.VMEM((rows, model), bf16), pltpu.VMEM((1, model), f32), pltpu.VMEM((1, rows), i32), dma((8,))],
    )
    pair_other = trade(pair, 1)
    received = [chosen[0]] + [trade(chosen[k], k) for k in range(1, n)]

    matrix, queries, held, target = call(
        functools.partial(stage_kernel, n),
        "stage",
        (counts, affine_matrix, queries, pair, pair_other, *received[n // 2 :]),
        [shape(affine_matrix.shape, bf16), shape(queries.shape, bf16), shape((2 * rows, pair.shape[1]), bf16), shape((1, n * rows), i32)],
        0,
        limit=16,
        in_specs=[ANY] * 3 + [VMEM] * 2 + [ANY] * (n // 2),
        remote=3,
        scratch=[pltpu.SMEM(counts.shape, i32), dma((3,))],
    )
    order = [0, 1]
    mask = n // 2
    held_other = trade(held, mask)
    order = order + [k ^ mask for k in order]
    while mask > 2:
        mask //= 2
        held = jnp.concatenate([held, held_other], axis=0)
        held_other = trade(held, mask)
        order = order + [k ^ mask for k in order]

    (own,) = call(
        functools.partial(compact_kernel, n, owners),
        "compact",
        (target, *received),
        [shape((survivors, half), bf16)],
        2 * survivors * n * rows * half,
    )
    other = swap(own)

    products = [
        call(
            functools.partial(project_kernel, c * chunk),
            "project",
            (own, other, matrix),
            [shape((near, chunk), f32), shape((near, chunk), bf16)],
            4 * survivors * half * chunk,
        )
        for c in range(2)
    ]
    context, columns = call(
        functools.partial(attention_kernel, n, kv_heads, order, owners),
        "attention",
        (queries, held, held_other, products[1][1]),
        [shape(queries.shape, f32), shape((n, rows), f32)],
        4 * rows * n * rows * queries.shape[1],
        limit=32,
        in_specs=[VMEM] * 3 + [ANY],
    )
    first, far, *sent = call(
        pair_sum_kernel,
        "pair_sum",
        (products[0][0], trade(products[0][1], 1), products[1][1], columns),
        [shape((lines, chunk), f32), shape((near, chunk), bf16)] + [shape((lines, chunk), bf16)] * (n // 2 - 1),
        near * chunk,
        in_specs=[VMEM] * 3 + [ANY],
    )
    parts = [first] + [trade(x, 2 * (i + 1)) for i, x in enumerate(sent)]
    far = trade(far, 1)

    columns = columns + swap(columns)
    done, last, own_columns, *sent = call(
        functools.partial(pair_sum_last_kernel, n),
        "pair_sum_last",
        (products[1][0], far, columns[: n // 2], trade(columns[n // 2 :], 1), *parts),
        [shape((lines, chunk), f32), shape((lines, chunk), f32), shape((1, rows), f32)] + [shape((lines, chunk + 2 * rows), bf16)] * (n // 2 - 1),
        near * chunk,
    )
    parts = [last] + [trade(x, 2 * (i + 1)) for i, x in enumerate(sent)]

    triples, scores = call(
        finish_kernel,
        "finish",
        (affine_offset_vector.reshape(1, width), done, own_columns, *parts),
        [shape((lines, width), f32), shape((1, rows), f32)],
        n * lines * width,
    )
    return (context, scores.reshape(rows), triples)


def solution(mesh):
    in_specs = (
        P(("grp", "seq"), "ten"),
        P(("grp", "seq"), "ten"),
        P(("grp", "seq"), "ten"),
        P(("grp", "seq"), None),
        P(),
        P(("grp", "seq")),
        P("grp"),
        P("seq", "ten"),
        P("ten"),
    )
    out_specs = (P(("grp", "seq"), "ten"), P(("grp", "seq")), P(("grp", "seq"), "ten"))
    return jax.shard_map(shards, mesh=mesh, in_specs=in_specs, out_specs=out_specs, check_vma=False)
```

```python
import functools
import math

import jax
import jax.numpy as jnp
from jax import lax
from jax.experimental import pallas as pl
from jax.experimental.pallas import tpu as pltpu
from jax.sharding import PartitionSpec as P

HEAD_SIZE = 128
QUERY_HEADS = 32
VMEM = pl.BlockSpec(memory_space=pltpu.VMEM)
ANY = pl.BlockSpec(memory_space=pl.ANY)
MIB = 1024 * 1024


def call(body, name, inputs, outputs, flops, limit=16, in_specs=None, scratch=(), remote=0):
    inputs = [pltpu.with_memory_space_constraint(x, pltpu.HBM) if i < remote else x for i, x in enumerate(inputs)]
    size = sum(math.prod(x.shape) * x.dtype.itemsize for x in list(inputs) + list(outputs))
    return pl.pallas_call(
        body,
        out_shape=list(outputs),
        in_specs=in_specs or [VMEM] * len(inputs),
        out_specs=[VMEM] * len(outputs),
        scratch_shapes=list(scratch),
        compiler_params=pltpu.CompilerParams(vmem_limit_bytes=limit * MIB),
        cost_estimate=pl.CostEstimate(flops=flops, bytes_accessed=size, transcendentals=0),
        name=name,
    )(*inputs)


def norm_select_kernel(n, hidden_in, gain_in, kept_in, keys_in, values_in, pair, out, hidden, gain, kept, sems):
    rows, width = hidden.shape
    block = width // n
    half = block // 2
    pieces = 4
    piece = width // pieces
    key_width = keys_in.shape[1]
    loads = [
        pltpu.make_async_copy(
            hidden_in.at[:, i * piece : (i + 1) * piece], hidden.at[:, i * piece : (i + 1) * piece], sems.at[i]
        )
        for i in range(pieces)
    ]
    loads += [
        pltpu.make_async_copy(gain_in, gain, sems.at[pieces]),
        pltpu.make_async_copy(kept_in, kept, sems.at[pieces + 1]),
        pltpu.make_async_copy(keys_in, pair.at[:, :key_width], sems.at[pieces + 2]),
        pltpu.make_async_copy(values_in, pair.at[:, key_width:], sems.at[pieces + 3]),
    ]
    for load in loads:
        load.start()
    t = lax.axis_index("ten")
    step = min(piece, 1024)
    total = jnp.zeros((rows, step), jnp.float32)
    for i in range(pieces):
        loads[i].wait()
        for j in range(i * piece, (i + 1) * piece, step):
            part = hidden[:, j : j + step].astype(jnp.float32)
            total += part * part
    scale = lax.rsqrt(jnp.sum(total, axis=1, keepdims=True) / width + 1e-06)
    for load in loads[pieces:]:
        load.wait()
    selector = (kept[...] == lax.broadcasted_iota(jnp.int32, (rows, rows), 0)).astype(jnp.bfloat16)
    for k in range(n):
        start = pl.multiple_of(k * block + t * half, half)
        columns = pl.ds(start, half)
        normed = (hidden[:, columns].astype(jnp.float32) * scale * gain[:, columns]).astype(jnp.bfloat16)
        out[k * rows : (k + 1) * rows] = lax.dot_general(
            selector, normed, (((0,), (0,)), ((), ())), preferred_element_type=jnp.float32
        ).astype(jnp.bfloat16)


def stage_kernel(n, counts_in, matrix_in, queries_in, after, matrix, queries, target, counts, sems):
    loads = [
        pltpu.make_async_copy(counts_in, counts, sems.at[0]),
        pltpu.make_async_copy(matrix_in, matrix, sems.at[1]),
        pltpu.make_async_copy(queries_in, queries, sems.at[2]),
    ]
    for load in loads:
        load.start()
    total = target.shape[1]
    rows = total // n
    loads[0].wait()
    slot_all = lax.broadcasted_iota(jnp.int32, (1, total), 1)
    found = jnp.full((1, total), -1, jnp.int32)
    begin = jnp.int32(0)
    for source in range(n):
        slot = slot_all - source * rows
        inside = (slot >= 0) & (slot < counts[source])
        found = jnp.where(inside, begin + slot, found)
        begin += counts[source]
    target[...] = found
    for load in loads[1:]:
        load.wait()


def compact_kernel(n, target, received, out):
    lines = out.shape[0] // n
    parity = lax.rem(lax.axis_index("seq"), 2)
    line = lax.broadcasted_iota(jnp.int32, (lines, received.shape[0]), 0)
    owners = [2 * p + parity for p in range(n // 2)] + [2 * p + 1 - parity for p in range(n // 2)]
    pick = jnp.concatenate(
        [(line + owner * lines == target[...]).astype(jnp.float32) for owner in owners], axis=0
    ).astype(jnp.bfloat16)
    out[...] = jnp.dot(pick, received[...], preferred_element_type=jnp.float32).astype(jnp.bfloat16)


def project_kernel(first, own, other, matrix, near, far):
    survivors, half = own.shape
    lines = survivors // 2
    width = near.shape[1]
    t = lax.axis_index("ten")
    mine = pl.ds(pl.multiple_of(t * half, half), half)
    others = pl.ds(pl.multiple_of((1 - t) * half, half), half)
    tile = width // 2 if width % 256 == 0 else width
    for j in range(0, width, tile):
        lanes = slice(first + j, first + j + tile)
        part = jnp.dot(own[...], matrix[mine, lanes], preferred_element_type=jnp.float32)
        part += jnp.dot(other[...], matrix[others, lanes], preferred_element_type=jnp.float32)
        near[:, j : j + tile] = part[:lines]
        far[:, j : j + tile] = part[lines:].astype(jnp.bfloat16)


def own_rows(lines):
    place = lax.div(lax.axis_index("seq"), 2)
    return pl.ds(pl.multiple_of(place * lines, lines), lines)


def pair_sum_kernel(kept, received, next_in, after, own, next_out, out):
    mine = own_rows(own.shape[0])
    own[...] = kept[mine] + received[mine].astype(jnp.float32)
    out[...] = (kept[...] + received[...].astype(jnp.float32)).astype(jnp.bfloat16)
    next_out[...] = next_in[...]


def total_of(own, received, width):
    lines = own.shape[0]
    place = lax.div(lax.axis_index("seq"), 2)
    total = own[...]
    for p in range(received.shape[0] // lines):
        block = received[p * lines : (p + 1) * lines, :width].astype(jnp.float32)
        total += jnp.where(place == p, 0.0, block)
    return total


def pair_sum_last_kernel(kept, received, columns, columns_other, first, arrived, done, own, own_columns, out):
    lines, width = own.shape
    rows = columns.shape[1]
    place = lax.div(lax.axis_index("seq"), 2)
    done[...] = total_of(first, arrived, width)
    mine = own_rows(lines)
    own[...] = kept[mine] + received[mine].astype(jnp.float32)
    own_columns[...] = columns[:1] + columns_other[:1]
    out[:, :width] = (kept[...] + received[...].astype(jnp.float32)).astype(jnp.bfloat16)
    for p in range(kept.shape[0] // lines):
        at = pl.ds(lax.bitwise_xor(place, p), 1)
        total = columns[at] + columns_other[at]
        head = total.astype(jnp.bfloat16).astype(jnp.float32)
        extra = jnp.concatenate([head, total - head], axis=1).astype(jnp.bfloat16)
        out[p * lines : (p + 1) * lines, width:] = jnp.broadcast_to(extra, (lines, 2 * rows))


def attention_kernel(n, kv_heads, order, owners, queries, held_a, held_b, after, context, columns):
    rows = queries.shape[0]
    group = queries.shape[1] // (HEAD_SIZE * kv_heads)
    s = lax.axis_index("seq")
    keys_total = n * rows
    column = lax.broadcasted_iota(jnp.int32, (1, keys_total), 1)
    position = column
    for at, k in enumerate(order):
        inside = (column >= at * rows) & (column < (at + 1) * rows)
        position = jnp.where(inside, column + (lax.bitwise_xor(s, k) - s - at) * rows, position)
    row = lax.rem(lax.broadcasted_iota(jnp.int32, (group * rows, keys_total), 0), rows)
    allowed = position <= row
    sums = jnp.zeros((1, keys_total), jnp.float32)
    for g in range(kv_heads):
        key_lanes = slice(g * HEAD_SIZE, (g + 1) * HEAD_SIZE)
        value_lanes = slice((kv_heads + g) * HEAD_SIZE, (kv_heads + g + 1) * HEAD_SIZE)
        key = jnp.concatenate([held_a[:, key_lanes], held_b[:, key_lanes]], axis=0)
        value = jnp.concatenate([held_a[:, value_lanes], held_b[:, value_lanes]], axis=0)
        heads = range(g * group, (g + 1) * group)
        stacked = jnp.concatenate([queries[:, h * HEAD_SIZE : (h + 1) * HEAD_SIZE] for h in heads], axis=0)
        scores = lax.dot_general(
            stacked, key, (((1,), (1,)), ((), ())), preferred_element_type=jnp.float32
        ) * HEAD_SIZE ** (-0.5)
        scores = jnp.where(allowed, scores, -1e30)
        weights = jnp.exp(scores - jnp.max(scores, axis=1, keepdims=True))
        inverse = 1.0 / jnp.sum(weights, axis=1, keepdims=True)
        mixed = jnp.dot(weights.astype(jnp.bfloat16), value, preferred_element_type=jnp.float32) * inverse
        for i, h in enumerate(heads):
            context[:, h * HEAD_SIZE : (h + 1) * HEAD_SIZE] = mixed[i * rows : (i + 1) * rows]
        sums += jnp.sum(weights * inverse, axis=0, keepdims=True)
    for at, k in enumerate(order):
        i = owners.index(k)
        columns[i : i + 1, :] = sums[:, at * rows : (at + 1) * rows]


def finish_kernel(bias, done, own_columns, own, arrived, out, scores):
    lines, width = own.shape
    rows = own_columns.shape[1]
    out[:, :width] = done[...] + bias[:, :width]
    out[:, width:] = total_of(own, arrived, width) + bias[:, width:]
    place = lax.div(lax.axis_index("seq"), 2)
    sums = own_columns[...]
    for p in range(arrived.shape[0] // lines):
        extra = arrived[p * lines : p * lines + 16, width:].astype(jnp.float32)
        sums += jnp.where(place == p, 0.0, extra[:1, :rows] + extra[:1, rows:])
    scores[...] = sums / QUERY_HEADS


def shards(queries, keys, values, hidden, norm_gain, retained_lists, counts, affine_matrix, affine_offset_vector):
    n = lax.axis_size("seq")
    rows, model = hidden.shape
    kv_heads = keys.shape[1] // HEAD_SIZE
    half = affine_matrix.shape[0] // 2
    width = affine_matrix.shape[1]
    survivors = n * rows // 2
    lines = survivors // n
    chunk = width // 2
    near = survivors // 2
    owners = list(range(0, n, 2)) + list(range(1, n, 2))
    f32, bf16, i32 = jnp.float32, jnp.bfloat16, jnp.int32
    shape = jax.ShapeDtypeStruct
    dma = pltpu.SemaphoreType.DMA

    def trade(x, k):
        return lax.ppermute(x, "seq", [(i, i ^ k) for i in range(n)])

    def spread(x):
        groups = [[2 * p + parity for p in range(n // 2)] for parity in range(2)]
        return lax.all_to_all(x, "seq", 0, 0, axis_index_groups=groups, tiled=True)

    def swap(x):
        return lax.ppermute(x, "ten", [(0, 1), (1, 0)])

    pair, chosen = call(
        functools.partial(norm_select_kernel, n),
        "norm_select",
        (hidden, norm_gain.reshape(1, model), retained_lists.reshape(1, rows), keys, values),
        [shape((rows, 2 * keys.shape[1]), bf16), shape((n * rows, half), bf16)],
        4 * rows * model,
        limit=16,
        in_specs=[ANY] * 5,
        remote=5,
        scratch=[pltpu.VMEM((rows, model), bf16), pltpu.VMEM((1, model), f32), pltpu.VMEM((1, rows), i32), dma((8,))],
    )
    pair_other = trade(pair, 1)
    received = lax.all_to_all(chosen, "seq", 0, 0, tiled=True)

    matrix, queries, target = call(
        functools.partial(stage_kernel, n),
        "stage",
        (counts, affine_matrix, queries, pair_other),
        [shape(affine_matrix.shape, bf16), shape(queries.shape, bf16), shape((1, n * rows), i32)],
        0,
        in_specs=[ANY] * 4,
        remote=3,
        scratch=[pltpu.SMEM(counts.shape, i32), dma((3,))],
    )
    held, order = jnp.concatenate([pair, pair_other], axis=0), [0, 1]
    mask = n // 2
    held_other = trade(held, mask)
    order = order + [k ^ mask for k in order]
    while mask > 2:
        mask //= 2
        held = jnp.concatenate([held, held_other], axis=0)
        held_other = trade(held, mask)
        order = order + [k ^ mask for k in order]

    (own,) = call(
        functools.partial(compact_kernel, n),
        "compact",
        (target, received),
        [shape((survivors, half), bf16)],
        2 * survivors * n * rows * half,
    )
    other = swap(own)

    products = [
        call(
            functools.partial(project_kernel, c * chunk),
            "project",
            (own, other, matrix),
            [shape((near, chunk), f32), shape((near, chunk), bf16)],
            4 * survivors * half * chunk,
        )
        for c in range(2)
    ]
    context, columns = call(
        functools.partial(attention_kernel, n, kv_heads, order, owners),
        "attention",
        (queries, held, held_other, products[1][1]),
        [shape(queries.shape, f32), shape((n, rows), f32)],
        4 * rows * n * rows * queries.shape[1],
        limit=32,
        in_specs=[VMEM] * 3 + [ANY],
    )
    first, far, sent = call(
        pair_sum_kernel,
        "pair_sum",
        (products[0][0], trade(products[0][1], 1), products[1][1], columns),
        [shape((lines, chunk), f32), shape((near, chunk), bf16), shape((near, chunk), bf16)],
        near * chunk,
        in_specs=[VMEM] * 3 + [ANY],
    )
    arrived = spread(sent)
    far = trade(far, 1)

    columns = columns + swap(columns)
    done, last, own_columns, sent = call(
        pair_sum_last_kernel,
        "pair_sum_last",
        (products[1][0], far, columns[: n // 2], trade(columns[n // 2 :], 1), first, arrived),
        [shape((lines, chunk), f32), shape((lines, chunk), f32), shape((1, rows), f32), shape((near, chunk + 2 * rows), bf16)],
        near * chunk,
    )

    triples, scores = call(
        finish_kernel,
        "finish",
        (affine_offset_vector.reshape(1, width), done, own_columns, last, spread(sent)),
        [shape((lines, width), f32), shape((1, rows), f32)],
        n * lines * width,
    )
    return (context, scores.reshape(rows), triples)


def solution(mesh):
    in_specs = (
        P(("grp", "seq"), "ten"),
        P(("grp", "seq"), "ten"),
        P(("grp", "seq"), "ten"),
        P(("grp", "seq"), None),
        P(),
        P(("grp", "seq")),
        P("grp"),
        P("seq", "ten"),
        P("ten"),
    )
    out_specs = (P(("grp", "seq"), "ten"), P(("grp", "seq")), P(("grp", "seq"), "ten"))
    return jax.shard_map(shards, mesh=mesh, in_specs=in_specs, out_specs=out_specs, check_vma=False)
```

```python
import functools
import math

import jax
import jax.numpy as jnp
from jax import lax
from jax.experimental import pallas as pl
from jax.experimental.pallas import tpu as pltpu
from jax.sharding import PartitionSpec as P

HEAD_SIZE = 128
QUERY_HEADS = 32
VMEM = pl.BlockSpec(memory_space=pltpu.VMEM)
ANY = pl.BlockSpec(memory_space=pl.ANY)
MIB = 1024 * 1024


def call(body, name, inputs, outputs, flops, limit=16, in_specs=None, scratch=(), remote=0):
    inputs = [pltpu.with_memory_space_constraint(x, pltpu.HBM) if i < remote else x for i, x in enumerate(inputs)]
    size = sum(math.prod(x.shape) * x.dtype.itemsize for x in list(inputs) + list(outputs))
    return pl.pallas_call(
        body,
        out_shape=list(outputs),
        in_specs=in_specs or [VMEM] * len(inputs),
        out_specs=[VMEM] * len(outputs),
        scratch_shapes=list(scratch),
        compiler_params=pltpu.CompilerParams(vmem_limit_bytes=limit * MIB),
        cost_estimate=pl.CostEstimate(flops=flops, bytes_accessed=size, transcendentals=0),
        name=name,
    )(*inputs)


def norm_select_kernel(n, hidden_in, gain_in, kept_in, keys_in, values_in, pair, *refs):
    outs, (hidden, gain, kept, sems) = refs[:n], refs[n:]
    rows, width = hidden.shape
    block = width // n
    half = block // 2
    pieces = 4
    piece = width // pieces
    key_width = keys_in.shape[1]
    loads = [
        pltpu.make_async_copy(
            hidden_in.at[:, i * piece : (i + 1) * piece], hidden.at[:, i * piece : (i + 1) * piece], sems.at[i]
        )
        for i in range(pieces)
    ]
    loads += [
        pltpu.make_async_copy(gain_in, gain, sems.at[pieces]),
        pltpu.make_async_copy(kept_in, kept, sems.at[pieces + 1]),
        pltpu.make_async_copy(keys_in, pair.at[:, :key_width], sems.at[pieces + 2]),
        pltpu.make_async_copy(values_in, pair.at[:, key_width:], sems.at[pieces + 3]),
    ]
    for load in loads:
        load.start()
    s, t = lax.axis_index("seq"), lax.axis_index("ten")
    step = min(piece, 1024)
    total = jnp.zeros((rows, step), jnp.float32)
    for i in range(pieces):
        loads[i].wait()
        for j in range(i * piece, (i + 1) * piece, step):
            part = hidden[:, j : j + step].astype(jnp.float32)
            total += part * part
    scale = lax.rsqrt(jnp.sum(total, axis=1, keepdims=True) / width + 1e-06)
    for load in loads[pieces:]:
        load.wait()
    selector = (kept[...] == lax.broadcasted_iota(jnp.int32, (rows, rows), 0)).astype(jnp.bfloat16)
    for k in range(n):
        start = pl.multiple_of(lax.bitwise_xor(s, k) * block + t * half, half)
        columns = pl.ds(start, half)
        normed = (hidden[:, columns].astype(jnp.float32) * scale * gain[:, columns]).astype(jnp.bfloat16)
        outs[k][...] = lax.dot_general(
            selector, normed, (((0,), (0,)), ((), ())), preferred_element_type=jnp.float32
        ).astype(jnp.bfloat16)


def stage_kernel(n, counts_in, matrix_in, queries_in, *refs):
    matrix, queries, target, counts, sems = refs[-5:]
    loads = [
        pltpu.make_async_copy(counts_in, counts, sems.at[0]),
        pltpu.make_async_copy(matrix_in, matrix, sems.at[1]),
        pltpu.make_async_copy(queries_in, queries, sems.at[2]),
    ]
    for load in loads:
        load.start()
    rows = target.shape[1] // n
    s = lax.axis_index("seq")
    loads[0].wait()
    slot_all = lax.broadcasted_iota(jnp.int32, (1, n * rows), 1)
    found = jnp.full((1, n * rows), -1, jnp.int32)
    for k in range(n):
        source = lax.bitwise_xor(s, k)
        begin = jnp.int32(0)
        for i in range(n):
            begin += jnp.where(i < source, counts[i], 0)
        slot = slot_all - k * rows
        inside = (slot >= 0) & (slot < counts[source])
        found = jnp.where(inside, begin + slot, found)
    target[...] = found
    for load in loads[1:]:
        load.wait()


def compact_kernel(n, target, *refs):
    blocks, out = refs[:n], refs[n]
    lines = out.shape[0] // n
    s = lax.axis_index("seq")
    received = jnp.concatenate([b[...] for b in blocks], axis=0)
    line = lax.broadcasted_iota(jnp.int32, (lines, received.shape[0]), 0)
    pick = jnp.concatenate(
        [(line + lax.bitwise_xor(s, k) * lines == target[...]).astype(jnp.float32) for k in range(n)], axis=0
    ).astype(jnp.bfloat16)
    out[...] = jnp.dot(pick, received, preferred_element_type=jnp.float32).astype(jnp.bfloat16)


def halving_order(n, masks):
    return sorted(range(n), key=lambda k: [k & mask for mask in masks])


def project_kernel(first, order, own, other, matrix, near, far):
    survivors, half = own.shape
    lines = survivors // len(order)
    width = near.shape[1]
    t = lax.axis_index("ten")
    mine = pl.ds(pl.multiple_of(t * half, half), half)
    others = pl.ds(pl.multiple_of((1 - t) * half, half), half)
    tile = width // 2 if width % 256 == 0 else width
    for j in range(0, width, tile):
        lanes = slice(first + j, first + j + tile)
        part = jnp.dot(own[...], matrix[mine, lanes], preferred_element_type=jnp.float32)
        part += jnp.dot(other[...], matrix[others, lanes], preferred_element_type=jnp.float32)
        for i, k in enumerate(order):
            block = part[k * lines : (k + 1) * lines]
            if i < len(order) // 2:
                near[i * lines : (i + 1) * lines, j : j + tile] = block
            else:
                i -= len(order) // 2
                far[i * lines : (i + 1) * lines, j : j + tile] = block.astype(jnp.bfloat16)


def hop_sum_kernel(kept, received, columns_in, keep, sent, columns):
    rows = keep.shape[0]
    columns[...] = columns_in[...]
    total = kept[...] + received[...].astype(jnp.float32)
    keep[...] = total[:rows]
    sent[...] = total[rows:].astype(jnp.bfloat16)


def hop_sum_both_kernel(*refs):
    *parts, columns_in, keep, sent, columns = refs
    columns[...] = columns_in[...]
    count = len(parts) // 2
    rows = keep.shape[0]
    width = keep.shape[1] // count
    for c in range(count):
        lanes = slice(c * width, (c + 1) * width)
        total = parts[c][...] + parts[count + c][...].astype(jnp.float32)
        keep[:, lanes] = total[:rows]
        sent[:, lanes] = total[rows:].astype(jnp.bfloat16)


def attention_kernel(n, kv_heads, order, masks, queries, held_a, held_b, after, context, columns):
    rows = queries.shape[0]
    group = queries.shape[1] // (HEAD_SIZE * kv_heads)
    s = lax.axis_index("seq")
    keys_total = n * rows
    column = lax.broadcasted_iota(jnp.int32, (1, keys_total), 1)
    position = column
    for at, k in enumerate(order):
        inside = (column >= at * rows) & (column < (at + 1) * rows)
        position = jnp.where(inside, column + (lax.bitwise_xor(s, k) - s - at) * rows, position)
    row = lax.rem(lax.broadcasted_iota(jnp.int32, (group * rows, keys_total), 0), rows)
    allowed = position <= row
    sums = jnp.zeros((1, keys_total), jnp.float32)
    for g in range(kv_heads):
        key_lanes = slice(g * HEAD_SIZE, (g + 1) * HEAD_SIZE)
        value_lanes = slice((kv_heads + g) * HEAD_SIZE, (kv_heads + g + 1) * HEAD_SIZE)
        key = jnp.concatenate([held_a[:, key_lanes], held_b[:, key_lanes]], axis=0)
        value = jnp.concatenate([held_a[:, value_lanes], held_b[:, value_lanes]], axis=0)
        heads = range(g * group, (g + 1) * group)
        stacked = jnp.concatenate([queries[:, h * HEAD_SIZE : (h + 1) * HEAD_SIZE] for h in heads], axis=0)
        scores = lax.dot_general(
            stacked, key, (((1,), (1,)), ((), ())), preferred_element_type=jnp.float32
        ) * HEAD_SIZE ** (-0.5)
        scores = jnp.where(allowed, scores, -1e30)
        weights = jnp.exp(scores - jnp.max(scores, axis=1, keepdims=True))
        inverse = 1.0 / jnp.sum(weights, axis=1, keepdims=True)
        mixed = jnp.dot(weights.astype(jnp.bfloat16), value, preferred_element_type=jnp.float32) * inverse
        for i, h in enumerate(heads):
            context[:, h * HEAD_SIZE : (h + 1) * HEAD_SIZE] = mixed[i * rows : (i + 1) * rows]
        sums += jnp.sum(weights * inverse, axis=0, keepdims=True)
    for at, k in enumerate(order):
        i = halving_order(n, masks).index(k)
        columns[i : i + 1, :] = sums[:, at * rows : (at + 1) * rows]


def finish_kernel(bias, kept, received, out):
    out[...] = kept[...] + received[...].astype(jnp.float32) + bias[...]


def shards(queries, keys, values, hidden, norm_gain, retained_lists, counts, affine_matrix, affine_offset_vector):
    n = lax.axis_size("seq")
    rows, model = hidden.shape
    kv_heads = keys.shape[1] // HEAD_SIZE
    half = affine_matrix.shape[0] // 2
    width = affine_matrix.shape[1]
    survivors = n * rows // 2
    lines = survivors // n
    chunk = width // 2
    near = survivors // 2
    f32, bf16, i32 = jnp.float32, jnp.bfloat16, jnp.int32
    shape = jax.ShapeDtypeStruct
    dma = pltpu.SemaphoreType.DMA

    def trade(x, k):
        return lax.ppermute(x, "seq", [(i, i ^ k) for i in range(n)])

    def swap(x):
        return lax.ppermute(x, "ten", [(0, 1), (1, 0)])

    pair, *chosen = call(
        functools.partial(norm_select_kernel, n),
        "norm_select",
        (hidden, norm_gain.reshape(1, model), retained_lists.reshape(1, rows), keys, values),
        [shape((rows, 2 * keys.shape[1]), bf16)] + [shape((rows, half), bf16)] * n,
        4 * rows * model,
        limit=16,
        in_specs=[ANY] * 5,
        remote=5,
        scratch=[pltpu.VMEM((rows, model), bf16), pltpu.VMEM((1, model), f32), pltpu.VMEM((1, rows), i32), dma((8,))],
    )
    pair_other = trade(pair, 1)
    received = [chosen[0]] + [trade(chosen[k], k) for k in range(1, n)]
    turns = [k for i in range(n // 2) for k in (n // 2 + i, i) if k]
    matrix, queries, target = call(
        functools.partial(stage_kernel, n),
        "stage",
        (counts, affine_matrix, queries, *[received[k] for k in turns[:5]]),
        [shape(affine_matrix.shape, bf16), shape(queries.shape, bf16), shape((1, n * rows), i32)],
        0,
        in_specs=[ANY] * 8,
        remote=3,
        scratch=[pltpu.SMEM(counts.shape, i32), dma((3,))],
    )
    held, order, mask = jnp.concatenate([pair, pair_other], axis=0), [0, 1], 2
    while mask < n // 2:
        held = jnp.concatenate([held, trade(held, mask)], axis=0)
        order = order + [k ^ mask for k in order]
        mask *= 2
    held_other = trade(held, mask)
    order = order + [k ^ mask for k in order]

    (own,) = call(
        functools.partial(compact_kernel, n),
        "compact",
        (target, *received),
        [shape((survivors, half), bf16)],
        2 * survivors * n * rows * half,
    )
    other = swap(own)

    rest = [1 << i for i in range(2, n.bit_length() - 1)]
    masks = [[1, 2] + rest, [2, 1] + rest]
    products = [
        call(
            functools.partial(project_kernel, c * chunk, halving_order(n, masks[c])),
            "project",
            (own, other, matrix),
            [shape((near, chunk), f32), shape((near, chunk), bf16)],
            4 * survivors * half * chunk,
        )
        for c in range(2)
    ]
    context, columns = call(
        functools.partial(attention_kernel, n, kv_heads, order, masks[0]),
        "attention",
        (queries, held, held_other, products[1][1]),
        [shape(queries.shape, f32), shape((n, rows), f32)],
        4 * rows * n * rows * queries.shape[1],
        limit=32,
        in_specs=[VMEM] * 3 + [ANY],
    )
    kept = [product[0] for product in products]
    arrived = [trade(product[1], masks[c][0]) for c, product in enumerate(products)]
    def column_hop(columns, mask):
        left = columns.shape[0] // 2
        return columns[:left] + trade(columns[left:], mask)

    lines_left = near // 2
    for c in (1, 0):
        keep, sent, columns = call(
            hop_sum_kernel,
            "hop_sum",
            (kept[c], arrived[c], columns),
            [shape((lines_left, chunk), f32), shape((lines_left, chunk), bf16), shape(columns.shape, f32)],
            near * chunk,
        )
        kept[c], arrived[c] = keep, trade(sent, masks[c][1])
    columns = column_hop(columns + swap(columns), masks[0][0])
    for mask in rest:
        lines_left //= 2
        keep, sent, columns = call(
            hop_sum_both_kernel,
            "hop_sum_both",
            (*kept, *arrived, columns),
            [shape((lines_left, width), f32), shape((lines_left, width), bf16), shape(columns.shape, f32)],
            lines_left * width,
        )
        kept, arrived = [keep], [trade(sent, mask)]
    for mask in masks[0][1:]:
        columns = column_hop(columns, mask)

    (triples,) = call(
        finish_kernel,
        "finish",
        (affine_offset_vector.reshape(1, width), kept[0], arrived[0]),
        [shape((lines, width), f32)],
        n * lines * width,
    )
    return (context, columns.reshape(rows) / QUERY_HEADS, triples)


def solution(mesh):
    in_specs = (
        P(("grp", "seq"), "ten"),
        P(("grp", "seq"), "ten"),
        P(("grp", "seq"), "ten"),
        P(("grp", "seq"), None),
        P(),
        P(("grp", "seq")),
        P("grp"),
        P("seq", "ten"),
        P("ten"),
    )
    out_specs = (P(("grp", "seq"), "ten"), P(("grp", "seq")), P(("grp", "seq"), "ten"))
    return jax.shard_map(shards, mesh=mesh, in_specs=in_specs, out_specs=out_specs, check_vma=False)
```

```python
import functools
import math

import jax
import jax.numpy as jnp
from jax import lax
from jax.experimental import pallas as pl
from jax.experimental.pallas import tpu as pltpu
from jax.sharding import PartitionSpec as P

HEAD_SIZE = 128
QUERY_HEADS = 32
VMEM = pl.BlockSpec(memory_space=pltpu.VMEM)
ANY = pl.BlockSpec(memory_space=pl.ANY)
MIB = 1024 * 1024


def call(body, name, inputs, outputs, flops, limit=16, in_specs=None, scratch=(), remote=0):
    inputs = [pltpu.with_memory_space_constraint(x, pltpu.HBM) if i < remote else x for i, x in enumerate(inputs)]
    size = sum(math.prod(x.shape) * x.dtype.itemsize for x in list(inputs) + list(outputs))
    return pl.pallas_call(
        body,
        out_shape=list(outputs),
        in_specs=in_specs or [VMEM] * len(inputs),
        out_specs=[VMEM] * len(outputs),
        scratch_shapes=list(scratch),
        compiler_params=pltpu.CompilerParams(vmem_limit_bytes=limit * MIB),
        cost_estimate=pl.CostEstimate(flops=flops, bytes_accessed=size, transcendentals=0),
        name=name,
    )(*inputs)


def norm_select_kernel(n, hidden_in, gain_in, kept_in, keys_in, values_in, pair, *refs):
    outs, (hidden, gain, kept, sems) = refs[:n], refs[n:]
    rows, width = hidden.shape
    block = width // n
    half = block // 2
    pieces = 4
    piece = width // pieces
    key_width = keys_in.shape[1]
    loads = [
        pltpu.make_async_copy(
            hidden_in.at[:, i * piece : (i + 1) * piece], hidden.at[:, i * piece : (i + 1) * piece], sems.at[i]
        )
        for i in range(pieces)
    ]
    loads += [
        pltpu.make_async_copy(gain_in, gain, sems.at[pieces]),
        pltpu.make_async_copy(kept_in, kept, sems.at[pieces + 1]),
        pltpu.make_async_copy(keys_in, pair.at[:, :key_width], sems.at[pieces + 2]),
        pltpu.make_async_copy(values_in, pair.at[:, key_width:], sems.at[pieces + 3]),
    ]
    for load in loads:
        load.start()
    s, t = lax.axis_index("seq"), lax.axis_index("ten")
    step = min(piece, 1024)
    total = jnp.zeros((rows, step), jnp.float32)
    for i in range(pieces):
        loads[i].wait()
        for j in range(i * piece, (i + 1) * piece, step):
            part = hidden[:, j : j + step].astype(jnp.float32)
            total += part * part
    scale = lax.rsqrt(jnp.sum(total, axis=1, keepdims=True) / width + 1e-06)
    for load in loads[pieces:]:
        load.wait()
    selector = (kept[...] == lax.broadcasted_iota(jnp.int32, (rows, rows), 0)).astype(jnp.bfloat16)
    for k in range(n):
        start = pl.multiple_of(lax.bitwise_xor(s, k) * block + t * half, half)
        columns = pl.ds(start, half)
        normed = (hidden[:, columns].astype(jnp.float32) * scale * gain[:, columns]).astype(jnp.bfloat16)
        outs[k][...] = lax.dot_general(
            selector, normed, (((0,), (0,)), ((), ())), preferred_element_type=jnp.float32
        ).astype(jnp.bfloat16)


def stage_kernel(n, counts_in, matrix_in, queries_in, *refs):
    matrix, queries, target, counts, sems = refs[-5:]
    loads = [
        pltpu.make_async_copy(counts_in, counts, sems.at[0]),
        pltpu.make_async_copy(matrix_in, matrix, sems.at[1]),
        pltpu.make_async_copy(queries_in, queries, sems.at[2]),
    ]
    for load in loads:
        load.start()
    rows = target.shape[1] // n
    s = lax.axis_index("seq")
    loads[0].wait()
    slot_all = lax.broadcasted_iota(jnp.int32, (1, n * rows), 1)
    found = jnp.full((1, n * rows), -1, jnp.int32)
    for k in range(n):
        source = lax.bitwise_xor(s, k)
        begin = jnp.int32(0)
        for i in range(n):
            begin += jnp.where(i < source, counts[i], 0)
        slot = slot_all - k * rows
        inside = (slot >= 0) & (slot < counts[source])
        found = jnp.where(inside, begin + slot, found)
    target[...] = found
    for load in loads[1:]:
        load.wait()


def compact_kernel(n, target, after, *refs):
    blocks, out = refs[:n], refs[n]
    lines = out.shape[0] // n
    s = lax.axis_index("seq")
    received = jnp.concatenate([b[...] for b in blocks], axis=0)
    line = lax.broadcasted_iota(jnp.int32, (lines, received.shape[0]), 0)
    pick = jnp.concatenate(
        [(line + lax.bitwise_xor(s, k) * lines == target[...]).astype(jnp.float32) for k in range(n)], axis=0
    ).astype(jnp.bfloat16)
    out[...] = jnp.dot(pick, received, preferred_element_type=jnp.float32).astype(jnp.bfloat16)


def halving_order(n, masks):
    return sorted(range(n), key=lambda k: [k & mask for mask in masks])


def project_kernel(first, order, own, other, matrix, after, near, far):
    survivors, half = own.shape
    lines = survivors // len(order)
    width = near.shape[1]
    t = lax.axis_index("ten")
    mine = pl.ds(pl.multiple_of(t * half, half), half)
    others = pl.ds(pl.multiple_of((1 - t) * half, half), half)
    tile = width // 2 if width % 256 == 0 else width
    for j in range(0, width, tile):
        lanes = slice(first + j, first + j + tile)
        part = jnp.dot(own[...], matrix[mine, lanes], preferred_element_type=jnp.float32)
        part += jnp.dot(other[...], matrix[others, lanes], preferred_element_type=jnp.float32)
        for i, k in enumerate(order):
            block = part[k * lines : (k + 1) * lines]
            if i < len(order) // 2:
                near[i * lines : (i + 1) * lines, j : j + tile] = block
            else:
                i -= len(order) // 2
                far[i * lines : (i + 1) * lines, j : j + tile] = block.astype(jnp.bfloat16)


def hop_sum_kernel(kept, received, columns_in, keep, sent, columns):
    rows = keep.shape[0]
    columns[...] = columns_in[...]
    total = kept[...] + received[...].astype(jnp.float32)
    keep[...] = total[:rows]
    sent[...] = total[rows:].astype(jnp.bfloat16)


def hop_sum_both_kernel(*refs):
    *parts, columns_in, keep, sent, columns = refs
    columns[...] = columns_in[...]
    count = len(parts) // 2
    rows = keep.shape[0]
    width = keep.shape[1] // count
    for c in range(count):
        lanes = slice(c * width, (c + 1) * width)
        total = parts[c][...] + parts[count + c][...].astype(jnp.float32)
        keep[:, lanes] = total[:rows]
        sent[:, lanes] = total[rows:].astype(jnp.bfloat16)


def attention_kernel(n, kv_heads, order, masks, queries, held_a, held_b, after, context, columns):
    rows = queries.shape[0]
    group = queries.shape[1] // (HEAD_SIZE * kv_heads)
    s = lax.axis_index("seq")
    keys_total = n * rows
    column = lax.broadcasted_iota(jnp.int32, (1, keys_total), 1)
    position = column
    for at, k in enumerate(order):
        inside = (column >= at * rows) & (column < (at + 1) * rows)
        position = jnp.where(inside, column + (lax.bitwise_xor(s, k) - s - at) * rows, position)
    row = lax.rem(lax.broadcasted_iota(jnp.int32, (group * rows, keys_total), 0), rows)
    allowed = position <= row
    sums = jnp.zeros((1, keys_total), jnp.float32)
    for g in range(kv_heads):
        key_lanes = slice(g * HEAD_SIZE, (g + 1) * HEAD_SIZE)
        value_lanes = slice((kv_heads + g) * HEAD_SIZE, (kv_heads + g + 1) * HEAD_SIZE)
        key = jnp.concatenate([held_a[:, key_lanes], held_b[:, key_lanes]], axis=0)
        value = jnp.concatenate([held_a[:, value_lanes], held_b[:, value_lanes]], axis=0)
        heads = range(g * group, (g + 1) * group)
        stacked = jnp.concatenate([queries[:, h * HEAD_SIZE : (h + 1) * HEAD_SIZE] for h in heads], axis=0)
        scores = lax.dot_general(
            stacked, key, (((1,), (1,)), ((), ())), preferred_element_type=jnp.float32
        ) * HEAD_SIZE ** (-0.5)
        scores = jnp.where(allowed, scores, -1e30)
        weights = jnp.exp(scores - jnp.max(scores, axis=1, keepdims=True))
        inverse = 1.0 / jnp.sum(weights, axis=1, keepdims=True)
        mixed = jnp.dot(weights.astype(jnp.bfloat16), value, preferred_element_type=jnp.float32) * inverse
        for i, h in enumerate(heads):
            context[:, h * HEAD_SIZE : (h + 1) * HEAD_SIZE] = mixed[i * rows : (i + 1) * rows]
        sums += jnp.sum(weights * inverse, axis=0, keepdims=True)
    for at, k in enumerate(order):
        i = halving_order(n, masks).index(k)
        columns[i : i + 1, :] = sums[:, at * rows : (at + 1) * rows]


def finish_kernel(bias, kept, received, out):
    out[...] = kept[...] + received[...].astype(jnp.float32) + bias[...]


def shards(queries, keys, values, hidden, norm_gain, retained_lists, counts, affine_matrix, affine_offset_vector):
    n = lax.axis_size("seq")
    rows, model = hidden.shape
    kv_heads = keys.shape[1] // HEAD_SIZE
    half = affine_matrix.shape[0] // 2
    width = affine_matrix.shape[1]
    survivors = n * rows // 2
    lines = survivors // n
    chunk = width // 2
    near = survivors // 2
    f32, bf16, i32 = jnp.float32, jnp.bfloat16, jnp.int32
    shape = jax.ShapeDtypeStruct
    dma = pltpu.SemaphoreType.DMA

    def trade(x, k):
        return lax.ppermute(x, "seq", [(i, i ^ k) for i in range(n)])

    def trade_across(x, k):
        return lax.ppermute(x, ("seq", "ten"), [(2 * i + t, 2 * (i ^ k) + 1 - t) for i in range(n) for t in range(2)])

    def swap(x):
        return lax.ppermute(x, "ten", [(0, 1), (1, 0)])

    def column_hop(columns, mask):
        left = columns.shape[0] // 2
        return columns[:left] + trade(columns[left:], mask)

    pair, *chosen = call(
        functools.partial(norm_select_kernel, n),
        "norm_select",
        (hidden, norm_gain.reshape(1, model), retained_lists.reshape(1, rows), keys, values),
        [shape((rows, 2 * keys.shape[1]), bf16)] + [shape((rows, half), bf16)] * n,
        4 * rows * model,
        limit=16,
        in_specs=[ANY] * 5,
        remote=5,
        scratch=[pltpu.VMEM((rows, model), bf16), pltpu.VMEM((1, model), f32), pltpu.VMEM((1, rows), i32), dma((8,))],
    )
    received = [chosen[0]] + [trade(chosen[k], k) for k in range(1, n)]
    turns = [k for i in range(n // 2) for k in (n // 2 + i, i) if k]
    matrix, queries, target = call(
        functools.partial(stage_kernel, n),
        "stage",
        (counts, affine_matrix, queries, *[received[k] for k in turns[:5]]),
        [shape(affine_matrix.shape, bf16), shape(queries.shape, bf16), shape((1, n * rows), i32)],
        1500 * affine_matrix.size,
        in_specs=[ANY] * 8,
        remote=3,
        scratch=[pltpu.SMEM(counts.shape, i32), dma((3,))],
    )
    held, order, mask = pair, [0], n // 2
    while mask > 1:
        held = jnp.concatenate([held, trade(held, mask)], axis=0)
        order = order + [k ^ mask for k in order]
        mask //= 2
    held_other = trade(held, 1)
    order = order + [k ^ 1 for k in order]

    (own,) = call(
        functools.partial(compact_kernel, n),
        "compact",
        (target, held_other, *received),
        [shape((survivors, half), bf16)],
        2 * survivors * n * rows * half,
        in_specs=[VMEM, ANY] + [VMEM] * n,
    )
    other = swap(own)
    rest = [1 << i for i in range(2, n.bit_length() - 1)]
    masks = [[1, 2] + rest, [2, 1] + rest]
    context, columns = call(
        functools.partial(attention_kernel, n, kv_heads, order, masks[0]),
        "attention",
        (queries, held, held_other, own),
        [shape(queries.shape, f32), shape((n, rows), f32)],
        4 * rows * n * rows * queries.shape[1],
        limit=32,
        in_specs=[VMEM] * 3 + [ANY],
    )

    products = [
        call(
            functools.partial(project_kernel, c * chunk, halving_order(n, masks[c])),
            "project",
            (own, other, matrix, columns),
            [shape((near, chunk), f32), shape((near, chunk), bf16)],
            4 * survivors * half * chunk,
            in_specs=[VMEM] * 3 + [ANY],
        )
        for c in range(2)
    ]
    kept = [product[0] for product in products]
    arrived = [trade(product[1], masks[c][0]) for c, product in enumerate(products)]
    far = columns[n // 2 :]
    columns = columns[: n // 2]
    columns = columns + swap(columns) + trade(far, 1) + trade_across(far, 1)
    lines_left = near // 2
    for c in (1, 0):
        keep, sent, columns = call(
            hop_sum_kernel,
            "hop_sum",
            (kept[c], arrived[c], columns),
            [shape((lines_left, chunk), f32), shape((lines_left, chunk), bf16), shape(columns.shape, f32)],
            near * chunk,
        )
        kept[c], arrived[c] = keep, trade(sent, masks[c][1])
    columns = column_hop(columns, masks[0][1])
    for mask in rest:
        lines_left //= 2
        keep, sent, columns = call(
            hop_sum_both_kernel,
            "hop_sum_both",
            (*kept, *arrived, columns),
            [shape((lines_left, width), f32), shape((lines_left, width), bf16), shape(columns.shape, f32)],
            lines_left * width,
        )
        kept, arrived = [keep], [trade(sent, mask)]
        columns = column_hop(columns, mask)

    (triples,) = call(
        finish_kernel,
        "finish",
        (affine_offset_vector.reshape(1, width), kept[0], arrived[0]),
        [shape((lines, width), f32)],
        n * lines * width,
    )
    return (context, columns.reshape(rows) / QUERY_HEADS, triples)


def solution(mesh):
    in_specs = (
        P(("grp", "seq"), "ten"),
        P(("grp", "seq"), "ten"),
        P(("grp", "seq"), "ten"),
        P(("grp", "seq"), None),
        P(),
        P(("grp", "seq")),
        P("grp"),
        P("seq", "ten"),
        P("ten"),
    )
    out_specs = (P(("grp", "seq"), "ten"), P(("grp", "seq")), P(("grp", "seq"), "ten"))
    return jax.shard_map(shards, mesh=mesh, in_specs=in_specs, out_specs=out_specs, check_vma=False)
```

```python
import functools
import math

import jax
import jax.numpy as jnp
from jax import lax
from jax.experimental import pallas as pl
from jax.experimental.pallas import tpu as pltpu
from jax.sharding import PartitionSpec as P

HEAD_SIZE = 128
QUERY_HEADS = 32
VMEM = pl.BlockSpec(memory_space=pltpu.VMEM)
ANY = pl.BlockSpec(memory_space=pl.ANY)
MIB = 1024 * 1024


def call(body, name, inputs, outputs, flops, limit=16, in_specs=None, scratch=(), remote=0):
    inputs = [pltpu.with_memory_space_constraint(x, pltpu.HBM) if i < remote else x for i, x in enumerate(inputs)]
    size = sum(math.prod(x.shape) * x.dtype.itemsize for x in list(inputs) + list(outputs))
    return pl.pallas_call(
        body,
        out_shape=list(outputs),
        in_specs=in_specs or [VMEM] * len(inputs),
        out_specs=[VMEM] * len(outputs),
        scratch_shapes=list(scratch),
        compiler_params=pltpu.CompilerParams(vmem_limit_bytes=limit * MIB),
        cost_estimate=pl.CostEstimate(flops=flops, bytes_accessed=size, transcendentals=0),
        name=name,
    )(*inputs)


def norm_select_kernel(n, hidden_in, gain_in, kept_in, keys_in, values_in, *refs):
    outs, (hidden, gain, kept, pair, sems) = refs[:n], refs[n:]
    rows, width = hidden.shape
    block = width // n
    half = block // 2
    pieces = 4
    piece = width // pieces
    key_width = keys_in.shape[1]
    loads = [
        pltpu.make_async_copy(
            hidden_in.at[:, i * piece : (i + 1) * piece], hidden.at[:, i * piece : (i + 1) * piece], sems.at[i]
        )
        for i in range(pieces)
    ]
    loads += [
        pltpu.make_async_copy(gain_in, gain, sems.at[pieces]),
        pltpu.make_async_copy(kept_in, kept, sems.at[pieces + 1]),
        pltpu.make_async_copy(keys_in, pair.at[:, :key_width], sems.at[pieces + 2]),
        pltpu.make_async_copy(values_in, pair.at[:, key_width:], sems.at[pieces + 3]),
    ]
    for load in loads:
        load.start()
    s, t = lax.axis_index("seq"), lax.axis_index("ten")
    step = min(piece, 1024)
    total = jnp.zeros((rows, step), jnp.float32)
    for i in range(pieces):
        loads[i].wait()
        for j in range(i * piece, (i + 1) * piece, step):
            part = hidden[:, j : j + step].astype(jnp.float32)
            total += part * part
    scale = lax.rsqrt(jnp.sum(total, axis=1, keepdims=True) / width + 1e-06)
    for load in loads[pieces:]:
        load.wait()
    selector = (kept[...] == lax.broadcasted_iota(jnp.int32, (rows, rows), 0)).astype(jnp.bfloat16)
    for k in range(n):
        start = pl.multiple_of(lax.bitwise_xor(s, k) * block + t * half, half)
        columns = pl.ds(start, half)
        normed = (hidden[:, columns].astype(jnp.float32) * scale * gain[:, columns]).astype(jnp.bfloat16)
        outs[k][:, half:] = pair[...]
        outs[k][:, :half] = lax.dot_general(
            selector, normed, (((0,), (0,)), ((), ())), preferred_element_type=jnp.float32
        ).astype(jnp.bfloat16)


def stage_kernel(n, counts_in, matrix_in, queries_in, *refs):
    matrix, queries, target, counts, sems = refs[-5:]
    loads = [
        pltpu.make_async_copy(counts_in, counts, sems.at[0]),
        pltpu.make_async_copy(matrix_in, matrix, sems.at[1]),
        pltpu.make_async_copy(queries_in, queries, sems.at[2]),
    ]
    for load in loads:
        load.start()
    rows = target.shape[1] // n
    s = lax.axis_index("seq")
    loads[0].wait()
    slot_all = lax.broadcasted_iota(jnp.int32, (1, n * rows), 1)
    found = jnp.full((1, n * rows), -1, jnp.int32)
    for k in range(n):
        source = lax.bitwise_xor(s, k)
        begin = jnp.int32(0)
        for i in range(n):
            begin += jnp.where(i < source, counts[i], 0)
        slot = slot_all - k * rows
        inside = (slot >= 0) & (slot < counts[source])
        found = jnp.where(inside, begin + slot, found)
    target[...] = found
    for load in loads[1:]:
        load.wait()


def compact_kernel(n, target, *refs):
    blocks, out = refs[:n], refs[n]
    lines = out.shape[0] // n
    s = lax.axis_index("seq")
    received = jnp.concatenate([b[:, : out.shape[1]] for b in blocks], axis=0)
    line = lax.broadcasted_iota(jnp.int32, (lines, received.shape[0]), 0)
    pick = jnp.concatenate(
        [(line + lax.bitwise_xor(s, k) * lines == target[...]).astype(jnp.float32) for k in range(n)], axis=0
    ).astype(jnp.bfloat16)
    out[...] = jnp.dot(pick, received, preferred_element_type=jnp.float32).astype(jnp.bfloat16)


def halving_order(n, masks):
    return sorted(range(n), key=lambda k: [k & mask for mask in masks])


def project_kernel(first, order, own, other, matrix, after, near, far):
    survivors, half = own.shape
    lines = survivors // len(order)
    width = near.shape[1]
    t = lax.axis_index("ten")
    mine = pl.ds(pl.multiple_of(t * half, half), half)
    others = pl.ds(pl.multiple_of((1 - t) * half, half), half)
    tile = width // 2 if width % 256 == 0 else width
    for j in range(0, width, tile):
        lanes = slice(first + j, first + j + tile)
        part = jnp.dot(own[...], matrix[mine, lanes], preferred_element_type=jnp.float32)
        part += jnp.dot(other[...], matrix[others, lanes], preferred_element_type=jnp.float32)
        for i, k in enumerate(order):
            block = part[k * lines : (k + 1) * lines]
            if i < len(order) // 2:
                near[i * lines : (i + 1) * lines, j : j + tile] = block
            else:
                i -= len(order) // 2
                far[i * lines : (i + 1) * lines, j : j + tile] = block.astype(jnp.bfloat16)


def hop_sum_kernel(kept, received, columns_in, keep, sent, columns):
    rows = keep.shape[0]
    columns[...] = columns_in[...]
    total = kept[...] + received[...].astype(jnp.float32)
    keep[...] = total[:rows]
    sent[...] = total[rows:].astype(jnp.bfloat16)


def hop_sum_both_kernel(*refs):
    *parts, columns_in, keep, sent, columns = refs
    columns[...] = columns_in[...]
    count = len(parts) // 2
    rows = keep.shape[0]
    width = keep.shape[1] // count
    for c in range(count):
        lanes = slice(c * width, (c + 1) * width)
        total = parts[c][...] + parts[count + c][...].astype(jnp.float32)
        keep[:, lanes] = total[:rows]
        sent[:, lanes] = total[rows:].astype(jnp.bfloat16)


def attention_kernel(n, kv_heads, masks, queries, after, *refs):
    blocks, (context, columns) = refs[:n], refs[n:]
    first = blocks[0].shape[1] - 2 * kv_heads * HEAD_SIZE
    rows = queries.shape[0]
    group = queries.shape[1] // (HEAD_SIZE * kv_heads)
    s = lax.axis_index("seq")
    keys_total = n * rows
    column = lax.broadcasted_iota(jnp.int32, (1, keys_total), 1)
    position = column
    for k in range(n):
        inside = (column >= k * rows) & (column < (k + 1) * rows)
        position = jnp.where(inside, column + (lax.bitwise_xor(s, k) - s - k) * rows, position)
    row = lax.rem(lax.broadcasted_iota(jnp.int32, (group * rows, keys_total), 0), rows)
    allowed = position <= row
    sums = jnp.zeros((1, keys_total), jnp.float32)
    for g in range(kv_heads):
        key_at, value_at = first + g * HEAD_SIZE, first + (kv_heads + g) * HEAD_SIZE
        key = jnp.concatenate([b[:, key_at : key_at + HEAD_SIZE] for b in blocks], axis=0)
        value = jnp.concatenate([b[:, value_at : value_at + HEAD_SIZE] for b in blocks], axis=0)
        heads = range(g * group, (g + 1) * group)
        stacked = jnp.concatenate([queries[:, h * HEAD_SIZE : (h + 1) * HEAD_SIZE] for h in heads], axis=0)
        scores = lax.dot_general(
            stacked, key, (((1,), (1,)), ((), ())), preferred_element_type=jnp.float32
        ) * HEAD_SIZE ** (-0.5)
        scores = jnp.where(allowed, scores, -1e30)
        weights = jnp.exp(scores - jnp.max(scores, axis=1, keepdims=True))
        inverse = 1.0 / jnp.sum(weights, axis=1, keepdims=True)
        mixed = jnp.dot(weights.astype(jnp.bfloat16), value, preferred_element_type=jnp.float32) * inverse
        for i, h in enumerate(heads):
            context[:, h * HEAD_SIZE : (h + 1) * HEAD_SIZE] = mixed[i * rows : (i + 1) * rows]
        sums += jnp.sum(weights * inverse, axis=0, keepdims=True)
    for i, k in enumerate(halving_order(n, masks)):
        columns[i : i + 1, :] = sums[:, k * rows : (k + 1) * rows]


def finish_kernel(bias, kept, received, out):
    out[...] = kept[...] + received[...].astype(jnp.float32) + bias[...]


def shards(queries, keys, values, hidden, norm_gain, retained_lists, counts, affine_matrix, affine_offset_vector):
    n = lax.axis_size("seq")
    rows, model = hidden.shape
    kv_heads = keys.shape[1] // HEAD_SIZE
    half = affine_matrix.shape[0] // 2
    width = affine_matrix.shape[1]
    survivors = n * rows // 2
    lines = survivors // n
    chunk = width // 2
    near = survivors // 2
    f32, bf16, i32 = jnp.float32, jnp.bfloat16, jnp.int32
    shape = jax.ShapeDtypeStruct
    dma = pltpu.SemaphoreType.DMA

    def trade(x, k):
        return lax.ppermute(x, "seq", [(i, i ^ k) for i in range(n)])

    def trade_across(x, k):
        return lax.ppermute(x, ("seq", "ten"), [(2 * i + t, 2 * (i ^ k) + 1 - t) for i in range(n) for t in range(2)])

    def swap(x):
        return lax.ppermute(x, "ten", [(0, 1), (1, 0)])

    def column_hop(columns, mask):
        left = columns.shape[0] // 2
        return columns[:left] + trade(columns[left:], mask)

    chosen = call(
        functools.partial(norm_select_kernel, n),
        "norm_select",
        (hidden, norm_gain.reshape(1, model), retained_lists.reshape(1, rows), keys, values),
        [shape((rows, half + 2 * keys.shape[1]), bf16)] * n,
        4 * rows * model,
        limit=16,
        in_specs=[ANY] * 5,
        remote=5,
        scratch=[pltpu.VMEM((rows, model), bf16), pltpu.VMEM((1, model), f32), pltpu.VMEM((1, rows), i32), pltpu.VMEM((rows, 2 * keys.shape[1]), bf16), dma((8,))],
    )
    received = [chosen[0]] + [trade(chosen[k], k) for k in range(1, n)]
    turns = [k for i in range(n // 2) for k in (n // 2 + i, i) if k]
    matrix, queries, target = call(
        functools.partial(stage_kernel, n),
        "stage",
        (counts, affine_matrix, queries, *[received[k] for k in turns[:5]]),
        [shape(affine_matrix.shape, bf16), shape(queries.shape, bf16), shape((1, n * rows), i32)],
        1500 * affine_matrix.size,
        in_specs=[ANY] * 8,
        remote=3,
        scratch=[pltpu.SMEM(counts.shape, i32), dma((3,))],
    )
    (own,) = call(
        functools.partial(compact_kernel, n),
        "compact",
        (target, *received),
        [shape((survivors, half), bf16)],
        2 * survivors * n * rows * half,
    )
    other = swap(own)
    rest = [1 << i for i in range(2, n.bit_length() - 1)]
    masks = [[1, 2] + rest, [2, 1] + rest]
    context, columns = call(
        functools.partial(attention_kernel, n, kv_heads, masks[0]),
        "attention",
        (queries, own, *received),
        [shape(queries.shape, f32), shape((n, rows), f32)],
        4 * rows * n * rows * queries.shape[1],
        limit=32,
        in_specs=[VMEM, ANY] + [VMEM] * n,
    )

    products = [
        call(
            functools.partial(project_kernel, c * chunk, halving_order(n, masks[c])),
            "project",
            (own, other, matrix, columns),
            [shape((near, chunk), f32), shape((near, chunk), bf16)],
            4 * survivors * half * chunk,
            in_specs=[VMEM] * 3 + [ANY],
        )
        for c in range(2)
    ]
    kept = [product[0] for product in products]
    arrived = [trade(product[1], masks[c][0]) for c, product in enumerate(products)]
    far = columns[n // 2 :]
    columns = columns[: n // 2]
    columns = columns + swap(columns) + trade(far, 1) + trade_across(far, 1)
    lines_left = near // 2
    for c in (1, 0):
        keep, sent, columns = call(
            hop_sum_kernel,
            "hop_sum",
            (kept[c], arrived[c], columns),
            [shape((lines_left, chunk), f32), shape((lines_left, chunk), bf16), shape(columns.shape, f32)],
            near * chunk,
        )
        kept[c], arrived[c] = keep, trade(sent, masks[c][1])
    columns = column_hop(columns, masks[0][1])
    for mask in rest:
        lines_left //= 2
        keep, sent, columns = call(
            hop_sum_both_kernel,
            "hop_sum_both",
            (*kept, *arrived, columns),
            [shape((lines_left, width), f32), shape((lines_left, width), bf16), shape(columns.shape, f32)],
            lines_left * width,
        )
        kept, arrived = [keep], [trade(sent, mask)]
        columns = column_hop(columns, mask)

    (triples,) = call(
        finish_kernel,
        "finish",
        (affine_offset_vector.reshape(1, width), kept[0], arrived[0]),
        [shape((lines, width), f32)],
        n * lines * width,
    )
    return (context, columns.reshape(rows) / QUERY_HEADS, triples)


def solution(mesh):
    in_specs = (
        P(("grp", "seq"), "ten"),
        P(("grp", "seq"), "ten"),
        P(("grp", "seq"), "ten"),
        P(("grp", "seq"), None),
        P(),
        P(("grp", "seq")),
        P("grp"),
        P("seq", "ten"),
        P("ten"),
    )
    out_specs = (P(("grp", "seq"), "ten"), P(("grp", "seq")), P(("grp", "seq"), "ten"))
    return jax.shard_map(shards, mesh=mesh, in_specs=in_specs, out_specs=out_specs, check_vma=False)
```

```python
import functools
import math

import jax
import jax.numpy as jnp
from jax import lax
from jax.experimental import pallas as pl
from jax.experimental.pallas import tpu as pltpu
from jax.sharding import PartitionSpec as P

HEAD_SIZE = 128
QUERY_HEADS = 32
VMEM = pl.BlockSpec(memory_space=pltpu.VMEM)
ANY = pl.BlockSpec(memory_space=pl.ANY)
MIB = 1024 * 1024


def call(body, name, inputs, outputs, flops, limit=16, in_specs=None, scratch=(), remote=0):
    inputs = [pltpu.with_memory_space_constraint(x, pltpu.HBM) if i < remote else x for i, x in enumerate(inputs)]
    size = sum(math.prod(x.shape) * x.dtype.itemsize for x in list(inputs) + list(outputs))
    return pl.pallas_call(
        body,
        out_shape=list(outputs),
        in_specs=in_specs or [VMEM] * len(inputs),
        out_specs=[VMEM] * len(outputs),
        scratch_shapes=list(scratch),
        compiler_params=pltpu.CompilerParams(vmem_limit_bytes=limit * MIB),
        cost_estimate=pl.CostEstimate(flops=flops, bytes_accessed=size, transcendentals=0),
        name=name,
    )(*inputs)


def norm_select_kernel(n, hidden_in, gain_in, kept_in, keys_in, values_in, *refs):
    outs, (hidden, gain, kept, pair, sems) = refs[:n], refs[n:]
    rows, width = hidden.shape
    block = width // n
    half = block // 2
    pieces = 4
    piece = width // pieces
    key_width = keys_in.shape[1]
    loads = [
        pltpu.make_async_copy(
            hidden_in.at[:, i * piece : (i + 1) * piece], hidden.at[:, i * piece : (i + 1) * piece], sems.at[i]
        )
        for i in range(pieces)
    ]
    loads += [
        pltpu.make_async_copy(gain_in, gain, sems.at[pieces]),
        pltpu.make_async_copy(kept_in, kept, sems.at[pieces + 1]),
        pltpu.make_async_copy(keys_in, pair.at[:, :key_width], sems.at[pieces + 2]),
        pltpu.make_async_copy(values_in, pair.at[:, key_width:], sems.at[pieces + 3]),
    ]
    for load in loads:
        load.start()
    s, t = lax.axis_index("seq"), lax.axis_index("ten")
    step = min(piece, 1024)
    total = jnp.zeros((rows, step), jnp.float32)
    for i in range(pieces):
        loads[i].wait()
        for j in range(i * piece, (i + 1) * piece, step):
            part = hidden[:, j : j + step].astype(jnp.float32)
            total += part * part
    scale = lax.rsqrt(jnp.sum(total, axis=1, keepdims=True) / width + 1e-06)
    for load in loads[pieces:]:
        load.wait()
    selector = (kept[...] == lax.broadcasted_iota(jnp.int32, (rows, rows), 0)).astype(jnp.bfloat16)
    for k in range(n):
        start = pl.multiple_of(lax.bitwise_xor(s, k) * block + t * half, half)
        columns = pl.ds(start, half)
        normed = (hidden[:, columns].astype(jnp.float32) * scale * gain[:, columns]).astype(jnp.bfloat16)
        if k < n // 2:
            outs[k][:, half:] = pair[...]
        outs[k][:, :half] = lax.dot_general(
            selector, normed, (((0,), (0,)), ((), ())), preferred_element_type=jnp.float32
        ).astype(jnp.bfloat16)


def stage_kernel(n, counts_in, matrix_in, queries_in, *refs):
    matrix, queries, target, counts, sems = refs[-5:]
    loads = [
        pltpu.make_async_copy(counts_in, counts, sems.at[0]),
        pltpu.make_async_copy(matrix_in, matrix, sems.at[1]),
        pltpu.make_async_copy(queries_in, queries, sems.at[2]),
    ]
    for load in loads:
        load.start()
    rows = target.shape[1] // n
    s = lax.axis_index("seq")
    loads[0].wait()
    slot_all = lax.broadcasted_iota(jnp.int32, (1, n * rows), 1)
    found = jnp.full((1, n * rows), -1, jnp.int32)
    for k in range(n):
        source = lax.bitwise_xor(s, k)
        begin = jnp.int32(0)
        for i in range(n):
            begin += jnp.where(i < source, counts[i], 0)
        slot = slot_all - k * rows
        inside = (slot >= 0) & (slot < counts[source])
        found = jnp.where(inside, begin + slot, found)
    target[...] = found
    for load in loads[1:]:
        load.wait()


def compact_kernel(n, target, *refs):
    blocks, (out, held) = refs[:n], refs[n:]
    rows, half = blocks[0].shape[0], out.shape[1]
    for k in range(n // 2):
        held[k * rows : (k + 1) * rows] = blocks[k][:, half:]
    lines = out.shape[0] // n
    s = lax.axis_index("seq")
    received = jnp.concatenate([b[:, :half] for b in blocks], axis=0)
    line = lax.broadcasted_iota(jnp.int32, (lines, received.shape[0]), 0)
    pick = jnp.concatenate(
        [(line + lax.bitwise_xor(s, k) * lines == target[...]).astype(jnp.float32) for k in range(n)], axis=0
    ).astype(jnp.bfloat16)
    out[...] = jnp.dot(pick, received, preferred_element_type=jnp.float32).astype(jnp.bfloat16)


def halving_order(n, masks):
    return sorted(range(n), key=lambda k: [k & mask for mask in masks])


def project_kernel(first, order, own, other, matrix, near, far):
    survivors, half = own.shape
    lines = survivors // len(order)
    width = near.shape[1]
    t = lax.axis_index("ten")
    mine = pl.ds(pl.multiple_of(t * half, half), half)
    others = pl.ds(pl.multiple_of((1 - t) * half, half), half)
    tile = width // 2 if width % 256 == 0 else width
    for j in range(0, width, tile):
        lanes = slice(first + j, first + j + tile)
        part = jnp.dot(own[...], matrix[mine, lanes], preferred_element_type=jnp.float32)
        part += jnp.dot(other[...], matrix[others, lanes], preferred_element_type=jnp.float32)
        for i, k in enumerate(order):
            block = part[k * lines : (k + 1) * lines]
            if i < len(order) // 2:
                near[i * lines : (i + 1) * lines, j : j + tile] = block
            else:
                i -= len(order) // 2
                far[i * lines : (i + 1) * lines, j : j + tile] = block.astype(jnp.bfloat16)


def hop_sum_kernel(kept, received, after, keep, sent):
    rows = keep.shape[0]
    total = kept[...] + received[...].astype(jnp.float32)
    keep[...] = total[:rows]
    sent[...] = total[rows:].astype(jnp.bfloat16)


def hop_sum_both_kernel(*refs):
    *parts, keep, sent = refs
    count = len(parts) // 2
    rows = keep.shape[0]
    width = keep.shape[1] // count
    for c in range(count):
        lanes = slice(c * width, (c + 1) * width)
        total = parts[c][...] + parts[count + c][...].astype(jnp.float32)
        keep[:, lanes] = total[:rows]
        sent[:, lanes] = total[rows:].astype(jnp.bfloat16)


def column_sum_kernel(scale, after, *refs):
    *parts, out = refs
    total = parts[0][...]
    for part in parts[1:]:
        total += part[...]
    out[...] = total * scale


def attention_kernel(n, kv_heads, masks, queries, near, far, after, context, columns):
    rows = queries.shape[0]
    group = queries.shape[1] // (HEAD_SIZE * kv_heads)
    s = lax.axis_index("seq")
    keys_total = n * rows
    column = lax.broadcasted_iota(jnp.int32, (1, keys_total), 1)
    position = column
    for k in range(n):
        inside = (column >= k * rows) & (column < (k + 1) * rows)
        position = jnp.where(inside, column + (lax.bitwise_xor(s, k) - s - k) * rows, position)
    row = lax.rem(lax.broadcasted_iota(jnp.int32, (group * rows, keys_total), 0), rows)
    allowed = position <= row
    sums = jnp.zeros((1, keys_total), jnp.float32)
    for g in range(kv_heads):
        key_lanes = slice(g * HEAD_SIZE, (g + 1) * HEAD_SIZE)
        value_lanes = slice((kv_heads + g) * HEAD_SIZE, (kv_heads + g + 1) * HEAD_SIZE)
        key = jnp.concatenate([near[:, key_lanes], far[:, key_lanes]], axis=0)
        value = jnp.concatenate([near[:, value_lanes], far[:, value_lanes]], axis=0)
        heads = range(g * group, (g + 1) * group)
        stacked = jnp.concatenate([queries[:, h * HEAD_SIZE : (h + 1) * HEAD_SIZE] for h in heads], axis=0)
        scores = lax.dot_general(
            stacked, key, (((1,), (1,)), ((), ())), preferred_element_type=jnp.float32
        ) * HEAD_SIZE ** (-0.5)
        scores = jnp.where(allowed, scores, -1e30)
        weights = jnp.exp(scores - jnp.max(scores, axis=1, keepdims=True))
        inverse = 1.0 / jnp.sum(weights, axis=1, keepdims=True)
        mixed = jnp.dot(weights.astype(jnp.bfloat16), value, preferred_element_type=jnp.float32) * inverse
        for i, h in enumerate(heads):
            context[:, h * HEAD_SIZE : (h + 1) * HEAD_SIZE] = mixed[i * rows : (i + 1) * rows]
        sums += jnp.sum(weights * inverse, axis=0, keepdims=True)
    for i, k in enumerate(halving_order(n, masks)):
        columns[i : i + 1, :] = sums[:, k * rows : (k + 1) * rows]


def finish_kernel(bias, kept, received, out):
    out[...] = kept[...] + received[...].astype(jnp.float32) + bias[...]


def shards(queries, keys, values, hidden, norm_gain, retained_lists, counts, affine_matrix, affine_offset_vector):
    n = lax.axis_size("seq")
    rows, model = hidden.shape
    kv_heads = keys.shape[1] // HEAD_SIZE
    half = affine_matrix.shape[0] // 2
    width = affine_matrix.shape[1]
    survivors = n * rows // 2
    lines = survivors // n
    chunk = width // 2
    near = survivors // 2
    f32, bf16, i32 = jnp.float32, jnp.bfloat16, jnp.int32
    shape = jax.ShapeDtypeStruct
    dma = pltpu.SemaphoreType.DMA

    def trade(x, k):
        return lax.ppermute(x, "seq", [(i, i ^ k) for i in range(n)])

    def trade_across(x, k):
        return lax.ppermute(x, ("seq", "ten"), [(2 * i + t, 2 * (i ^ k) + 1 - t) for i in range(n) for t in range(2)])

    def swap(x):
        return lax.ppermute(x, "ten", [(0, 1), (1, 0)])

    chosen = call(
        functools.partial(norm_select_kernel, n),
        "norm_select",
        (hidden, norm_gain.reshape(1, model), retained_lists.reshape(1, rows), keys, values),
        [shape((rows, half + 2 * keys.shape[1]), bf16)] * (n // 2) + [shape((rows, half), bf16)] * (n // 2),
        4 * rows * model,
        limit=16,
        in_specs=[ANY] * 5,
        remote=5,
        scratch=[pltpu.VMEM((rows, model), bf16), pltpu.VMEM((1, model), f32), pltpu.VMEM((1, rows), i32), pltpu.VMEM((rows, 2 * keys.shape[1]), bf16), dma((8,))],
    )
    received = [chosen[0]] + [trade(chosen[k], k) for k in range(1, n)]
    turns = [k for i in range(n // 2) for k in (n // 2 + i, i) if k]
    matrix, queries, target = call(
        functools.partial(stage_kernel, n),
        "stage",
        (counts, affine_matrix, queries, *[received[k] for k in turns[:5]]),
        [shape(affine_matrix.shape, bf16), shape(queries.shape, bf16), shape((1, n * rows), i32)],
        1500 * affine_matrix.size,
        in_specs=[ANY] * 8,
        remote=3,
        scratch=[pltpu.SMEM(counts.shape, i32), dma((3,))],
    )
    own, held = call(
        functools.partial(compact_kernel, n),
        "compact",
        (target, *received),
        [shape((survivors, half), bf16), shape((n // 2 * rows, 2 * keys.shape[1]), bf16)],
        2 * survivors * n * rows * half,
    )
    other = swap(own)
    rest = [1 << i for i in range(2, n.bit_length() - 1)]
    masks = [[1, 2] + rest, [2, 1] + rest]
    products = [
        call(
            functools.partial(project_kernel, c * chunk, halving_order(n, masks[c])),
            "project",
            (own, other, matrix),
            [shape((near, chunk), f32), shape((near, chunk), bf16)],
            4 * survivors * half * chunk,
        )
        for c in range(2)
    ]
    context, columns = call(
        functools.partial(attention_kernel, n, kv_heads, masks[0]),
        "attention",
        (queries, held, trade(held, n // 2), products[1][1]),
        [shape(queries.shape, f32), shape((n, rows), f32)],
        4 * rows * n * rows * queries.shape[1],
        limit=32,
        in_specs=[VMEM] * 3 + [ANY],
    )
    kept = [product[0] for product in products]
    arrived = [trade(product[1], masks[c][0]) for c, product in enumerate(products)]
    lines_left = near // 2
    for c in (1, 0):
        keep, sent = call(
            hop_sum_kernel,
            "hop_sum",
            (kept[c], arrived[c], products[c][1] if c else columns),
            [shape((lines_left, chunk), f32), shape((lines_left, chunk), bf16)],
            near * chunk,
            in_specs=[VMEM] * 2 + [ANY],
        )
        kept[c], arrived[c] = keep, trade(sent, masks[c][1])

    def column_sum(pieces, after, scale=1.0, remote=0):
        (total,) = call(
            functools.partial(column_sum_kernel, scale),
            "column_sum",
            (after, *pieces),
            [shape(pieces[0].shape, f32)],
            0,
            in_specs=[ANY] + [VMEM] * len(pieces),
            remote=remote,
        )
        return total

    pieces = [columns[i * (n // 4) : (i + 1) * (n // 4)] for i in range(4)]
    pieces = pieces[:1] + [trade(x, mask) for x, mask in zip(pieces[1:], (2, 1, 3))]
    for mask in rest:
        lines_left //= 2
        keep, sent = call(
            hop_sum_both_kernel,
            "hop_sum_both",
            (*kept, *arrived),
            [shape((lines_left, width), f32), shape((lines_left, width), bf16)],
            lines_left * width,
        )
        kept, arrived = [keep], [trade(sent, mask)]
        columns = column_sum(pieces, keep)
        left = columns.shape[0] // 2
        own, far = columns[:left], columns[left:]
        pieces = [own, trade(far, mask)]
        if mask == rest[-1]:
            pieces += [swap(own), trade_across(far, mask)]

    (triples,) = call(
        finish_kernel,
        "finish",
        (affine_offset_vector.reshape(1, width), kept[0], arrived[0]),
        [shape((lines, width), f32)],
        n * lines * width,
    )
    scores = column_sum(pieces, triples, 1.0 / QUERY_HEADS, remote=1)
    return (context, scores.reshape(rows), triples)


def solution(mesh):
    in_specs = (
        P(("grp", "seq"), "ten"),
        P(("grp", "seq"), "ten"),
        P(("grp", "seq"), "ten"),
        P(("grp", "seq"), None),
        P(),
        P(("grp", "seq")),
        P("grp"),
        P("seq", "ten"),
        P("ten"),
    )
    out_specs = (P(("grp", "seq"), "ten"), P(("grp", "seq")), P(("grp", "seq"), "ten"))
    return jax.shard_map(shards, mesh=mesh, in_specs=in_specs, out_specs=out_specs, check_vma=False)
```

```python
import functools
import math

import jax
import jax.numpy as jnp
from jax import lax
from jax.experimental import pallas as pl
from jax.experimental.pallas import tpu as pltpu
from jax.sharding import PartitionSpec as P

HEAD_SIZE = 128
QUERY_HEADS = 32
VMEM = pl.BlockSpec(memory_space=pltpu.VMEM)
ANY = pl.BlockSpec(memory_space=pl.ANY)
MIB = 1024 * 1024


def call(body, name, inputs, outputs, flops, limit=16, in_specs=None, scratch=(), remote=0):
    inputs = [pltpu.with_memory_space_constraint(x, pltpu.HBM) if i < remote else x for i, x in enumerate(inputs)]
    size = sum(math.prod(x.shape) * x.dtype.itemsize for x in list(inputs) + list(outputs))
    return pl.pallas_call(
        body,
        out_shape=list(outputs),
        in_specs=in_specs or [VMEM] * len(inputs),
        out_specs=[VMEM] * len(outputs),
        scratch_shapes=list(scratch),
        compiler_params=pltpu.CompilerParams(vmem_limit_bytes=limit * MIB),
        cost_estimate=pl.CostEstimate(flops=flops, bytes_accessed=size, transcendentals=0),
        name=name,
    )(*inputs)


def norm_select_kernel(n, hidden_in, gain_in, kept_in, keys_in, values_in, *refs):
    outs, (hidden, gain, kept, pair, sems) = refs[:n], refs[n:]
    rows, width = hidden.shape
    block = width // n
    half = block // 2
    pieces = 4
    piece = width // pieces
    key_width = keys_in.shape[1]
    loads = [
        pltpu.make_async_copy(
            hidden_in.at[:, i * piece : (i + 1) * piece], hidden.at[:, i * piece : (i + 1) * piece], sems.at[i]
        )
        for i in range(pieces)
    ]
    loads += [
        pltpu.make_async_copy(gain_in, gain, sems.at[pieces]),
        pltpu.make_async_copy(kept_in, kept, sems.at[pieces + 1]),
        pltpu.make_async_copy(keys_in, pair.at[:, :key_width], sems.at[pieces + 2]),
        pltpu.make_async_copy(values_in, pair.at[:, key_width:], sems.at[pieces + 3]),
    ]
    for load in loads:
        load.start()
    s, t = lax.axis_index("seq"), lax.axis_index("ten")
    step = min(piece, 1024)
    total = jnp.zeros((rows, step), jnp.float32)
    for i in range(pieces):
        loads[i].wait()
        for j in range(i * piece, (i + 1) * piece, step):
            part = hidden[:, j : j + step].astype(jnp.float32)
            total += part * part
    scale = lax.rsqrt(jnp.sum(total, axis=1, keepdims=True) / width + 1e-06)
    for load in loads[pieces:]:
        load.wait()
    selector = (kept[...] == lax.broadcasted_iota(jnp.int32, (rows, rows), 0)).astype(jnp.bfloat16)
    for k in range(n):
        start = pl.multiple_of(lax.bitwise_xor(s, k) * block + t * half, half)
        columns = pl.ds(start, half)
        normed = (hidden[:, columns].astype(jnp.float32) * scale * gain[:, columns]).astype(jnp.bfloat16)
        if k < n // 2:
            outs[k][:, half:] = pair[...]
        outs[k][:, :half] = lax.dot_general(
            selector, normed, (((0,), (0,)), ((), ())), preferred_element_type=jnp.float32
        ).astype(jnp.bfloat16)


def stage_kernel(n, counts_in, matrix_in, queries_in, *refs):
    matrix, queries, target, counts, sems = refs[-5:]
    loads = [
        pltpu.make_async_copy(counts_in, counts, sems.at[0]),
        pltpu.make_async_copy(matrix_in, matrix, sems.at[1]),
        pltpu.make_async_copy(queries_in, queries, sems.at[2]),
    ]
    for load in loads:
        load.start()
    rows = target.shape[1] // n
    s = lax.axis_index("seq")
    loads[0].wait()
    slot_all = lax.broadcasted_iota(jnp.int32, (1, n * rows), 1)
    found = jnp.full((1, n * rows), -1, jnp.int32)
    for k in range(n):
        source = lax.bitwise_xor(s, k)
        begin = jnp.int32(0)
        for i in range(n):
            begin += jnp.where(i < source, counts[i], 0)
        slot = slot_all - k * rows
        inside = (slot >= 0) & (slot < counts[source])
        found = jnp.where(inside, begin + slot, found)
    target[...] = found
    for load in loads[1:]:
        load.wait()


def compact_kernel(n, target, *refs):
    blocks, (out, held) = refs[:n], refs[n:]
    rows, half = blocks[0].shape[0], out.shape[1]
    for k in range(n // 2):
        held[k * rows : (k + 1) * rows] = blocks[k][:, half:]
    lines = out.shape[0] // n
    s = lax.axis_index("seq")
    received = jnp.concatenate([b[:, :half] for b in blocks], axis=0)
    line = lax.broadcasted_iota(jnp.int32, (lines, received.shape[0]), 0)
    pick = jnp.concatenate(
        [(line + lax.bitwise_xor(s, k) * lines == target[...]).astype(jnp.float32) for k in range(n)], axis=0
    ).astype(jnp.bfloat16)
    out[...] = jnp.dot(pick, received, preferred_element_type=jnp.float32).astype(jnp.bfloat16)


def halving_order(n, masks):
    return sorted(range(n), key=lambda k: [k & mask for mask in masks])


def project_kernel(first, order, own, other, matrix, near, far):
    survivors, half = own.shape
    lines = survivors // len(order)
    width = near.shape[1]
    t = lax.axis_index("ten")
    mine = pl.ds(pl.multiple_of(t * half, half), half)
    others = pl.ds(pl.multiple_of((1 - t) * half, half), half)
    tile = width // 2 if width % 256 == 0 else width
    for j in range(0, width, tile):
        lanes = slice(first + j, first + j + tile)
        part = jnp.dot(own[...], matrix[mine, lanes], preferred_element_type=jnp.float32)
        part += jnp.dot(other[...], matrix[others, lanes], preferred_element_type=jnp.float32)
        for i, k in enumerate(order):
            block = part[k * lines : (k + 1) * lines]
            if i < len(order) // 2:
                near[i * lines : (i + 1) * lines, j : j + tile] = block
            else:
                i -= len(order) // 2
                far[i * lines : (i + 1) * lines, j : j + tile] = block.astype(jnp.bfloat16)


def hop_sum_kernel(kept, received, after, keep, sent):
    rows = keep.shape[0]
    total = kept[...] + received[...].astype(jnp.float32)
    keep[...] = total[:rows]
    sent[...] = total[rows:].astype(jnp.bfloat16)


def hop_sum_both_kernel(*refs):
    *parts, keep, sent = refs
    count = len(parts) // 2
    rows = keep.shape[0]
    width = keep.shape[1] // count
    for c in range(count):
        lanes = slice(c * width, (c + 1) * width)
        total = parts[c][...] + parts[count + c][...].astype(jnp.float32)
        keep[:, lanes] = total[:rows]
        sent[:, lanes] = total[rows:].astype(jnp.bfloat16)


def column_sum_kernel(scale, after, *refs):
    *parts, out = refs
    total = parts[0][...]
    for part in parts[1:]:
        total += part[...]
    out[...] = total * scale


def attention_kernel(n, kv_heads, masks, queries, near, far, after, context, columns):
    rows = queries.shape[0]
    group = queries.shape[1] // (HEAD_SIZE * kv_heads)
    s = lax.axis_index("seq")
    keys_total = n * rows
    column = lax.broadcasted_iota(jnp.int32, (1, keys_total), 1)
    position = column
    for k in range(n):
        inside = (column >= k * rows) & (column < (k + 1) * rows)
        position = jnp.where(inside, column + (lax.bitwise_xor(s, k) - s - k) * rows, position)
    row = lax.rem(lax.broadcasted_iota(jnp.int32, (group * rows, keys_total), 0), rows)
    allowed = position <= row
    sums = jnp.zeros((1, keys_total), jnp.float32)
    for g in range(kv_heads):
        key_lanes = slice(g * HEAD_SIZE, (g + 1) * HEAD_SIZE)
        value_lanes = slice((kv_heads + g) * HEAD_SIZE, (kv_heads + g + 1) * HEAD_SIZE)
        key = jnp.concatenate([near[:, key_lanes], far[:, key_lanes]], axis=0)
        value = jnp.concatenate([near[:, value_lanes], far[:, value_lanes]], axis=0)
        heads = range(g * group, (g + 1) * group)
        stacked = jnp.concatenate([queries[:, h * HEAD_SIZE : (h + 1) * HEAD_SIZE] for h in heads], axis=0)
        scores = lax.dot_general(
            stacked, key, (((1,), (1,)), ((), ())), preferred_element_type=jnp.float32
        ) * HEAD_SIZE ** (-0.5)
        scores = jnp.where(allowed, scores, -1e30)
        weights = jnp.exp(scores - jnp.max(scores, axis=1, keepdims=True))
        inverse = 1.0 / jnp.sum(weights, axis=1, keepdims=True)
        mixed = jnp.dot(weights.astype(jnp.bfloat16), value, preferred_element_type=jnp.float32) * inverse
        for i, h in enumerate(heads):
            context[:, h * HEAD_SIZE : (h + 1) * HEAD_SIZE] = mixed[i * rows : (i + 1) * rows]
        sums += jnp.sum(weights * inverse, axis=0, keepdims=True)
    for i, k in enumerate(halving_order(n, masks)):
        columns[i : i + 1, :] = sums[:, k * rows : (k + 1) * rows]


def finish_kernel(bias, kept, received, out):
    out[...] = kept[...] + received[...].astype(jnp.float32) + bias[...]


def shards(queries, keys, values, hidden, norm_gain, retained_lists, counts, affine_matrix, affine_offset_vector):
    n = lax.axis_size("seq")
    rows, model = hidden.shape
    kv_heads = keys.shape[1] // HEAD_SIZE
    half = affine_matrix.shape[0] // 2
    width = affine_matrix.shape[1]
    survivors = n * rows // 2
    lines = survivors // n
    chunk = width // 2
    near = survivors // 2
    f32, bf16, i32 = jnp.float32, jnp.bfloat16, jnp.int32
    shape = jax.ShapeDtypeStruct
    dma = pltpu.SemaphoreType.DMA

    def trade(x, k):
        return lax.ppermute(x, "seq", [(i, i ^ k) for i in range(n)])

    def trade_across(x, k):
        return lax.ppermute(x, ("seq", "ten"), [(2 * i + t, 2 * (i ^ k) + 1 - t) for i in range(n) for t in range(2)])

    def swap(x):
        return lax.ppermute(x, "ten", [(0, 1), (1, 0)])

    chosen = call(
        functools.partial(norm_select_kernel, n),
        "norm_select",
        (hidden, norm_gain.reshape(1, model), retained_lists.reshape(1, rows), keys, values),
        [shape((rows, half + 2 * keys.shape[1]), bf16)] * (n // 2) + [shape((rows, half), bf16)] * (n // 2),
        4 * rows * model,
        limit=16,
        in_specs=[ANY] * 5,
        remote=5,
        scratch=[pltpu.VMEM((rows, model), bf16), pltpu.VMEM((1, model), f32), pltpu.VMEM((1, rows), i32), pltpu.VMEM((rows, 2 * keys.shape[1]), bf16), dma((8,))],
    )
    received = [chosen[0]] + [trade(chosen[k], k) for k in range(1, n)]
    turns = [k for i in range(n // 2) for k in (n // 2 + i, i) if k]
    matrix, queries, target = call(
        functools.partial(stage_kernel, n),
        "stage",
        (counts, affine_matrix, queries, *[received[k] for k in turns[:5]]),
        [shape(affine_matrix.shape, bf16), shape(queries.shape, bf16), shape((1, n * rows), i32)],
        1500 * affine_matrix.size,
        in_specs=[ANY] * 8,
        remote=3,
        scratch=[pltpu.SMEM(counts.shape, i32), dma((3,))],
    )
    own, held = call(
        functools.partial(compact_kernel, n),
        "compact",
        (target, *received),
        [shape((survivors, half), bf16), shape((n // 2 * rows, 2 * keys.shape[1]), bf16)],
        2 * survivors * n * rows * half,
    )
    other = swap(own)
    rest = [1 << i for i in range(2, n.bit_length() - 1)]
    masks = [[1, 2] + rest, [2, 1] + rest]
    products = [
        call(
            functools.partial(project_kernel, c * chunk, halving_order(n, masks[c])),
            "project",
            (own, other, matrix),
            [shape((near, chunk), f32), shape((near, chunk), bf16)],
            4 * survivors * half * chunk,
        )
        for c in range(2)
    ]
    context, columns = call(
        functools.partial(attention_kernel, n, kv_heads, masks[0]),
        "attention",
        (queries, held, trade(held, n // 2), products[1][1]),
        [shape(queries.shape, f32), shape((n, rows), f32)],
        120 * rows * n * rows * queries.shape[1],
        limit=32,
        in_specs=[VMEM] * 3 + [ANY],
    )
    kept = [product[0] for product in products]
    arrived = [trade(product[1], masks[c][0]) for c, product in enumerate(products)]
    lines_left = near // 2
    for c in (1, 0):
        keep, sent = call(
            hop_sum_kernel,
            "hop_sum",
            (kept[c], arrived[c], products[c][1] if c else columns),
            [shape((lines_left, chunk), f32), shape((lines_left, chunk), bf16)],
            near * chunk,
            in_specs=[VMEM] * 2 + [ANY],
        )
        kept[c], arrived[c] = keep, trade(sent, masks[c][1])

    def column_sum(pieces, after, scale=1.0, remote=0):
        (total,) = call(
            functools.partial(column_sum_kernel, scale),
            "column_sum",
            (after, *pieces),
            [shape(pieces[0].shape, f32)],
            0,
            in_specs=[ANY] + [VMEM] * len(pieces),
            remote=remote,
        )
        return total

    pieces = [columns[i * (n // 4) : (i + 1) * (n // 4)] for i in range(4)]
    pieces = pieces[:1] + [trade(x, mask) for x, mask in zip(pieces[1:], (2, 1, 3))]
    for mask in rest:
        lines_left //= 2
        keep, sent = call(
            hop_sum_both_kernel,
            "hop_sum_both",
            (*kept, *arrived),
            [shape((lines_left, width), f32), shape((lines_left, width), bf16)],
            lines_left * width,
        )
        kept, arrived = [keep], [trade(sent, mask)]
        columns = column_sum(pieces, keep)
        left = columns.shape[0] // 2
        own, far = columns[:left], columns[left:]
        pieces = [own, trade(far, mask)]
        if mask == rest[-1]:
            pieces += [swap(own), trade_across(far, mask)]

    (triples,) = call(
        finish_kernel,
        "finish",
        (affine_offset_vector.reshape(1, width), kept[0], arrived[0]),
        [shape((lines, width), f32)],
        n * lines * width,
    )
    scores = column_sum(pieces, triples, 1.0 / QUERY_HEADS, remote=1)
    return (context, scores.reshape(rows), triples)


def solution(mesh):
    in_specs = (
        P(("grp", "seq"), "ten"),
        P(("grp", "seq"), "ten"),
        P(("grp", "seq"), "ten"),
        P(("grp", "seq"), None),
        P(),
        P(("grp", "seq")),
        P("grp"),
        P("seq", "ten"),
        P("ten"),
    )
    out_specs = (P(("grp", "seq"), "ten"), P(("grp", "seq")), P(("grp", "seq"), "ten"))
    return jax.shard_map(shards, mesh=mesh, in_specs=in_specs, out_specs=out_specs, check_vma=False)
```

```python
import functools
import math

import jax
import jax.numpy as jnp
from jax import lax
from jax.experimental import pallas as pl
from jax.experimental.pallas import tpu as pltpu
from jax.sharding import PartitionSpec as P

HEAD_SIZE = 128
QUERY_HEADS = 32
VMEM = pl.BlockSpec(memory_space=pltpu.VMEM)
ANY = pl.BlockSpec(memory_space=pl.ANY)
MIB = 1024 * 1024


def call(body, name, inputs, outputs, flops, limit=16, in_specs=None, scratch=(), remote=0):
    inputs = [pltpu.with_memory_space_constraint(x, pltpu.HBM) if i < remote else x for i, x in enumerate(inputs)]
    size = sum(math.prod(x.shape) * x.dtype.itemsize for x in list(inputs) + list(outputs))
    return pl.pallas_call(
        body,
        out_shape=list(outputs),
        in_specs=in_specs or [VMEM] * len(inputs),
        out_specs=[VMEM] * len(outputs),
        scratch_shapes=list(scratch),
        compiler_params=pltpu.CompilerParams(vmem_limit_bytes=limit * MIB),
        cost_estimate=pl.CostEstimate(flops=flops, bytes_accessed=size, transcendentals=0),
        name=name,
    )(*inputs)


def norm_select_kernel(n, hidden_in, gain_in, kept_in, keys_in, values_in, *refs):
    outs, (hidden, gain, kept, pair, sems) = refs[:n], refs[n:]
    rows, width = hidden.shape
    block = width // n
    half = block // 2
    pieces = 4
    piece = width // pieces
    key_width = keys_in.shape[1]
    loads = [
        pltpu.make_async_copy(
            hidden_in.at[:, i * piece : (i + 1) * piece], hidden.at[:, i * piece : (i + 1) * piece], sems.at[i]
        )
        for i in range(pieces)
    ]
    loads += [
        pltpu.make_async_copy(gain_in, gain, sems.at[pieces]),
        pltpu.make_async_copy(kept_in, kept, sems.at[pieces + 1]),
        pltpu.make_async_copy(keys_in, pair.at[:, :key_width], sems.at[pieces + 2]),
        pltpu.make_async_copy(values_in, pair.at[:, key_width:], sems.at[pieces + 3]),
    ]
    for load in loads:
        load.start()
    s, t = lax.axis_index("seq"), lax.axis_index("ten")
    step = min(piece, 1024)
    total = jnp.zeros((rows, step), jnp.float32)
    for i in range(pieces):
        loads[i].wait()
        for j in range(i * piece, (i + 1) * piece, step):
            part = hidden[:, j : j + step].astype(jnp.float32)
            total += part * part
    scale = lax.rsqrt(jnp.sum(total, axis=1, keepdims=True) / width + 1e-06)
    for load in loads[pieces:]:
        load.wait()
    selector = (kept[...] == lax.broadcasted_iota(jnp.int32, (rows, rows), 0)).astype(jnp.bfloat16)
    for k in range(n):
        start = pl.multiple_of(lax.bitwise_xor(s, k) * block + t * half, half)
        columns = pl.ds(start, half)
        normed = (hidden[:, columns].astype(jnp.float32) * scale * gain[:, columns]).astype(jnp.bfloat16)
        if k < n // 2:
            outs[k][:, half:] = pair[...]
        outs[k][:, :half] = lax.dot_general(
            selector, normed, (((0,), (0,)), ((), ())), preferred_element_type=jnp.float32
        ).astype(jnp.bfloat16)


def relay_kernel(count, *refs):
    blocks, outs = refs[:count], refs[len(refs) - count :]
    for block, out in zip(blocks, outs):
        out[...] = block[...]


def stage_kernel(n, counts_in, matrix_in, queries_in, *refs):
    matrix, queries, target, counts, sems = refs[-5:]
    loads = [
        pltpu.make_async_copy(counts_in, counts, sems.at[0]),
        pltpu.make_async_copy(matrix_in, matrix, sems.at[1]),
        pltpu.make_async_copy(queries_in, queries, sems.at[2]),
    ]
    for load in loads:
        load.start()
    rows = target.shape[1] // n
    s = lax.axis_index("seq")
    loads[0].wait()
    slot_all = lax.broadcasted_iota(jnp.int32, (1, n * rows), 1)
    found = jnp.full((1, n * rows), -1, jnp.int32)
    for k in range(n):
        source = lax.bitwise_xor(s, k)
        begin = jnp.int32(0)
        for i in range(n):
            begin += jnp.where(i < source, counts[i], 0)
        slot = slot_all - k * rows
        inside = (slot >= 0) & (slot < counts[source])
        found = jnp.where(inside, begin + slot, found)
    target[...] = found
    for load in loads[1:]:
        load.wait()


def compact_kernel(n, target, *refs):
    blocks, (out, held) = refs[:n], refs[n:]
    rows, half = blocks[0].shape[0], out.shape[1]
    for k in range(n // 2):
        held[k * rows : (k + 1) * rows] = blocks[k][:, half:]
    lines = out.shape[0] // n
    s = lax.axis_index("seq")
    received = jnp.concatenate([b[:, :half] for b in blocks], axis=0)
    line = lax.broadcasted_iota(jnp.int32, (lines, received.shape[0]), 0)
    pick = jnp.concatenate(
        [(line + lax.bitwise_xor(s, k) * lines == target[...]).astype(jnp.float32) for k in range(n)], axis=0
    ).astype(jnp.bfloat16)
    out[...] = jnp.dot(pick, received, preferred_element_type=jnp.float32).astype(jnp.bfloat16)


def halving_order(n, masks):
    return sorted(range(n), key=lambda k: [k & mask for mask in masks])


def project_kernel(first, order, own, other, matrix, near, far):
    survivors, half = own.shape
    lines = survivors // len(order)
    width = near.shape[1]
    t = lax.axis_index("ten")
    mine = pl.ds(pl.multiple_of(t * half, half), half)
    others = pl.ds(pl.multiple_of((1 - t) * half, half), half)
    tile = width // 2 if width % 256 == 0 else width
    for j in range(0, width, tile):
        lanes = slice(first + j, first + j + tile)
        part = jnp.dot(own[...], matrix[mine, lanes], preferred_element_type=jnp.float32)
        part += jnp.dot(other[...], matrix[others, lanes], preferred_element_type=jnp.float32)
        for i, k in enumerate(order):
            block = part[k * lines : (k + 1) * lines]
            if i < len(order) // 2:
                near[i * lines : (i + 1) * lines, j : j + tile] = block
            else:
                i -= len(order) // 2
                far[i * lines : (i + 1) * lines, j : j + tile] = block.astype(jnp.bfloat16)


def hop_sum_kernel(kept, received, after, keep, sent):
    rows = keep.shape[0]
    total = kept[...] + received[...].astype(jnp.float32)
    keep[...] = total[:rows]
    sent[...] = total[rows:].astype(jnp.bfloat16)


def hop_sum_both_kernel(*refs):
    *parts, keep, sent = refs
    count = len(parts) // 2
    rows = keep.shape[0]
    width = keep.shape[1] // count
    for c in range(count):
        lanes = slice(c * width, (c + 1) * width)
        total = parts[c][...] + parts[count + c][...].astype(jnp.float32)
        keep[:, lanes] = total[:rows]
        sent[:, lanes] = total[rows:].astype(jnp.bfloat16)


def column_sum_kernel(scale, after, *refs):
    *parts, out = refs
    total = parts[0][...]
    for part in parts[1:]:
        total += part[...]
    out[...] = total * scale


def attention_kernel(n, kv_heads, masks, queries, near, far, after, context, columns):
    rows = queries.shape[0]
    group = queries.shape[1] // (HEAD_SIZE * kv_heads)
    s = lax.axis_index("seq")
    keys_total = n * rows
    column = lax.broadcasted_iota(jnp.int32, (1, keys_total), 1)
    position = column
    for k in range(n):
        inside = (column >= k * rows) & (column < (k + 1) * rows)
        position = jnp.where(inside, column + (lax.bitwise_xor(s, k) - s - k) * rows, position)
    row = lax.rem(lax.broadcasted_iota(jnp.int32, (group * rows, keys_total), 0), rows)
    allowed = position <= row
    sums = jnp.zeros((1, keys_total), jnp.float32)
    for g in range(kv_heads):
        key_lanes = slice(g * HEAD_SIZE, (g + 1) * HEAD_SIZE)
        value_lanes = slice((kv_heads + g) * HEAD_SIZE, (kv_heads + g + 1) * HEAD_SIZE)
        key = jnp.concatenate([near[:, key_lanes], far[:, key_lanes]], axis=0)
        value = jnp.concatenate([near[:, value_lanes], far[:, value_lanes]], axis=0)
        heads = range(g * group, (g + 1) * group)
        stacked = jnp.concatenate([queries[:, h * HEAD_SIZE : (h + 1) * HEAD_SIZE] for h in heads], axis=0)
        scores = lax.dot_general(
            stacked, key, (((1,), (1,)), ((), ())), preferred_element_type=jnp.float32
        ) * HEAD_SIZE ** (-0.5)
        scores = jnp.where(allowed, scores, -1e30)
        weights = jnp.exp(scores - jnp.max(scores, axis=1, keepdims=True))
        inverse = 1.0 / jnp.sum(weights, axis=1, keepdims=True)
        mixed = jnp.dot(weights.astype(jnp.bfloat16), value, preferred_element_type=jnp.float32) * inverse
        for i, h in enumerate(heads):
            context[:, h * HEAD_SIZE : (h + 1) * HEAD_SIZE] = mixed[i * rows : (i + 1) * rows]
        sums += jnp.sum(weights * inverse, axis=0, keepdims=True)
    for i, k in enumerate(halving_order(n, masks)):
        columns[i : i + 1, :] = sums[:, k * rows : (k + 1) * rows]


def finish_kernel(bias, kept, received, out):
    out[...] = kept[...] + received[...].astype(jnp.float32) + bias[...]


def shards(queries, keys, values, hidden, norm_gain, retained_lists, counts, affine_matrix, affine_offset_vector):
    n = lax.axis_size("seq")
    rows, model = hidden.shape
    kv_heads = keys.shape[1] // HEAD_SIZE
    half = affine_matrix.shape[0] // 2
    width = affine_matrix.shape[1]
    survivors = n * rows // 2
    lines = survivors // n
    chunk = width // 2
    near = survivors // 2
    f32, bf16, i32 = jnp.float32, jnp.bfloat16, jnp.int32
    shape = jax.ShapeDtypeStruct
    dma = pltpu.SemaphoreType.DMA

    def trade(x, k):
        return lax.ppermute(x, "seq", [(i, i ^ k) for i in range(n)])

    def trade_across(x, k):
        return lax.ppermute(x, ("seq", "ten"), [(2 * i + t, 2 * (i ^ k) + 1 - t) for i in range(n) for t in range(2)])

    def swap(x):
        return lax.ppermute(x, "ten", [(0, 1), (1, 0)])

    chosen = call(
        functools.partial(norm_select_kernel, n),
        "norm_select",
        (hidden, norm_gain.reshape(1, model), retained_lists.reshape(1, rows), keys, values),
        [shape((rows, half + 2 * keys.shape[1]), bf16)] * (n // 2) + [shape((rows, half), bf16)] * (n // 2),
        4 * rows * model,
        limit=16,
        in_specs=[ANY] * 5,
        remote=5,
        scratch=[pltpu.VMEM((rows, model), bf16), pltpu.VMEM((1, model), f32), pltpu.VMEM((1, rows), i32), pltpu.VMEM((rows, 2 * keys.shape[1]), bf16), dma((8,))],
    )
    last = range(n - n // 4, n)
    received = [chosen[0]] + [trade(chosen[k], k) for k in range(1, last[0])]
    relayed = call(
        functools.partial(relay_kernel, len(last)),
        "relay",
        (*[chosen[k] for k in last], *received[1 : n // 2]),
        [shape((rows, half), bf16)] * len(last),
        0,
        in_specs=[VMEM] * len(last) + [ANY] * (n // 2 - 1),
    )
    received += [trade(x, k) for k, x in zip(last, relayed)]
    matrix, queries, target = call(
        functools.partial(stage_kernel, n),
        "stage",
        (counts, affine_matrix, queries, *received[n // 2 : last[0]]),
        [shape(affine_matrix.shape, bf16), shape(queries.shape, bf16), shape((1, n * rows), i32)],
        1500 * affine_matrix.size,
        in_specs=[ANY] * (3 + n // 4),
        remote=3,
        scratch=[pltpu.SMEM(counts.shape, i32), dma((3,))],
    )
    own, held = call(
        functools.partial(compact_kernel, n),
        "compact",
        (target, *received),
        [shape((survivors, half), bf16), shape((n // 2 * rows, 2 * keys.shape[1]), bf16)],
        2 * survivors * n * rows * half,
    )
    other = swap(own)
    rest = [1 << i for i in range(2, n.bit_length() - 1)]
    masks = [[1, 2] + rest, [2, 1] + rest]
    products = [
        call(
            functools.partial(project_kernel, c * chunk, halving_order(n, masks[c])),
            "project",
            (own, other, matrix),
            [shape((near, chunk), f32), shape((near, chunk), bf16)],
            4 * survivors * half * chunk,
        )
        for c in range(2)
    ]
    context, columns = call(
        functools.partial(attention_kernel, n, kv_heads, masks[0]),
        "attention",
        (queries, held, trade(held, n // 2), products[1][1]),
        [shape(queries.shape, f32), shape((n, rows), f32)],
        120 * rows * n * rows * queries.shape[1],
        limit=32,
        in_specs=[VMEM] * 3 + [ANY],
    )
    kept = [product[0] for product in products]
    arrived = [trade(product[1], masks[c][0]) for c, product in enumerate(products)]
    lines_left = near // 2
    for c in (1, 0):
        keep, sent = call(
            hop_sum_kernel,
            "hop_sum",
            (kept[c], arrived[c], products[c][1] if c else columns),
            [shape((lines_left, chunk), f32), shape((lines_left, chunk), bf16)],
            near * chunk,
            in_specs=[VMEM] * 2 + [ANY],
        )
        kept[c], arrived[c] = keep, trade(sent, masks[c][1])

    def column_sum(pieces, after, scale=1.0, remote=0):
        (total,) = call(
            functools.partial(column_sum_kernel, scale),
            "column_sum",
            (after, *pieces),
            [shape(pieces[0].shape, f32)],
            0,
            in_specs=[ANY] + [VMEM] * len(pieces),
            remote=remote,
        )
        return total

    pieces = [columns[i * (n // 4) : (i + 1) * (n // 4)] for i in range(4)]
    pieces = pieces[:1] + [trade(x, mask) for x, mask in zip(pieces[1:], (2, 1, 3))]
    for mask in rest:
        lines_left //= 2
        keep, sent = call(
            hop_sum_both_kernel,
            "hop_sum_both",
            (*kept, *arrived),
            [shape((lines_left, width), f32), shape((lines_left, width), bf16)],
            lines_left * width,
        )
        kept, arrived = [keep], [trade(sent, mask)]
        columns = column_sum(pieces, keep)
        left = columns.shape[0] // 2
        own, far = columns[:left], columns[left:]
        pieces = [own, trade(far, mask)]
        if mask == rest[-1]:
            pieces += [swap(own), trade_across(far, mask)]

    (triples,) = call(
        finish_kernel,
        "finish",
        (affine_offset_vector.reshape(1, width), kept[0], arrived[0]),
        [shape((lines, width), f32)],
        n * lines * width,
    )
    scores = column_sum(pieces, triples, 1.0 / QUERY_HEADS, remote=1)
    return (context, scores.reshape(rows), triples)


def solution(mesh):
    in_specs = (
        P(("grp", "seq"), "ten"),
        P(("grp", "seq"), "ten"),
        P(("grp", "seq"), "ten"),
        P(("grp", "seq"), None),
        P(),
        P(("grp", "seq")),
        P("grp"),
        P("seq", "ten"),
        P("ten"),
    )
    out_specs = (P(("grp", "seq"), "ten"), P(("grp", "seq")), P(("grp", "seq"), "ten"))
    return jax.shard_map(shards, mesh=mesh, in_specs=in_specs, out_specs=out_specs, check_vma=False)
```

```python
import functools
import math

import jax
import jax.numpy as jnp
from jax import lax
from jax.experimental import pallas as pl
from jax.experimental.pallas import tpu as pltpu
from jax.sharding import PartitionSpec as P

HEAD_SIZE = 128
QUERY_HEADS = 32
VMEM = pl.BlockSpec(memory_space=pltpu.VMEM)
ANY = pl.BlockSpec(memory_space=pl.ANY)
MIB = 1024 * 1024


def call(body, name, inputs, outputs, flops, limit=16, in_specs=None, scratch=(), remote=0):
    inputs = [pltpu.with_memory_space_constraint(x, pltpu.HBM) if i < remote else x for i, x in enumerate(inputs)]
    size = sum(math.prod(x.shape) * x.dtype.itemsize for x in list(inputs) + list(outputs))
    return pl.pallas_call(
        body,
        out_shape=list(outputs),
        in_specs=in_specs or [VMEM] * len(inputs),
        out_specs=[VMEM] * len(outputs),
        scratch_shapes=list(scratch),
        compiler_params=pltpu.CompilerParams(vmem_limit_bytes=limit * MIB),
        cost_estimate=pl.CostEstimate(flops=flops, bytes_accessed=size, transcendentals=0),
        name=name,
    )(*inputs)


def norm_select_kernel(n, hidden_in, gain_in, kept_in, keys_in, values_in, *refs):
    outs, (hidden, gain, kept, pair, sems) = refs[:n], refs[n:]
    rows, width = hidden.shape
    block = width // n
    half = block // 2
    pieces = 4
    piece = width // pieces
    key_width = keys_in.shape[1]
    loads = [
        pltpu.make_async_copy(
            hidden_in.at[:, i * piece : (i + 1) * piece], hidden.at[:, i * piece : (i + 1) * piece], sems.at[i]
        )
        for i in range(pieces)
    ]
    loads += [
        pltpu.make_async_copy(gain_in, gain, sems.at[pieces]),
        pltpu.make_async_copy(kept_in, kept, sems.at[pieces + 1]),
        pltpu.make_async_copy(keys_in, pair.at[:, :key_width], sems.at[pieces + 2]),
        pltpu.make_async_copy(values_in, pair.at[:, key_width:], sems.at[pieces + 3]),
    ]
    for load in loads:
        load.start()
    s, t = lax.axis_index("seq"), lax.axis_index("ten")
    step = min(piece, 1024)
    total = jnp.zeros((rows, step), jnp.float32)
    for i in range(pieces):
        loads[i].wait()
        for j in range(i * piece, (i + 1) * piece, step):
            part = hidden[:, j : j + step].astype(jnp.float32)
            total += part * part
    scale = lax.rsqrt(jnp.sum(total, axis=1, keepdims=True) / width + 1e-06)
    for load in loads[pieces:]:
        load.wait()
    selector = (kept[...] == lax.broadcasted_iota(jnp.int32, (rows, rows), 0)).astype(jnp.bfloat16)
    for k in range(n):
        start = pl.multiple_of(lax.bitwise_xor(s, k) * block + t * half, half)
        columns = pl.ds(start, half)
        normed = (hidden[:, columns].astype(jnp.float32) * scale * gain[:, columns]).astype(jnp.bfloat16)
        if outs[k].shape[1] > half:
            outs[k][:, half:] = pair[...]
        outs[k][:, :half] = lax.dot_general(
            selector, normed, (((0,), (0,)), ((), ())), preferred_element_type=jnp.float32
        ).astype(jnp.bfloat16)


def gather_kernel(near, far, after, out):
    rows = near.shape[0] + far.shape[0] - out.shape[0]
    out[: near.shape[0] - rows] = near[rows:]
    out[near.shape[0] - rows :] = far[...]


def relay_kernel(count, *refs):
    blocks, outs = refs[:count], refs[len(refs) - count :]
    for block, out in zip(blocks, outs):
        out[...] = block[...]


def stage_kernel(n, counts_in, matrix_in, queries_in, *refs):
    matrix, queries, target, counts, sems = refs[-5:]
    loads = [
        pltpu.make_async_copy(counts_in, counts, sems.at[0]),
        pltpu.make_async_copy(matrix_in, matrix, sems.at[1]),
        pltpu.make_async_copy(queries_in, queries, sems.at[2]),
    ]
    for load in loads:
        load.start()
    rows = target.shape[1] // n
    s = lax.axis_index("seq")
    loads[0].wait()
    slot_all = lax.broadcasted_iota(jnp.int32, (1, n * rows), 1)
    found = jnp.full((1, n * rows), -1, jnp.int32)
    for k in range(n):
        source = lax.bitwise_xor(s, k)
        begin = jnp.int32(0)
        for i in range(n):
            begin += jnp.where(i < source, counts[i], 0)
        slot = slot_all - k * rows
        inside = (slot >= 0) & (slot < counts[source])
        found = jnp.where(inside, begin + slot, found)
    target[...] = found
    for load in loads[1:]:
        load.wait()


def compact_kernel(n, target, *refs):
    blocks, (out, even) = refs[:n], refs[n:]
    rows, half = blocks[0].shape[0], out.shape[1]
    for i in range(n // 4):
        even[i * rows : (i + 1) * rows] = blocks[2 * i][:, half:]
    lines = out.shape[0] // n
    s = lax.axis_index("seq")
    received = jnp.concatenate([b[:, :half] for b in blocks], axis=0)
    line = lax.broadcasted_iota(jnp.int32, (lines, received.shape[0]), 0)
    pick = jnp.concatenate(
        [(line + lax.bitwise_xor(s, k) * lines == target[...]).astype(jnp.float32) for k in range(n)], axis=0
    ).astype(jnp.bfloat16)
    out[...] = jnp.dot(pick, received, preferred_element_type=jnp.float32).astype(jnp.bfloat16)


def halving_order(n, masks):
    return sorted(range(n), key=lambda k: [k & mask for mask in masks])


def project_kernel(first, order, own, other, matrix, near, far):
    survivors, half = own.shape
    lines = survivors // len(order)
    width = near.shape[1]
    t = lax.axis_index("ten")
    mine = pl.ds(pl.multiple_of(t * half, half), half)
    others = pl.ds(pl.multiple_of((1 - t) * half, half), half)
    tile = width // 2 if width % 256 == 0 else width
    for j in range(0, width, tile):
        lanes = slice(first + j, first + j + tile)
        part = jnp.dot(own[...], matrix[mine, lanes], preferred_element_type=jnp.float32)
        part += jnp.dot(other[...], matrix[others, lanes], preferred_element_type=jnp.float32)
        for i, k in enumerate(order):
            block = part[k * lines : (k + 1) * lines]
            if i < len(order) // 2:
                near[i * lines : (i + 1) * lines, j : j + tile] = block
            else:
                i -= len(order) // 2
                far[i * lines : (i + 1) * lines, j : j + tile] = block.astype(jnp.bfloat16)


def hop_sum_kernel(kept, received, after, keep, sent):
    rows = keep.shape[0]
    total = kept[...] + received[...].astype(jnp.float32)
    keep[...] = total[:rows]
    sent[...] = total[rows:].astype(jnp.bfloat16)


def hop_sum_both_kernel(*refs):
    *parts, keep, sent = refs
    count = len(parts) // 2
    rows = keep.shape[0]
    width = keep.shape[1] // count
    for c in range(count):
        lanes = slice(c * width, (c + 1) * width)
        total = parts[c][...] + parts[count + c][...].astype(jnp.float32)
        keep[:, lanes] = total[:rows]
        sent[:, lanes] = total[rows:].astype(jnp.bfloat16)


def column_sum_kernel(scale, after, *refs):
    *parts, out = refs
    total = parts[0][...]
    for part in parts[1:]:
        total += part[...]
    out[...] = total * scale


def attention_kernel(n, kv_heads, masks, queries, pair, near, far, odd, context, columns):
    rows = queries.shape[0]
    group = queries.shape[1] // (HEAD_SIZE * kv_heads)
    s = lax.axis_index("seq")
    keys_total = n * rows
    column = lax.broadcasted_iota(jnp.int32, (1, keys_total), 1)
    position = column
    order = list(range(0, n, 2)) + list(range(1, n, 2))
    first = pair.shape[1] - 2 * kv_heads * HEAD_SIZE
    for at, k in enumerate(order):
        inside = (column >= at * rows) & (column < (at + 1) * rows)
        position = jnp.where(inside, column + (lax.bitwise_xor(s, k) - s - at) * rows, position)
    row = lax.rem(lax.broadcasted_iota(jnp.int32, (group * rows, keys_total), 0), rows)
    allowed = position <= row
    sums = jnp.zeros((1, keys_total), jnp.float32)
    for g in range(kv_heads):
        key_lanes = slice(g * HEAD_SIZE, (g + 1) * HEAD_SIZE)
        value_lanes = slice((kv_heads + g) * HEAD_SIZE, (kv_heads + g + 1) * HEAD_SIZE)
        key, value = [
            jnp.concatenate([near[:, x], far[:, x], pair[:, first + x.start : first + x.stop], odd[:, x]], axis=0)
            for x in (key_lanes, value_lanes)
        ]
        heads = range(g * group, (g + 1) * group)
        stacked = jnp.concatenate([queries[:, h * HEAD_SIZE : (h + 1) * HEAD_SIZE] for h in heads], axis=0)
        scores = lax.dot_general(
            stacked, key, (((1,), (1,)), ((), ())), preferred_element_type=jnp.float32
        ) * HEAD_SIZE ** (-0.5)
        scores = jnp.where(allowed, scores, -1e30)
        weights = jnp.exp(scores - jnp.max(scores, axis=1, keepdims=True))
        inverse = 1.0 / jnp.sum(weights, axis=1, keepdims=True)
        mixed = jnp.dot(weights.astype(jnp.bfloat16), value, preferred_element_type=jnp.float32) * inverse
        for i, h in enumerate(heads):
            context[:, h * HEAD_SIZE : (h + 1) * HEAD_SIZE] = mixed[i * rows : (i + 1) * rows]
        sums += jnp.sum(weights * inverse, axis=0, keepdims=True)
    for i, k in enumerate(halving_order(n, masks)):
        at = order.index(k)
        columns[i : i + 1, :] = sums[:, at * rows : (at + 1) * rows]


def finish_kernel(bias, kept, received, out):
    out[...] = kept[...] + received[...].astype(jnp.float32) + bias[...]


def shards(queries, keys, values, hidden, norm_gain, retained_lists, counts, affine_matrix, affine_offset_vector):
    n = lax.axis_size("seq")
    rows, model = hidden.shape
    kv_heads = keys.shape[1] // HEAD_SIZE
    half = affine_matrix.shape[0] // 2
    width = affine_matrix.shape[1]
    survivors = n * rows // 2
    lines = survivors // n
    chunk = width // 2
    near = survivors // 2
    f32, bf16, i32 = jnp.float32, jnp.bfloat16, jnp.int32
    shape = jax.ShapeDtypeStruct
    dma = pltpu.SemaphoreType.DMA

    def trade(x, k):
        return lax.ppermute(x, "seq", [(i, i ^ k) for i in range(n)])

    def trade_across(x, k):
        return lax.ppermute(x, ("seq", "ten"), [(2 * i + t, 2 * (i ^ k) + 1 - t) for i in range(n) for t in range(2)])

    def swap(x):
        return lax.ppermute(x, "ten", [(0, 1), (1, 0)])

    chosen = call(
        functools.partial(norm_select_kernel, n),
        "norm_select",
        (hidden, norm_gain.reshape(1, model), retained_lists.reshape(1, rows), keys, values),
        [shape((rows, half + (2 * keys.shape[1] if k == 1 or k in range(0, n // 2, 2) else 0)), bf16) for k in range(n)],
        4 * rows * model,
        limit=16,
        in_specs=[ANY] * 5,
        remote=5,
        scratch=[pltpu.VMEM((rows, model), bf16), pltpu.VMEM((1, model), f32), pltpu.VMEM((1, rows), i32), pltpu.VMEM((rows, 2 * keys.shape[1]), bf16), dma((8,))],
    )
    last = range(n - n // 4, n)
    received = [chosen[0]] + [trade(chosen[k], k) for k in range(1, last[0])]
    relayed = call(
        functools.partial(relay_kernel, len(last)),
        "relay",
        (*[chosen[k] for k in last], received[1], received[3]),
        [shape((rows, half), bf16)] * len(last),
        0,
        in_specs=[VMEM] * len(last) + [ANY] * 2,
    )
    received += [trade(x, k) for k, x in zip(last, relayed)]
    matrix, queries, target = call(
        functools.partial(stage_kernel, n),
        "stage",
        (counts, affine_matrix, queries, *received[n // 2 : last[0]]),
        [shape(affine_matrix.shape, bf16), shape(queries.shape, bf16), shape((1, n * rows), i32)],
        1500 * affine_matrix.size,
        in_specs=[ANY] * (3 + n // 4),
        remote=3,
        scratch=[pltpu.SMEM(counts.shape, i32), dma((3,))],
    )
    own, even = call(
        functools.partial(compact_kernel, n),
        "compact",
        (target, *received),
        [shape((survivors, half), bf16), shape((n // 4 * rows, 2 * keys.shape[1]), bf16)],
        2 * survivors * n * rows * half,
    )
    other = swap(own)
    rest = [1 << i for i in range(2, n.bit_length() - 1)]
    masks = [[1, 2] + rest, [2, 1] + rest]
    products = [
        call(
            functools.partial(project_kernel, c * chunk, halving_order(n, masks[c])),
            "project",
            (own, other, matrix),
            [shape((near, chunk), f32), shape((near, chunk), bf16)],
            4 * survivors * half * chunk,
        )
        for c in range(2)
    ]
    far = trade(even, n // 2)
    (gathered,) = call(
        gather_kernel,
        "gather",
        (even, far, products[0][1]),
        [shape((n // 2 * rows - rows, even.shape[1]), bf16)],
        1500 * affine_matrix.size,
        in_specs=[VMEM] * 2 + [ANY],
    )
    context, columns = call(
        functools.partial(attention_kernel, n, kv_heads, masks[0]),
        "attention",
        (queries, received[1], even, far, trade(gathered, 1)),
        [shape(queries.shape, f32), shape((n, rows), f32)],
        4 * rows * n * rows * queries.shape[1],
        limit=32,
    )
    kept = [product[0] for product in products]
    arrived = [trade(product[1], masks[c][0]) for c, product in enumerate(products)]
    lines_left = near // 2
    for c in (1, 0):
        keep, sent = call(
            hop_sum_kernel,
            "hop_sum",
            (kept[c], arrived[c], products[c][1] if c else columns),
            [shape((lines_left, chunk), f32), shape((lines_left, chunk), bf16)],
            near * chunk,
            in_specs=[VMEM] * 2 + [ANY],
        )
        kept[c], arrived[c] = keep, trade(sent, masks[c][1])

    def column_sum(pieces, after, scale=1.0, remote=0):
        (total,) = call(
            functools.partial(column_sum_kernel, scale),
            "column_sum",
            (after, *pieces),
            [shape(pieces[0].shape, f32)],
            0,
            in_specs=[ANY] + [VMEM] * len(pieces),
            remote=remote,
        )
        return total

    pieces = [columns[i * (n // 4) : (i + 1) * (n // 4)] for i in range(4)]
    pieces = pieces[:1] + [trade(x, mask) for x, mask in zip(pieces[1:], (2, 1, 3))]
    for mask in rest:
        lines_left //= 2
        keep, sent = call(
            hop_sum_both_kernel,
            "hop_sum_both",
            (*kept, *arrived),
            [shape((lines_left, width), f32), shape((lines_left, width), bf16)],
            lines_left * width,
        )
        kept, arrived = [keep], [trade(sent, mask)]
        columns = column_sum(pieces, keep)
        left = columns.shape[0] // 2
        own, far = columns[:left], columns[left:]
        pieces = [own, trade(far, mask)]
        if mask == rest[-1]:
            pieces += [swap(own), trade_across(far, mask)]

    (triples,) = call(
        finish_kernel,
        "finish",
        (affine_offset_vector.reshape(1, width), kept[0], arrived[0]),
        [shape((lines, width), f32)],
        n * lines * width,
    )
    scores = column_sum(pieces, triples, 1.0 / QUERY_HEADS, remote=1)
    return (context, scores.reshape(rows), triples)


def solution(mesh):
    in_specs = (
        P(("grp", "seq"), "ten"),
        P(("grp", "seq"), "ten"),
        P(("grp", "seq"), "ten"),
        P(("grp", "seq"), None),
        P(),
        P(("grp", "seq")),
        P("grp"),
        P("seq", "ten"),
        P("ten"),
    )
    out_specs = (P(("grp", "seq"), "ten"), P(("grp", "seq")), P(("grp", "seq"), "ten"))
    return jax.shard_map(shards, mesh=mesh, in_specs=in_specs, out_specs=out_specs, check_vma=False)
```

```python
import functools
import math

import jax
import jax.numpy as jnp
from jax import lax
from jax.experimental import pallas as pl
from jax.experimental.pallas import tpu as pltpu
from jax.sharding import PartitionSpec as P

HEAD_SIZE = 128
QUERY_HEADS = 32
VMEM = pl.BlockSpec(memory_space=pltpu.VMEM)
ANY = pl.BlockSpec(memory_space=pl.ANY)
MIB = 1024 * 1024


def call(body, name, inputs, outputs, flops, limit=16, in_specs=None, scratch=(), remote=0):
    inputs = [pltpu.with_memory_space_constraint(x, pltpu.HBM) if i < remote else x for i, x in enumerate(inputs)]
    size = sum(math.prod(x.shape) * x.dtype.itemsize for x in list(inputs) + list(outputs))
    return pl.pallas_call(
        body,
        out_shape=list(outputs),
        in_specs=in_specs or [VMEM] * len(inputs),
        out_specs=[VMEM] * len(outputs),
        scratch_shapes=list(scratch),
        compiler_params=pltpu.CompilerParams(vmem_limit_bytes=limit * MIB),
        cost_estimate=pl.CostEstimate(flops=flops, bytes_accessed=size, transcendentals=0),
        name=name,
    )(*inputs)


def norm_select_kernel(n, hidden_in, gain_in, kept_in, keys_in, values_in, *refs):
    outs, (hidden, gain, kept, pair, sems) = refs[:n], refs[n:]
    rows, width = hidden.shape
    block = width // n
    half = block // 2
    pieces = 4
    piece = width // pieces
    key_width = keys_in.shape[1]
    loads = [
        pltpu.make_async_copy(
            hidden_in.at[:, i * piece : (i + 1) * piece], hidden.at[:, i * piece : (i + 1) * piece], sems.at[i]
        )
        for i in range(pieces)
    ]
    loads += [
        pltpu.make_async_copy(gain_in, gain, sems.at[pieces]),
        pltpu.make_async_copy(kept_in, kept, sems.at[pieces + 1]),
        pltpu.make_async_copy(keys_in, pair.at[:, :key_width], sems.at[pieces + 2]),
        pltpu.make_async_copy(values_in, pair.at[:, key_width:], sems.at[pieces + 3]),
    ]
    for load in loads:
        load.start()
    s, t = lax.axis_index("seq"), lax.axis_index("ten")
    step = min(piece, 1024)
    total = jnp.zeros((rows, step), jnp.float32)
    for i in range(pieces):
        loads[i].wait()
        for j in range(i * piece, (i + 1) * piece, step):
            part = hidden[:, j : j + step].astype(jnp.float32)
            total += part * part
    scale = lax.rsqrt(jnp.sum(total, axis=1, keepdims=True) / width + 1e-06)
    for load in loads[pieces:]:
        load.wait()
    selector = (kept[...] == lax.broadcasted_iota(jnp.int32, (rows, rows), 0)).astype(jnp.bfloat16)
    for k in range(n):
        start = pl.multiple_of(lax.bitwise_xor(s, k) * block + t * half, half)
        columns = pl.ds(start, half)
        normed = (hidden[:, columns].astype(jnp.float32) * scale * gain[:, columns]).astype(jnp.bfloat16)
        if outs[k].shape[1] > half:
            outs[k][:, half:] = pair[...]
        outs[k][:, :half] = lax.dot_general(
            selector, normed, (((0,), (0,)), ((), ())), preferred_element_type=jnp.float32
        ).astype(jnp.bfloat16)


def pass_kernel(block, after, out):
    out[...] = block[...]


def relay_kernel(count, *refs):
    blocks, outs = refs[:count], refs[len(refs) - count :]
    for block, out in zip(blocks, outs):
        out[...] = block[...]


def stage_kernel(n, counts_in, matrix_in, queries_in, *refs):
    matrix, queries, target, counts, sems = refs[-5:]
    loads = [
        pltpu.make_async_copy(counts_in, counts, sems.at[0]),
        pltpu.make_async_copy(matrix_in, matrix, sems.at[1]),
        pltpu.make_async_copy(queries_in, queries, sems.at[2]),
    ]
    for load in loads:
        load.start()
    rows = target.shape[1] // n
    s = lax.axis_index("seq")
    loads[0].wait()
    slot_all = lax.broadcasted_iota(jnp.int32, (1, n * rows), 1)
    found = jnp.full((1, n * rows), -1, jnp.int32)
    for k in range(n):
        source = lax.bitwise_xor(s, k)
        begin = jnp.int32(0)
        for i in range(n):
            begin += jnp.where(i < source, counts[i], 0)
        slot = slot_all - k * rows
        inside = (slot >= 0) & (slot < counts[source])
        found = jnp.where(inside, begin + slot, found)
    target[...] = found
    for load in loads[1:]:
        load.wait()


def compact_kernel(n, target, *refs):
    blocks, (out, even, odd) = refs[:n], refs[n:]
    rows, half = blocks[0].shape[0], out.shape[1]
    for i in range(n // 4):
        even[i * rows : (i + 1) * rows] = blocks[2 * i][:, half:]
        odd[i * rows : (i + 1) * rows] = blocks[2 * i + 1][:, half:]
    lines = out.shape[0] // n
    s = lax.axis_index("seq")
    received = jnp.concatenate([b[:, :half] for b in blocks], axis=0)
    line = lax.broadcasted_iota(jnp.int32, (lines, received.shape[0]), 0)
    pick = jnp.concatenate(
        [(line + lax.bitwise_xor(s, k) * lines == target[...]).astype(jnp.float32) for k in range(n)], axis=0
    ).astype(jnp.bfloat16)
    out[...] = jnp.dot(pick, received, preferred_element_type=jnp.float32).astype(jnp.bfloat16)


def halving_order(n, masks):
    return sorted(range(n), key=lambda k: [k & mask for mask in masks])


def project_own_kernel(own, matrix, out):
    half = own.shape[1]
    mine = pl.ds(pl.multiple_of(lax.axis_index("ten") * half, half), half)
    tile = out.shape[1] // 4 if out.shape[1] % 512 == 0 else out.shape[1]
    for j in range(0, out.shape[1], tile):
        out[:, j : j + tile] = jnp.dot(own[...], matrix[mine, j : j + tile], preferred_element_type=jnp.float32)


def project_kernel(first, order, product, other, matrix, near, far):
    survivors, half = other.shape
    lines = survivors // len(order)
    width = near.shape[1]
    t = lax.axis_index("ten")
    others = pl.ds(pl.multiple_of((1 - t) * half, half), half)
    tile = width // 2 if width % 256 == 0 else width
    for j in range(0, width, tile):
        lanes = slice(first + j, first + j + tile)
        part = product[:, lanes]
        part += jnp.dot(other[...], matrix[others, lanes], preferred_element_type=jnp.float32)
        for i, k in enumerate(order):
            block = part[k * lines : (k + 1) * lines]
            if i < len(order) // 2:
                near[i * lines : (i + 1) * lines, j : j + tile] = block
            else:
                i -= len(order) // 2
                far[i * lines : (i + 1) * lines, j : j + tile] = block.astype(jnp.bfloat16)


def hop_sum_kernel(kept, received, after, keep, sent):
    rows = keep.shape[0]
    total = kept[...] + received[...].astype(jnp.float32)
    keep[...] = total[:rows]
    sent[...] = total[rows:].astype(jnp.bfloat16)


def hop_sum_both_kernel(*refs):
    *parts, keep, sent = refs
    count = len(parts) // 2
    rows = keep.shape[0]
    width = keep.shape[1] // count
    for c in range(count):
        lanes = slice(c * width, (c + 1) * width)
        total = parts[c][...] + parts[count + c][...].astype(jnp.float32)
        keep[:, lanes] = total[:rows]
        sent[:, lanes] = total[rows:].astype(jnp.bfloat16)


def column_sum_kernel(scale, after, *refs):
    *parts, out = refs
    total = parts[0][...]
    for part in parts[1:]:
        total += part[...]
    out[...] = total * scale


def attention_kernel(n, kv_heads, masks, queries, even_near, even_far, odd_near, odd_far, context, columns):
    rows = queries.shape[0]
    group = queries.shape[1] // (HEAD_SIZE * kv_heads)
    s = lax.axis_index("seq")
    keys_total = n * rows
    column = lax.broadcasted_iota(jnp.int32, (1, keys_total), 1)
    position = column
    order = list(range(0, n, 2)) + list(range(1, n, 2))
    for at, k in enumerate(order):
        inside = (column >= at * rows) & (column < (at + 1) * rows)
        position = jnp.where(inside, column + (lax.bitwise_xor(s, k) - s - at) * rows, position)
    row = lax.rem(lax.broadcasted_iota(jnp.int32, (group * rows, keys_total), 0), rows)
    allowed = position <= row
    sums = jnp.zeros((1, keys_total), jnp.float32)
    for g in range(kv_heads):
        key_lanes = slice(g * HEAD_SIZE, (g + 1) * HEAD_SIZE)
        value_lanes = slice((kv_heads + g) * HEAD_SIZE, (kv_heads + g + 1) * HEAD_SIZE)
        key, value = [
            jnp.concatenate([block[:, x] for block in (even_near, even_far, odd_near, odd_far)], axis=0)
            for x in (key_lanes, value_lanes)
        ]
        heads = range(g * group, (g + 1) * group)
        stacked = jnp.concatenate([queries[:, h * HEAD_SIZE : (h + 1) * HEAD_SIZE] for h in heads], axis=0)
        scores = lax.dot_general(
            stacked, key, (((1,), (1,)), ((), ())), preferred_element_type=jnp.float32
        ) * HEAD_SIZE ** (-0.5)
        scores = jnp.where(allowed, scores, -1e30)
        weights = jnp.exp(scores - jnp.max(scores, axis=1, keepdims=True))
        inverse = 1.0 / jnp.sum(weights, axis=1, keepdims=True)
        mixed = jnp.dot(weights.astype(jnp.bfloat16), value, preferred_element_type=jnp.float32) * inverse
        for i, h in enumerate(heads):
            context[:, h * HEAD_SIZE : (h + 1) * HEAD_SIZE] = mixed[i * rows : (i + 1) * rows]
        sums += jnp.sum(weights * inverse, axis=0, keepdims=True)
    for i, k in enumerate(halving_order(n, masks)):
        at = order.index(k)
        columns[i : i + 1, :] = sums[:, at * rows : (at + 1) * rows]


def finish_kernel(bias, kept, received, out):
    out[...] = kept[...] + received[...].astype(jnp.float32) + bias[...]


def shards(queries, keys, values, hidden, norm_gain, retained_lists, counts, affine_matrix, affine_offset_vector):
    n = lax.axis_size("seq")
    rows, model = hidden.shape
    kv_heads = keys.shape[1] // HEAD_SIZE
    half = affine_matrix.shape[0] // 2
    width = affine_matrix.shape[1]
    survivors = n * rows // 2
    lines = survivors // n
    chunk = width // 2
    near = survivors // 2
    f32, bf16, i32 = jnp.float32, jnp.bfloat16, jnp.int32
    shape = jax.ShapeDtypeStruct
    dma = pltpu.SemaphoreType.DMA

    def trade(x, k):
        return lax.ppermute(x, "seq", [(i, i ^ k) for i in range(n)])

    def trade_across(x, k):
        return lax.ppermute(x, ("seq", "ten"), [(2 * i + t, 2 * (i ^ k) + 1 - t) for i in range(n) for t in range(2)])

    def swap(x):
        return lax.ppermute(x, "ten", [(0, 1), (1, 0)])

    chosen = call(
        functools.partial(norm_select_kernel, n),
        "norm_select",
        (hidden, norm_gain.reshape(1, model), retained_lists.reshape(1, rows), keys, values),
        [shape((rows, half + (2 * keys.shape[1] if k < n // 2 else 0)), bf16) for k in range(n)],
        4 * rows * model,
        limit=16,
        in_specs=[ANY] * 5,
        remote=5,
        scratch=[pltpu.VMEM((rows, model), bf16), pltpu.VMEM((1, model), f32), pltpu.VMEM((1, rows), i32), pltpu.VMEM((rows, 2 * keys.shape[1]), bf16), dma((8,))],
    )
    last = range(n - n // 4, n)
    received = [chosen[0]] + [trade(chosen[k], k) for k in range(1, last[0])]
    relayed = call(
        functools.partial(relay_kernel, len(last)),
        "relay",
        (*[chosen[k] for k in last], received[1], received[3]),
        [shape((rows, half), bf16)] * len(last),
        0,
        in_specs=[VMEM] * len(last) + [ANY] * 2,
    )
    received += [trade(x, k) for k, x in zip(last, relayed)]
    matrix, queries, target = call(
        functools.partial(stage_kernel, n),
        "stage",
        (counts, affine_matrix, queries, *received[n // 2 : last[0]]),
        [shape(affine_matrix.shape, bf16), shape(queries.shape, bf16), shape((1, n * rows), i32)],
        1500 * affine_matrix.size,
        in_specs=[ANY] * (3 + n // 4),
        remote=3,
        scratch=[pltpu.SMEM(counts.shape, i32), dma((3,))],
    )
    own, even, odd = call(
        functools.partial(compact_kernel, n),
        "compact",
        (target, *received),
        [shape((survivors, half), bf16)] + [shape((n // 4 * rows, 2 * keys.shape[1]), bf16)] * 2,
        2 * survivors * n * rows * half,
    )
    other = swap(own)
    rest = [1 << i for i in range(2, n.bit_length() - 1)]
    masks = [[1, 2] + rest, [2, 1] + rest]
    (product,) = call(
        project_own_kernel,
        "project_own",
        (own, matrix),
        [shape((survivors, width), f32)],
        2 * survivors * half * width,
    )
    products = [
        call(
            functools.partial(project_kernel, c * chunk, halving_order(n, masks[c])),
            "project",
            (product, other, matrix),
            [shape((near, chunk), f32), shape((near, chunk), bf16)],
            2 * survivors * half * chunk,
        )
        for c in range(2)
    ]
    far = trade(even, n // 2)
    (passed,) = call(
        pass_kernel,
        "pass",
        (far, products[1][1]),
        [shape(far.shape, bf16)],
        1500 * affine_matrix.size,
        in_specs=[VMEM, ANY],
    )
    context, columns = call(
        functools.partial(attention_kernel, n, kv_heads, masks[0]),
        "attention",
        (queries, even, far, odd, trade(passed, 1)),
        [shape(queries.shape, f32), shape((n, rows), f32)],
        4 * rows * n * rows * queries.shape[1],
        limit=32,
    )
    kept = [product[0] for product in products]
    arrived = [trade(product[1], masks[c][0]) for c, product in enumerate(products)]
    lines_left = near // 2
    for c in (0, 1):
        keep, sent = call(
            hop_sum_kernel,
            "hop_sum",
            (kept[c], arrived[c], kept[0] if c else columns),
            [shape((lines_left, chunk), f32), shape((lines_left, chunk), bf16)],
            near * chunk,
            in_specs=[VMEM] * 2 + [ANY],
        )
        kept[c], arrived[c] = keep, trade(sent, masks[c][1])

    def column_sum(pieces, after, scale=1.0, remote=0):
        (total,) = call(
            functools.partial(column_sum_kernel, scale),
            "column_sum",
            (after, *pieces),
            [shape(pieces[0].shape, f32)],
            0,
            in_specs=[ANY] + [VMEM] * len(pieces),
            remote=remote,
        )
        return total

    pieces = [columns[i * (n // 4) : (i + 1) * (n // 4)] for i in range(4)]
    pieces = pieces[:1] + [trade(x, mask) for x, mask in zip(pieces[1:], (2, 1, 3))]
    for mask in rest:
        lines_left //= 2
        keep, sent = call(
            hop_sum_both_kernel,
            "hop_sum_both",
            (*kept, *arrived),
            [shape((lines_left, width), f32), shape((lines_left, width), bf16)],
            lines_left * width,
        )
        kept, arrived = [keep], [trade(sent, mask)]
        columns = column_sum(pieces, keep)
        left = columns.shape[0] // 2
        own, far = columns[:left], columns[left:]
        pieces = [own, trade(far, mask)]
        if mask == rest[-1]:
            pieces += [swap(own), trade_across(far, mask)]

    (triples,) = call(
        finish_kernel,
        "finish",
        (affine_offset_vector.reshape(1, width), kept[0], arrived[0]),
        [shape((lines, width), f32)],
        n * lines * width,
    )
    scores = column_sum(pieces, triples, 1.0 / QUERY_HEADS, remote=1)
    return (context, scores.reshape(rows), triples)


def solution(mesh):
    in_specs = (
        P(("grp", "seq"), "ten"),
        P(("grp", "seq"), "ten"),
        P(("grp", "seq"), "ten"),
        P(("grp", "seq"), None),
        P(),
        P(("grp", "seq")),
        P("grp"),
        P("seq", "ten"),
        P("ten"),
    )
    out_specs = (P(("grp", "seq"), "ten"), P(("grp", "seq")), P(("grp", "seq"), "ten"))
    return jax.shard_map(shards, mesh=mesh, in_specs=in_specs, out_specs=out_specs, check_vma=False)
```

```python
import functools
import math

import jax
import jax.numpy as jnp
from jax import lax
from jax.experimental import pallas as pl
from jax.experimental.pallas import tpu as pltpu
from jax.sharding import PartitionSpec as P

HEAD_SIZE = 128
QUERY_HEADS = 32
VMEM = pl.BlockSpec(memory_space=pltpu.VMEM)
ANY = pl.BlockSpec(memory_space=pl.ANY)
MIB = 1024 * 1024


def call(body, name, inputs, outputs, flops, limit=16, in_specs=None, scratch=(), remote=0):
    inputs = [pltpu.with_memory_space_constraint(x, pltpu.HBM) if i < remote else x for i, x in enumerate(inputs)]
    size = sum(math.prod(x.shape) * x.dtype.itemsize for x in list(inputs) + list(outputs))
    return pl.pallas_call(
        body,
        out_shape=list(outputs),
        in_specs=in_specs or [VMEM] * len(inputs),
        out_specs=[VMEM] * len(outputs),
        scratch_shapes=list(scratch),
        compiler_params=pltpu.CompilerParams(vmem_limit_bytes=limit * MIB),
        cost_estimate=pl.CostEstimate(flops=flops, bytes_accessed=size, transcendentals=0),
        name=name,
    )(*inputs)


def norm_select_kernel(n, hidden_in, gain_in, kept_in, keys_in, values_in, *refs):
    outs, (hidden, gain, kept, pair, sems) = refs[:n], refs[n:]
    rows, width = hidden.shape
    block = width // n
    half = block // 2
    pieces = 4
    piece = width // pieces
    key_width = keys_in.shape[1]
    loads = [
        pltpu.make_async_copy(
            hidden_in.at[:, i * piece : (i + 1) * piece], hidden.at[:, i * piece : (i + 1) * piece], sems.at[i]
        )
        for i in range(pieces)
    ]
    loads += [
        pltpu.make_async_copy(gain_in, gain, sems.at[pieces]),
        pltpu.make_async_copy(kept_in, kept, sems.at[pieces + 1]),
        pltpu.make_async_copy(keys_in, pair.at[:, :key_width], sems.at[pieces + 2]),
        pltpu.make_async_copy(values_in, pair.at[:, key_width:], sems.at[pieces + 3]),
    ]
    for load in loads:
        load.start()
    s, t = lax.axis_index("seq"), lax.axis_index("ten")
    step = min(piece, 1024)
    total = jnp.zeros((rows, step), jnp.float32)
    for i in range(pieces):
        loads[i].wait()
        for j in range(i * piece, (i + 1) * piece, step):
            part = hidden[:, j : j + step].astype(jnp.float32)
            total += part * part
    scale = lax.rsqrt(jnp.sum(total, axis=1, keepdims=True) / width + 1e-06)
    for load in loads[pieces:]:
        load.wait()
    selector = (kept[...] == lax.broadcasted_iota(jnp.int32, (rows, rows), 0)).astype(jnp.bfloat16)
    for k in range(n):
        start = pl.multiple_of(lax.bitwise_xor(s, k) * block + t * half, half)
        columns = pl.ds(start, half)
        normed = (hidden[:, columns].astype(jnp.float32) * scale * gain[:, columns]).astype(jnp.bfloat16)
        if outs[k].shape[1] > half:
            outs[k][:, half:] = pair[...]
        outs[k][:, :half] = lax.dot_general(
            selector, normed, (((0,), (0,)), ((), ())), preferred_element_type=jnp.float32
        ).astype(jnp.bfloat16)


def gather_kernel(near, far, after, out):
    rows = near.shape[0] + far.shape[0] - out.shape[0]
    out[: near.shape[0] - rows] = near[rows:]
    out[near.shape[0] - rows :] = far[...]


def relay_kernel(count, *refs):
    blocks, outs = refs[:count], refs[len(refs) - count :]
    for block, out in zip(blocks, outs):
        out[...] = block[...]


def stage_kernel(n, counts_in, matrix_in, queries_in, *refs):
    matrix, queries, target, counts, sems = refs[-5:]
    loads = [
        pltpu.make_async_copy(counts_in, counts, sems.at[0]),
        pltpu.make_async_copy(matrix_in, matrix, sems.at[1]),
        pltpu.make_async_copy(queries_in, queries, sems.at[2]),
    ]
    for load in loads:
        load.start()
    rows = target.shape[1] // n
    s = lax.axis_index("seq")
    loads[0].wait()
    slot_all = lax.broadcasted_iota(jnp.int32, (1, n * rows), 1)
    found = jnp.full((1, n * rows), -1, jnp.int32)
    for k in range(n):
        source = lax.bitwise_xor(s, k)
        begin = jnp.int32(0)
        for i in range(n):
            begin += jnp.where(i < source, counts[i], 0)
        slot = slot_all - k * rows
        inside = (slot >= 0) & (slot < counts[source])
        found = jnp.where(inside, begin + slot, found)
    target[...] = found
    for load in loads[1:]:
        load.wait()


def compact_kernel(n, target, *refs):
    blocks, (out, even, pair) = refs[:n], refs[n:]
    pair[...] = blocks[1][:, out.shape[1] :]
    rows, half = blocks[0].shape[0], out.shape[1]
    for i in range(n // 4):
        even[i * rows : (i + 1) * rows] = blocks[2 * i][:, half:]
    lines = out.shape[0] // n
    s = lax.axis_index("seq")
    received = jnp.concatenate([b[:, :half] for b in blocks], axis=0)
    line = lax.broadcasted_iota(jnp.int32, (lines, received.shape[0]), 0)
    pick = jnp.concatenate(
        [(line + lax.bitwise_xor(s, k) * lines == target[...]).astype(jnp.float32) for k in range(n)], axis=0
    ).astype(jnp.bfloat16)
    out[...] = jnp.dot(pick, received, preferred_element_type=jnp.float32).astype(jnp.bfloat16)


def halving_order(n, masks):
    return sorted(range(n), key=lambda k: [k & mask for mask in masks])


def project_own_kernel(own, matrix, out):
    half = own.shape[1]
    mine = pl.ds(pl.multiple_of(lax.axis_index("ten") * half, half), half)
    tile = out.shape[1] // 4 if out.shape[1] % 512 == 0 else out.shape[1]
    for j in range(0, out.shape[1], tile):
        out[:, j : j + tile] = jnp.dot(own[...], matrix[mine, j : j + tile], preferred_element_type=jnp.float32)


def project_kernel(first, order, product, other, matrix, near, far):
    survivors, half = other.shape
    lines = survivors // len(order)
    width = near.shape[1]
    t = lax.axis_index("ten")
    others = pl.ds(pl.multiple_of((1 - t) * half, half), half)
    tile = width // 2 if width % 256 == 0 else width
    for j in range(0, width, tile):
        lanes = slice(first + j, first + j + tile)
        part = product[:, lanes]
        part += jnp.dot(other[...], matrix[others, lanes], preferred_element_type=jnp.float32)
        for i, k in enumerate(order):
            block = part[k * lines : (k + 1) * lines]
            if i < len(order) // 2:
                near[i * lines : (i + 1) * lines, j : j + tile] = block
            else:
                i -= len(order) // 2
                far[i * lines : (i + 1) * lines, j : j + tile] = block.astype(jnp.bfloat16)


def hop_sum_kernel(kept, received, after, keep, sent):
    rows = keep.shape[0]
    total = kept[...] + received[...].astype(jnp.float32)
    keep[...] = total[:rows]
    sent[...] = total[rows:].astype(jnp.bfloat16)


def hop_sum_both_kernel(*refs):
    *parts, keep, sent = refs
    count = len(parts) // 2
    rows = keep.shape[0]
    width = keep.shape[1] // count
    for c in range(count):
        lanes = slice(c * width, (c + 1) * width)
        total = parts[c][...] + parts[count + c][...].astype(jnp.float32)
        keep[:, lanes] = total[:rows]
        sent[:, lanes] = total[rows:].astype(jnp.bfloat16)


def column_sum_kernel(scale, after, *refs):
    *parts, out = refs
    total = parts[0][...]
    for part in parts[1:]:
        total += part[...]
    out[...] = total * scale


def attention_kernel(n, kv_heads, masks, queries, near, far, pair, odd, after, context, columns):
    rows = queries.shape[0]
    group = queries.shape[1] // (HEAD_SIZE * kv_heads)
    s = lax.axis_index("seq")
    keys_total = n * rows
    column = lax.broadcasted_iota(jnp.int32, (1, keys_total), 1)
    position = column
    order = list(range(0, n, 2)) + list(range(1, n, 2))
    for at, k in enumerate(order):
        inside = (column >= at * rows) & (column < (at + 1) * rows)
        position = jnp.where(inside, column + (lax.bitwise_xor(s, k) - s - at) * rows, position)
    row = lax.rem(lax.broadcasted_iota(jnp.int32, (group * rows, keys_total), 0), rows)
    allowed = position <= row
    sums = jnp.zeros((1, keys_total), jnp.float32)
    for g in range(kv_heads):
        key_lanes = slice(g * HEAD_SIZE, (g + 1) * HEAD_SIZE)
        value_lanes = slice((kv_heads + g) * HEAD_SIZE, (kv_heads + g + 1) * HEAD_SIZE)
        key, value = [
            jnp.concatenate([block[:, x] for block in (near, far, pair, odd)], axis=0)
            for x in (key_lanes, value_lanes)
        ]
        heads = range(g * group, (g + 1) * group)
        stacked = jnp.concatenate([queries[:, h * HEAD_SIZE : (h + 1) * HEAD_SIZE] for h in heads], axis=0)
        scores = lax.dot_general(
            stacked, key, (((1,), (1,)), ((), ())), preferred_element_type=jnp.float32
        ) * HEAD_SIZE ** (-0.5)
        scores = jnp.where(allowed, scores, -1e30)
        weights = jnp.exp(scores - jnp.max(scores, axis=1, keepdims=True))
        inverse = 1.0 / jnp.sum(weights, axis=1, keepdims=True)
        mixed = jnp.dot(weights.astype(jnp.bfloat16), value, preferred_element_type=jnp.float32) * inverse
        for i, h in enumerate(heads):
            context[:, h * HEAD_SIZE : (h + 1) * HEAD_SIZE] = mixed[i * rows : (i + 1) * rows]
        sums += jnp.sum(weights * inverse, axis=0, keepdims=True)
    for i, k in enumerate(halving_order(n, masks)):
        at = order.index(k)
        columns[i : i + 1, :] = sums[:, at * rows : (at + 1) * rows]


def finish_kernel(bias, kept, received, out):
    out[...] = kept[...] + received[...].astype(jnp.float32) + bias[...]


def shards(queries, keys, values, hidden, norm_gain, retained_lists, counts, affine_matrix, affine_offset_vector):
    n = lax.axis_size("seq")
    rows, model = hidden.shape
    kv_heads = keys.shape[1] // HEAD_SIZE
    half = affine_matrix.shape[0] // 2
    width = affine_matrix.shape[1]
    survivors = n * rows // 2
    lines = survivors // n
    chunk = width // 2
    near = survivors // 2
    f32, bf16, i32 = jnp.float32, jnp.bfloat16, jnp.int32
    shape = jax.ShapeDtypeStruct
    dma = pltpu.SemaphoreType.DMA

    def trade(x, k):
        return lax.ppermute(x, "seq", [(i, i ^ k) for i in range(n)])

    def trade_across(x, k):
        return lax.ppermute(x, ("seq", "ten"), [(2 * i + t, 2 * (i ^ k) + 1 - t) for i in range(n) for t in range(2)])

    def swap(x):
        return lax.ppermute(x, "ten", [(0, 1), (1, 0)])

    chosen = call(
        functools.partial(norm_select_kernel, n),
        "norm_select",
        (hidden, norm_gain.reshape(1, model), retained_lists.reshape(1, rows), keys, values),
        [shape((rows, half + (2 * keys.shape[1] if k == 1 or k in range(0, n // 2, 2) else 0)), bf16) for k in range(n)],
        4 * rows * model,
        limit=16,
        in_specs=[ANY] * 5,
        remote=5,
        scratch=[pltpu.VMEM((rows, model), bf16), pltpu.VMEM((1, model), f32), pltpu.VMEM((1, rows), i32), pltpu.VMEM((rows, 2 * keys.shape[1]), bf16), dma((8,))],
    )
    last = range(n - n // 4, n)
    received = [chosen[0]] + [trade(chosen[k], k) for k in range(1, last[0])]
    relayed = call(
        functools.partial(relay_kernel, len(last)),
        "relay",
        (*[chosen[k] for k in last], received[1], received[3]),
        [shape((rows, half), bf16)] * len(last),
        0,
        in_specs=[VMEM] * len(last) + [ANY] * 2,
    )
    received += [trade(x, k) for k, x in zip(last, relayed)]
    matrix, queries, target = call(
        functools.partial(stage_kernel, n),
        "stage",
        (counts, affine_matrix, queries, *received[n // 2 : last[0]]),
        [shape(affine_matrix.shape, bf16), shape(queries.shape, bf16), shape((1, n * rows), i32)],
        1500 * affine_matrix.size,
        in_specs=[ANY] * (3 + n // 4),
        remote=3,
        scratch=[pltpu.SMEM(counts.shape, i32), dma((3,))],
    )
    own, even, pair = call(
        functools.partial(compact_kernel, n),
        "compact",
        (target, *received),
        [shape((survivors, half), bf16)] + [shape((x * rows, 2 * keys.shape[1]), bf16) for x in (n // 4, 1)],
        2 * survivors * n * rows * half,
    )
    other = swap(own)
    rest = [1 << i for i in range(2, n.bit_length() - 1)]
    masks = [[1, 2] + rest, [2, 1] + rest]
    (product,) = call(
        project_own_kernel,
        "project_own",
        (own, matrix),
        [shape((survivors, width), f32)],
        2 * survivors * half * width,
    )
    products = [
        call(
            functools.partial(project_kernel, c * chunk, halving_order(n, masks[c])),
            "project",
            (product, other, matrix),
            [shape((near, chunk), f32), shape((near, chunk), bf16)],
            2 * survivors * half * chunk,
        )
        for c in range(2)
    ]
    far = trade(even, n // 2)
    (gathered,) = call(
        gather_kernel,
        "gather",
        (even, far, products[1][1]),
        [shape((n // 2 * rows - rows, even.shape[1]), bf16)],
        1500 * affine_matrix.size,
        in_specs=[VMEM] * 2 + [ANY],
    )
    odd = trade(gathered, 1)
    kept = [product[0] for product in products]
    arrived = [trade(product[1], masks[c][0]) for c, product in enumerate(products)]
    lines_left = near // 2
    for c in (0, 1):
        keep, sent = call(
            hop_sum_kernel,
            "hop_sum",
            (kept[c], arrived[c], kept[0] if c else products[1][1]),
            [shape((lines_left, chunk), f32), shape((lines_left, chunk), bf16)],
            near * chunk,
            in_specs=[VMEM] * 2 + [ANY],
        )
        kept[c], arrived[c] = keep, trade(sent, masks[c][1])

    context, columns = call(
        functools.partial(attention_kernel, n, kv_heads, masks[0]),
        "attention",
        (queries, even, far, pair, odd, kept[0]),
        [shape(queries.shape, f32), shape((n, rows), f32)],
        4 * rows * n * rows * queries.shape[1],
        limit=32,
        in_specs=[VMEM] * 5 + [ANY],
    )

    def column_sum(pieces, after, scale=1.0, remote=0):
        (total,) = call(
            functools.partial(column_sum_kernel, scale),
            "column_sum",
            (after, *pieces),
            [shape(pieces[0].shape, f32)],
            0,
            in_specs=[ANY] + [VMEM] * len(pieces),
            remote=remote,
        )
        return total

    pieces = [columns[i * (n // 4) : (i + 1) * (n // 4)] for i in range(4)]
    pieces = pieces[:1] + [trade(x, mask) for x, mask in zip(pieces[1:], (2, 1, 3))]
    for mask in rest:
        lines_left //= 2
        keep, sent = call(
            hop_sum_both_kernel,
            "hop_sum_both",
            (*kept, *arrived),
            [shape((lines_left, width), f32), shape((lines_left, width), bf16)],
            lines_left * width,
        )
        kept, arrived = [keep], [trade(sent, mask)]
        columns = column_sum(pieces, keep)
        left = columns.shape[0] // 2
        own, far = columns[:left], columns[left:]
        pieces = [own, trade(far, mask)]
        if mask == rest[-1]:
            pieces += [swap(own), trade_across(far, mask)]

    (triples,) = call(
        finish_kernel,
        "finish",
        (affine_offset_vector.reshape(1, width), kept[0], arrived[0]),
        [shape((lines, width), f32)],
        n * lines * width,
    )
    scores = column_sum(pieces, triples, 1.0 / QUERY_HEADS, remote=1)
    return (context, scores.reshape(rows), triples)


def solution(mesh):
    in_specs = (
        P(("grp", "seq"), "ten"),
        P(("grp", "seq"), "ten"),
        P(("grp", "seq"), "ten"),
        P(("grp", "seq"), None),
        P(),
        P(("grp", "seq")),
        P("grp"),
        P("seq", "ten"),
        P("ten"),
    )
    out_specs = (P(("grp", "seq"), "ten"), P(("grp", "seq")), P(("grp", "seq"), "ten"))
    return jax.shard_map(shards, mesh=mesh, in_specs=in_specs, out_specs=out_specs, check_vma=False)
```

```python
import functools
import math

import jax
import jax.numpy as jnp
from jax import lax
from jax.experimental import pallas as pl
from jax.experimental.pallas import tpu as pltpu
from jax.sharding import PartitionSpec as P

HEAD_SIZE = 128
QUERY_HEADS = 32
VMEM = pl.BlockSpec(memory_space=pltpu.VMEM)
ANY = pl.BlockSpec(memory_space=pl.ANY)
MIB = 1024 * 1024


def call(body, name, inputs, outputs, flops, limit=16, in_specs=None, scratch=(), remote=0):
    inputs = [pltpu.with_memory_space_constraint(x, pltpu.HBM) if i < remote else x for i, x in enumerate(inputs)]
    size = sum(math.prod(x.shape) * x.dtype.itemsize for x in list(inputs) + list(outputs))
    return pl.pallas_call(
        body,
        out_shape=list(outputs),
        in_specs=in_specs or [VMEM] * len(inputs),
        out_specs=[VMEM] * len(outputs),
        scratch_shapes=list(scratch),
        compiler_params=pltpu.CompilerParams(vmem_limit_bytes=limit * MIB),
        cost_estimate=pl.CostEstimate(flops=flops, bytes_accessed=size, transcendentals=0),
        name=name,
    )(*inputs)


def norm_select_kernel(n, hidden_in, gain_in, kept_in, keys_in, values_in, *refs):
    outs, (hidden, gain, kept, pair, sems) = refs[:n], refs[n:]
    rows, width = hidden.shape
    block = width // n
    half = block // 2
    pieces = 4
    piece = width // pieces
    key_width = keys_in.shape[1]
    loads = [
        pltpu.make_async_copy(
            hidden_in.at[:, i * piece : (i + 1) * piece], hidden.at[:, i * piece : (i + 1) * piece], sems.at[i]
        )
        for i in range(pieces)
    ]
    loads += [
        pltpu.make_async_copy(gain_in, gain, sems.at[pieces]),
        pltpu.make_async_copy(kept_in, kept, sems.at[pieces + 1]),
        pltpu.make_async_copy(keys_in, pair.at[:, :key_width], sems.at[pieces + 2]),
        pltpu.make_async_copy(values_in, pair.at[:, key_width:], sems.at[pieces + 3]),
    ]
    for load in loads:
        load.start()
    s, t = lax.axis_index("seq"), lax.axis_index("ten")
    step = min(piece, 1024)
    total = jnp.zeros((rows, step), jnp.float32)
    for i in range(pieces):
        loads[i].wait()
        for j in range(i * piece, (i + 1) * piece, step):
            part = hidden[:, j : j + step].astype(jnp.float32)
            total += part * part
    scale = lax.rsqrt(jnp.sum(total, axis=1, keepdims=True) / width + 1e-06)
    for load in loads[pieces:]:
        load.wait()
    selector = (kept[...] == lax.broadcasted_iota(jnp.int32, (rows, rows), 0)).astype(jnp.bfloat16)
    for k in range(n):
        start = pl.multiple_of(lax.bitwise_xor(s, k) * block + t * half, half)
        columns = pl.ds(start, half)
        normed = (hidden[:, columns].astype(jnp.float32) * scale * gain[:, columns]).astype(jnp.bfloat16)
        if outs[k].shape[1] > half:
            outs[k][:, half:] = pair[...]
        outs[k][:, :half] = lax.dot_general(
            selector, normed, (((0,), (0,)), ((), ())), preferred_element_type=jnp.float32
        ).astype(jnp.bfloat16)


def gather_kernel(near, far, after, out):
    rows = near.shape[0] + far.shape[0] - out.shape[0]
    out[: near.shape[0] - rows] = near[rows:]
    out[near.shape[0] - rows :] = far[...]


def relay_kernel(count, *refs):
    blocks, outs = refs[:count], refs[len(refs) - count :]
    for block, out in zip(blocks, outs):
        out[...] = block[...]


def stage_kernel(n, counts_in, matrix_in, queries_in, *refs):
    matrix, queries, target, counts, sems = refs[-5:]
    loads = [
        pltpu.make_async_copy(counts_in, counts, sems.at[0]),
        pltpu.make_async_copy(matrix_in, matrix, sems.at[1]),
        pltpu.make_async_copy(queries_in, queries, sems.at[2]),
    ]
    for load in loads:
        load.start()
    rows = target.shape[1] // n
    s = lax.axis_index("seq")
    loads[0].wait()
    slot_all = lax.broadcasted_iota(jnp.int32, (1, n * rows), 1)
    found = jnp.full((1, n * rows), -1, jnp.int32)
    for k in range(n):
        source = lax.bitwise_xor(s, k)
        begin = jnp.int32(0)
        for i in range(n):
            begin += jnp.where(i < source, counts[i], 0)
        slot = slot_all - k * rows
        inside = (slot >= 0) & (slot < counts[source])
        found = jnp.where(inside, begin + slot, found)
    target[...] = found
    for load in loads[1:]:
        load.wait()


def compact_kernel(n, target, *refs):
    blocks, (out, even, pair) = refs[:n], refs[n:]
    pair[...] = blocks[1][:, out.shape[1] :]
    rows, half = blocks[0].shape[0], out.shape[1]
    for i in range(n // 4):
        even[i * rows : (i + 1) * rows] = blocks[2 * i][:, half:]
    lines = out.shape[0] // n
    s = lax.axis_index("seq")
    received = jnp.concatenate([b[:, :half] for b in blocks], axis=0)
    line = lax.broadcasted_iota(jnp.int32, (lines, received.shape[0]), 0)
    pick = jnp.concatenate(
        [(line + lax.bitwise_xor(s, k) * lines == target[...]).astype(jnp.float32) for k in range(n)], axis=0
    ).astype(jnp.bfloat16)
    out[...] = jnp.dot(pick, received, preferred_element_type=jnp.float32).astype(jnp.bfloat16)


def halving_order(n, masks):
    return sorted(range(n), key=lambda k: [k & mask for mask in masks])


def project_own_kernel(own, matrix, out):
    half = own.shape[1]
    mine = pl.ds(pl.multiple_of(lax.axis_index("ten") * half, half), half)
    tile = out.shape[1] // 4 if out.shape[1] % 512 == 0 else out.shape[1]
    for j in range(0, out.shape[1], tile):
        out[:, j : j + tile] = jnp.dot(own[...], matrix[mine, j : j + tile], preferred_element_type=jnp.float32)


def project_kernel(first, order, product, other, matrix, near, far):
    survivors, half = other.shape
    lines = survivors // len(order)
    width = near.shape[1]
    t = lax.axis_index("ten")
    others = pl.ds(pl.multiple_of((1 - t) * half, half), half)
    tile = width // 2 if width % 256 == 0 else width
    for j in range(0, width, tile):
        lanes = slice(first + j, first + j + tile)
        part = product[:, lanes]
        part += jnp.dot(other[...], matrix[others, lanes], preferred_element_type=jnp.float32)
        for i, k in enumerate(order):
            block = part[k * lines : (k + 1) * lines]
            if i < len(order) // 2:
                near[i * lines : (i + 1) * lines, j : j + tile] = block
            else:
                i -= len(order) // 2
                far[i * lines : (i + 1) * lines, j : j + tile] = block.astype(jnp.bfloat16)


def hop_sum_kernel(kept, received, after, keep, sent):
    rows = keep.shape[0]
    total = kept[...] + received[...].astype(jnp.float32)
    keep[...] = total[:rows]
    sent[...] = total[rows:].astype(jnp.bfloat16)


def hop_sum_both_kernel(*refs):
    *parts, keep, sent = refs
    count = len(parts) // 2
    rows = keep.shape[0]
    first = 0
    for c in range(count):
        lanes = slice(first, first + parts[c].shape[1])
        first = lanes.stop
        total = parts[c][...] + parts[count + c][...].astype(jnp.float32)
        keep[:, lanes] = total[:rows]
        sent[:, lanes] = total[rows:].astype(jnp.bfloat16)


def column_sum_kernel(scale, after, *refs):
    *parts, out = refs
    total = parts[0][...]
    for part in parts[1:]:
        total += part[...]
    out[...] = total * scale


def attention_kernel(n, kv_heads, masks, queries, near, far, pair, odd, after, context, columns):
    rows = queries.shape[0]
    group = queries.shape[1] // (HEAD_SIZE * kv_heads)
    s = lax.axis_index("seq")
    keys_total = n * rows
    column = lax.broadcasted_iota(jnp.int32, (1, keys_total), 1)
    position = column
    order = list(range(0, n, 2)) + list(range(1, n, 2))
    for at, k in enumerate(order):
        inside = (column >= at * rows) & (column < (at + 1) * rows)
        position = jnp.where(inside, column + (lax.bitwise_xor(s, k) - s - at) * rows, position)
    row = lax.rem(lax.broadcasted_iota(jnp.int32, (group * rows, keys_total), 0), rows)
    allowed = position <= row
    sums = jnp.zeros((1, keys_total), jnp.float32)
    for g in range(kv_heads):
        key_lanes = slice(g * HEAD_SIZE, (g + 1) * HEAD_SIZE)
        value_lanes = slice((kv_heads + g) * HEAD_SIZE, (kv_heads + g + 1) * HEAD_SIZE)
        key, value = [
            jnp.concatenate([block[:, x] for block in (near, far, pair, odd)], axis=0)
            for x in (key_lanes, value_lanes)
        ]
        heads = range(g * group, (g + 1) * group)
        stacked = jnp.concatenate([queries[:, h * HEAD_SIZE : (h + 1) * HEAD_SIZE] for h in heads], axis=0)
        scores = lax.dot_general(
            stacked, key, (((1,), (1,)), ((), ())), preferred_element_type=jnp.float32
        ) * HEAD_SIZE ** (-0.5)
        scores = jnp.where(allowed, scores, -1e30)
        weights = jnp.exp(scores - jnp.max(scores, axis=1, keepdims=True))
        inverse = 1.0 / jnp.sum(weights, axis=1, keepdims=True)
        mixed = jnp.dot(weights.astype(jnp.bfloat16), value, preferred_element_type=jnp.float32) * inverse
        for i, h in enumerate(heads):
            context[:, h * HEAD_SIZE : (h + 1) * HEAD_SIZE] = mixed[i * rows : (i + 1) * rows]
        sums += jnp.sum(weights * inverse, axis=0, keepdims=True)
    for i, k in enumerate(halving_order(n, masks)):
        at = order.index(k)
        columns[i : i + 1, :] = sums[:, at * rows : (at + 1) * rows]


def finish_kernel(bias, kept, received, *refs):
    *parts, out, scores = refs
    out[...] = kept[...] + received[...].astype(jnp.float32) + bias[...]
    total = parts[0][...]
    for part in parts[1:]:
        total += part[...]
    scores[...] = total / QUERY_HEADS


def shards(queries, keys, values, hidden, norm_gain, retained_lists, counts, affine_matrix, affine_offset_vector):
    n = lax.axis_size("seq")
    rows, model = hidden.shape
    kv_heads = keys.shape[1] // HEAD_SIZE
    half = affine_matrix.shape[0] // 2
    width = affine_matrix.shape[1]
    survivors = n * rows // 2
    lines = survivors // n
    cut = width * 3 // 5 // HEAD_SIZE * HEAD_SIZE
    chunks = [cut, width - cut]
    near = survivors // 2
    f32, bf16, i32 = jnp.float32, jnp.bfloat16, jnp.int32
    shape = jax.ShapeDtypeStruct
    dma = pltpu.SemaphoreType.DMA

    def trade(x, k):
        return lax.ppermute(x, "seq", [(i, i ^ k) for i in range(n)])

    def trade_across(x, k):
        return lax.ppermute(x, ("seq", "ten"), [(2 * i + t, 2 * (i ^ k) + 1 - t) for i in range(n) for t in range(2)])

    def swap(x):
        return lax.ppermute(x, "ten", [(0, 1), (1, 0)])

    chosen = call(
        functools.partial(norm_select_kernel, n),
        "norm_select",
        (hidden, norm_gain.reshape(1, model), retained_lists.reshape(1, rows), keys, values),
        [shape((rows, half + (2 * keys.shape[1] if k == 1 or k in range(0, n // 2, 2) else 0)), bf16) for k in range(n)],
        4 * rows * model,
        limit=16,
        in_specs=[ANY] * 5,
        remote=5,
        scratch=[pltpu.VMEM((rows, model), bf16), pltpu.VMEM((1, model), f32), pltpu.VMEM((1, rows), i32), pltpu.VMEM((rows, 2 * keys.shape[1]), bf16), dma((8,))],
    )
    last = range(n - n // 4, n)
    received = [chosen[0]] + [trade(chosen[k], k) for k in range(1, last[0])]
    relayed = call(
        functools.partial(relay_kernel, len(last)),
        "relay",
        (*[chosen[k] for k in last], received[1], received[3]),
        [shape((rows, half), bf16)] * len(last),
        0,
        in_specs=[VMEM] * len(last) + [ANY] * 2,
    )
    received += [trade(x, k) for k, x in zip(last, relayed)]
    matrix, queries, target = call(
        functools.partial(stage_kernel, n),
        "stage",
        (counts, affine_matrix, queries, *received[n // 2 : last[0]]),
        [shape(affine_matrix.shape, bf16), shape(queries.shape, bf16), shape((1, n * rows), i32)],
        1500 * affine_matrix.size,
        in_specs=[ANY] * (3 + n // 4),
        remote=3,
        scratch=[pltpu.SMEM(counts.shape, i32), dma((3,))],
    )
    own, even, pair = call(
        functools.partial(compact_kernel, n),
        "compact",
        (target, *received),
        [shape((survivors, half), bf16)] + [shape((x * rows, 2 * keys.shape[1]), bf16) for x in (n // 4, 1)],
        2 * survivors * n * rows * half,
    )
    other = swap(own)
    rest = [1 << i for i in range(2, n.bit_length() - 1)]
    masks = [[1, 2] + rest, [2, 1] + rest]
    (product,) = call(
        project_own_kernel,
        "project_own",
        (own, matrix),
        [shape((survivors, width), f32)],
        2 * survivors * half * width,
    )
    products = [
        call(
            functools.partial(project_kernel, c * cut, halving_order(n, masks[c])),
            "project",
            (product, other, matrix),
            [shape((near, chunk), f32), shape((near, chunk), bf16)],
            2 * survivors * half * chunk,
        )
        for c, chunk in enumerate(chunks)
    ]
    far = trade(even, n // 2)
    (gathered,) = call(
        gather_kernel,
        "gather",
        (even, far, products[1][1]),
        [shape((n // 2 * rows - rows, even.shape[1]), bf16)],
        1500 * affine_matrix.size,
        in_specs=[VMEM] * 2 + [ANY],
    )
    odd = trade(gathered, 1)
    kept = [product[0] for product in products]
    arrived = [trade(product[1], masks[c][0]) for c, product in enumerate(products)]
    lines_left = near // 2
    for c, chunk in enumerate(chunks):
        keep, sent = call(
            hop_sum_kernel,
            "hop_sum",
            (kept[c], arrived[c], kept[0] if c else products[1][1]),
            [shape((lines_left, chunk), f32), shape((lines_left, chunk), bf16)],
            near * chunk,
            in_specs=[VMEM] * 2 + [ANY],
        )
        kept[c], arrived[c] = keep, trade(sent, masks[c][1])

    context, columns = call(
        functools.partial(attention_kernel, n, kv_heads, masks[0]),
        "attention",
        (queries, even, far, pair, odd, kept[0]),
        [shape(queries.shape, f32), shape((n, rows), f32)],
        4 * rows * n * rows * queries.shape[1],
        limit=32,
        in_specs=[VMEM] * 5 + [ANY],
    )

    def column_sum(pieces, after, scale=1.0, remote=0):
        (total,) = call(
            functools.partial(column_sum_kernel, scale),
            "column_sum",
            (after, *pieces),
            [shape(pieces[0].shape, f32)],
            0,
            in_specs=[ANY] + [VMEM] * len(pieces),
            remote=remote,
        )
        return total

    pieces = [columns[i * (n // 4) : (i + 1) * (n // 4)] for i in range(4)]
    pieces = pieces[:1] + [trade(x, mask) for x, mask in zip(pieces[1:], (2, 1, 3))]
    for mask in rest:
        lines_left //= 2
        keep, sent = call(
            hop_sum_both_kernel,
            "hop_sum_both",
            (*kept, *arrived),
            [shape((lines_left, width), f32), shape((lines_left, width), bf16)],
            lines_left * width,
        )
        kept, arrived = [keep], [trade(sent, mask)]
        columns = column_sum(pieces, keep)
        left = columns.shape[0] // 2
        own, far = columns[:left], columns[left:]
        pieces = [own, trade(far, mask)]
        if mask == rest[-1]:
            pieces += [swap(own), trade_across(far, mask)]

    triples, scores = call(
        finish_kernel,
        "finish",
        (affine_offset_vector.reshape(1, width), kept[0], arrived[0], *pieces),
        [shape((lines, width), f32), shape((1, rows), f32)],
        n * lines * width,
    )
    return (context, scores.reshape(rows), triples)


def solution(mesh):
    in_specs = (
        P(("grp", "seq"), "ten"),
        P(("grp", "seq"), "ten"),
        P(("grp", "seq"), "ten"),
        P(("grp", "seq"), None),
        P(),
        P(("grp", "seq")),
        P("grp"),
        P("seq", "ten"),
        P("ten"),
    )
    out_specs = (P(("grp", "seq"), "ten"), P(("grp", "seq")), P(("grp", "seq"), "ten"))
    return jax.shard_map(shards, mesh=mesh, in_specs=in_specs, out_specs=out_specs, check_vma=False)
```

```python
import functools
import math

import jax
import jax.numpy as jnp
from jax import lax
from jax.experimental import pallas as pl
from jax.experimental.pallas import tpu as pltpu
from jax.sharding import PartitionSpec as P

HEAD_SIZE = 128
QUERY_HEADS = 32
VMEM = pl.BlockSpec(memory_space=pltpu.VMEM)
ANY = pl.BlockSpec(memory_space=pl.ANY)
MIB = 1024 * 1024


def call(body, name, inputs, outputs, flops, limit=16, in_specs=None, scratch=(), remote=0):
    inputs = [pltpu.with_memory_space_constraint(x, pltpu.HBM) if i < remote else x for i, x in enumerate(inputs)]
    size = sum(math.prod(x.shape) * x.dtype.itemsize for x in list(inputs) + list(outputs))
    return pl.pallas_call(
        body,
        out_shape=list(outputs),
        in_specs=in_specs or [VMEM] * len(inputs),
        out_specs=[VMEM] * len(outputs),
        scratch_shapes=list(scratch),
        compiler_params=pltpu.CompilerParams(vmem_limit_bytes=limit * MIB),
        cost_estimate=pl.CostEstimate(flops=flops, bytes_accessed=size, transcendentals=0),
        name=name,
    )(*inputs)


def norm_select_kernel(n, hidden_in, gain_in, kept_in, keys_in, values_in, *refs):
    outs, (hidden, gain, kept, pair, sems) = refs[:n], refs[n:]
    rows, width = hidden.shape
    block = width // n
    half = block // 2
    pieces = 4
    piece = width // pieces
    key_width = keys_in.shape[1]
    loads = [
        pltpu.make_async_copy(
            hidden_in.at[:, i * piece : (i + 1) * piece], hidden.at[:, i * piece : (i + 1) * piece], sems.at[i]
        )
        for i in range(pieces)
    ]
    loads += [
        pltpu.make_async_copy(gain_in, gain, sems.at[pieces]),
        pltpu.make_async_copy(kept_in, kept, sems.at[pieces + 1]),
        pltpu.make_async_copy(keys_in, pair.at[:, :key_width], sems.at[pieces + 2]),
        pltpu.make_async_copy(values_in, pair.at[:, key_width:], sems.at[pieces + 3]),
    ]
    for load in loads:
        load.start()
    s, t = lax.axis_index("seq"), lax.axis_index("ten")
    step = min(piece, 1024)
    total = jnp.zeros((rows, step), jnp.float32)
    for i in range(pieces):
        loads[i].wait()
        for j in range(i * piece, (i + 1) * piece, step):
            part = hidden[:, j : j + step].astype(jnp.float32)
            total += part * part
    scale = lax.rsqrt(jnp.sum(total, axis=1, keepdims=True) / width + 1e-06)
    for load in loads[pieces:]:
        load.wait()
    selector = (kept[...] == lax.broadcasted_iota(jnp.int32, (rows, rows), 0)).astype(jnp.bfloat16)
    for k in range(n):
        start = pl.multiple_of(lax.bitwise_xor(s, k) * block + t * half, half)
        columns = pl.ds(start, half)
        normed = (hidden[:, columns].astype(jnp.float32) * scale * gain[:, columns]).astype(jnp.bfloat16)
        if outs[k].shape[1] > half:
            outs[k][:, half:] = pair[...]
        outs[k][:, :half] = lax.dot_general(
            selector, normed, (((0,), (0,)), ((), ())), preferred_element_type=jnp.float32
        ).astype(jnp.bfloat16)


def gather_kernel(near, far, after, out):
    rows = near.shape[0] + far.shape[0] - out.shape[0]
    out[: near.shape[0] - rows] = near[rows:]
    out[near.shape[0] - rows :] = far[...]


def relay_kernel(count, *refs):
    blocks, outs = refs[:count], refs[len(refs) - count :]
    for block, out in zip(blocks, outs):
        out[...] = block[...]


def stage_kernel(n, counts_in, matrix_in, queries_in, *refs):
    matrix, queries, target, counts, sems = refs[-5:]
    loads = [
        pltpu.make_async_copy(counts_in, counts, sems.at[0]),
        pltpu.make_async_copy(matrix_in, matrix, sems.at[1]),
        pltpu.make_async_copy(queries_in, queries, sems.at[2]),
    ]
    for load in loads:
        load.start()
    rows = target.shape[1] // n
    s = lax.axis_index("seq")
    loads[0].wait()
    slot_all = lax.broadcasted_iota(jnp.int32, (1, n * rows), 1)
    found = jnp.full((1, n * rows), -1, jnp.int32)
    for k in range(n):
        source = lax.bitwise_xor(s, k)
        begin = jnp.int32(0)
        for i in range(n):
            begin += jnp.where(i < source, counts[i], 0)
        slot = slot_all - k * rows
        inside = (slot >= 0) & (slot < counts[source])
        found = jnp.where(inside, begin + slot, found)
    target[...] = found
    for load in loads[1:]:
        load.wait()


def compact_kernel(n, target, *refs):
    blocks, (out, even, pair) = refs[:n], refs[n:]
    pair[...] = blocks[1][:, out.shape[1] :]
    rows, half = blocks[0].shape[0], out.shape[1]
    for i in range(n // 4):
        even[i * rows : (i + 1) * rows] = blocks[2 * i][:, half:]
    lines = out.shape[0] // n
    s = lax.axis_index("seq")
    received = jnp.concatenate([b[:, :half] for b in blocks], axis=0)
    line = lax.broadcasted_iota(jnp.int32, (lines, received.shape[0]), 0)
    pick = jnp.concatenate(
        [(line + lax.bitwise_xor(s, k) * lines == target[...]).astype(jnp.float32) for k in range(n)], axis=0
    ).astype(jnp.bfloat16)
    out[...] = jnp.dot(pick, received, preferred_element_type=jnp.float32).astype(jnp.bfloat16)


def halving_order(n, masks):
    return sorted(range(n), key=lambda k: [k & mask for mask in masks])


def project_own_kernel(own, matrix, out):
    half = own.shape[1]
    mine = pl.ds(pl.multiple_of(lax.axis_index("ten") * half, half), half)
    tile = out.shape[1] // 4 if out.shape[1] % 512 == 0 else out.shape[1]
    for j in range(0, out.shape[1], tile):
        out[:, j : j + tile] = jnp.dot(own[...], matrix[mine, j : j + tile], preferred_element_type=jnp.float32)


def project_kernel(first, order, product, other, matrix, near, far):
    survivors, half = other.shape
    lines = survivors // len(order)
    width = near.shape[1]
    t = lax.axis_index("ten")
    others = pl.ds(pl.multiple_of((1 - t) * half, half), half)
    tile = width // 2 if width % 256 == 0 else width
    for j in range(0, width, tile):
        lanes = slice(first + j, first + j + tile)
        part = product[:, lanes]
        part += jnp.dot(other[...], matrix[others, lanes], preferred_element_type=jnp.float32)
        for i, k in enumerate(order):
            block = part[k * lines : (k + 1) * lines]
            if i < len(order) // 2:
                near[i * lines : (i + 1) * lines, j : j + tile] = block
            else:
                i -= len(order) // 2
                far[i * lines : (i + 1) * lines, j : j + tile] = block.astype(jnp.bfloat16)


def hop_sum_kernel(kept, received, after, keep, sent):
    rows = keep.shape[0]
    total = kept[...] + received[...].astype(jnp.float32)
    keep[...] = total[:rows]
    sent[...] = total[rows:].astype(jnp.bfloat16)


def hop_sum_both_kernel(*refs):
    *parts, keep, sent = refs
    count = len(parts) // 2
    rows = keep.shape[0]
    first = 0
    for c in range(count):
        lanes = slice(first, first + parts[c].shape[1])
        first = lanes.stop
        total = parts[c][...] + parts[count + c][...].astype(jnp.float32)
        keep[:, lanes] = total[:rows]
        sent[:, lanes] = total[rows:].astype(jnp.bfloat16)


def column_sum_kernel(scale, after, *refs):
    *parts, out = refs
    total = parts[0][...]
    for part in parts[1:]:
        total += part[...]
    out[...] = total * scale


def attention_kernel(n, kv_heads, masks, queries, near, far, pair, odd, after, context, columns):
    rows = queries.shape[0]
    group = queries.shape[1] // (HEAD_SIZE * kv_heads)
    s = lax.axis_index("seq")
    keys_total = n * rows
    column = lax.broadcasted_iota(jnp.int32, (1, keys_total), 1)
    position = column
    order = list(range(0, n, 2)) + list(range(1, n, 2))
    for at, k in enumerate(order):
        inside = (column >= at * rows) & (column < (at + 1) * rows)
        position = jnp.where(inside, column + (lax.bitwise_xor(s, k) - s - at) * rows, position)
    row = lax.rem(lax.broadcasted_iota(jnp.int32, (group * rows, keys_total), 0), rows)
    allowed = position <= row
    sums = jnp.zeros((1, keys_total), jnp.float32)
    for g in range(kv_heads):
        key_lanes = slice(g * HEAD_SIZE, (g + 1) * HEAD_SIZE)
        value_lanes = slice((kv_heads + g) * HEAD_SIZE, (kv_heads + g + 1) * HEAD_SIZE)
        key, value = [
            jnp.concatenate([block[:, x] for block in (near, far, pair, odd)], axis=0)
            for x in (key_lanes, value_lanes)
        ]
        heads = range(g * group, (g + 1) * group)
        stacked = jnp.concatenate([queries[:, h * HEAD_SIZE : (h + 1) * HEAD_SIZE] for h in heads], axis=0)
        scores = lax.dot_general(
            stacked, key, (((1,), (1,)), ((), ())), preferred_element_type=jnp.float32
        ) * HEAD_SIZE ** (-0.5)
        scores = jnp.where(allowed, scores, -1e30)
        weights = jnp.exp(scores - jnp.max(scores, axis=1, keepdims=True))
        inverse = 1.0 / jnp.sum(weights, axis=1, keepdims=True)
        mixed = jnp.dot(weights.astype(jnp.bfloat16), value, preferred_element_type=jnp.float32) * inverse
        for i, h in enumerate(heads):
            context[:, h * HEAD_SIZE : (h + 1) * HEAD_SIZE] = mixed[i * rows : (i + 1) * rows]
        sums += jnp.sum(weights * inverse, axis=0, keepdims=True)
    for i, k in enumerate(halving_order(n, masks)):
        at = order.index(k)
        columns[i : i + 1, :] = sums[:, at * rows : (at + 1) * rows]


def finish_kernel(bias, kept, received, *refs):
    *parts, out, scores = refs
    out[...] = kept[...] + received[...].astype(jnp.float32) + bias[...]
    total = parts[0][...]
    for part in parts[1:]:
        total += part[...]
    scores[...] = total / QUERY_HEADS


def shards(queries, keys, values, hidden, norm_gain, retained_lists, counts, affine_matrix, affine_offset_vector):
    n = lax.axis_size("seq")
    rows, model = hidden.shape
    kv_heads = keys.shape[1] // HEAD_SIZE
    half = affine_matrix.shape[0] // 2
    width = affine_matrix.shape[1]
    survivors = n * rows // 2
    lines = survivors // n
    cut = width // 2
    chunks = [cut, width - cut]
    near = survivors // 2
    f32, bf16, i32 = jnp.float32, jnp.bfloat16, jnp.int32
    shape = jax.ShapeDtypeStruct
    dma = pltpu.SemaphoreType.DMA

    def trade(x, k):
        return lax.ppermute(x, "seq", [(i, i ^ k) for i in range(n)])

    def trade_across(x, k):
        return lax.ppermute(x, ("seq", "ten"), [(2 * i + t, 2 * (i ^ k) + 1 - t) for i in range(n) for t in range(2)])

    def swap(x):
        return lax.ppermute(x, "ten", [(0, 1), (1, 0)])

    chosen = call(
        functools.partial(norm_select_kernel, n),
        "norm_select",
        (hidden, norm_gain.reshape(1, model), retained_lists.reshape(1, rows), keys, values),
        [shape((rows, half + (2 * keys.shape[1] if k == 1 or k in range(0, n // 2, 2) else 0)), bf16) for k in range(n)],
        4 * rows * model,
        limit=16,
        in_specs=[ANY] * 5,
        remote=5,
        scratch=[pltpu.VMEM((rows, model), bf16), pltpu.VMEM((1, model), f32), pltpu.VMEM((1, rows), i32), pltpu.VMEM((rows, 2 * keys.shape[1]), bf16), dma((8,))],
    )
    received = {0: chosen[0]}
    received.update({k: trade(chosen[k], k) for k in [1, *range(n // 2, n)]})
    relayed = call(
        functools.partial(relay_kernel, n // 2 - 2),
        "relay",
        (*chosen[2 : n // 2], received[1]),
        [shape(x.shape, bf16) for x in chosen[2 : n // 2]],
        0,
        in_specs=[VMEM] * (n // 2 - 2) + [ANY],
    )
    received.update({k: trade(x, k) for k, x in zip(range(2, n // 2), relayed)})
    received = [received[k] for k in range(n)]
    matrix, queries, target = call(
        functools.partial(stage_kernel, n),
        "stage",
        (counts, affine_matrix, queries, *received[n // 2 : n // 2 + 2]),
        [shape(affine_matrix.shape, bf16), shape(queries.shape, bf16), shape((1, n * rows), i32)],
        1500 * affine_matrix.size,
        in_specs=[ANY] * 5,
        remote=3,
        scratch=[pltpu.SMEM(counts.shape, i32), dma((3,))],
    )
    own, even, pair = call(
        functools.partial(compact_kernel, n),
        "compact",
        (target, *received),
        [shape((survivors, half), bf16)] + [shape((x * rows, 2 * keys.shape[1]), bf16) for x in (n // 4, 1)],
        2 * survivors * n * rows * half,
    )
    other = swap(own)
    rest = [1 << i for i in range(2, n.bit_length() - 1)]
    masks = [[1, 2] + rest, [2, 1] + rest]
    (product,) = call(
        project_own_kernel,
        "project_own",
        (own, matrix),
        [shape((survivors, width), f32)],
        2 * survivors * half * width,
    )
    products = [
        call(
            functools.partial(project_kernel, c * cut, halving_order(n, masks[c])),
            "project",
            (product, other, matrix),
            [shape((near, chunk), f32), shape((near, chunk), bf16)],
            2 * survivors * half * chunk,
        )
        for c, chunk in enumerate(chunks)
    ]
    far = trade(even, n // 2)
    (gathered,) = call(
        gather_kernel,
        "gather",
        (even, far, products[1][1]),
        [shape((n // 2 * rows - rows, even.shape[1]), bf16)],
        1500 * affine_matrix.size,
        in_specs=[VMEM] * 2 + [ANY],
    )
    odd = trade(gathered, 1)
    kept = [product[0] for product in products]
    arrived = [trade(product[1], masks[c][0]) for c, product in enumerate(products)]
    lines_left = near // 2
    for c, chunk in enumerate(chunks):
        keep, sent = call(
            hop_sum_kernel,
            "hop_sum",
            (kept[c], arrived[c], kept[0] if c else products[1][1]),
            [shape((lines_left, chunk), f32), shape((lines_left, chunk), bf16)],
            near * chunk,
            in_specs=[VMEM] * 2 + [ANY],
        )
        kept[c], arrived[c] = keep, trade(sent, masks[c][1])

    context, columns = call(
        functools.partial(attention_kernel, n, kv_heads, masks[0]),
        "attention",
        (queries, even, far, pair, odd, kept[0]),
        [shape(queries.shape, f32), shape((n, rows), f32)],
        4 * rows * n * rows * queries.shape[1],
        limit=32,
        in_specs=[VMEM] * 5 + [ANY],
    )

    def column_sum(pieces, after, scale=1.0, remote=0):
        (total,) = call(
            functools.partial(column_sum_kernel, scale),
            "column_sum",
            (after, *pieces),
            [shape(pieces[0].shape, f32)],
            0,
            in_specs=[ANY] + [VMEM] * len(pieces),
            remote=remote,
        )
        return total

    pieces = [columns[i * (n // 4) : (i + 1) * (n // 4)] for i in range(4)]
    pieces = pieces[:1] + [trade(x, mask) for x, mask in zip(pieces[1:], (2, 1, 3))]
    for mask in rest:
        lines_left //= 2
        keep, sent = call(
            hop_sum_both_kernel,
            "hop_sum_both",
            (*kept, *arrived),
            [shape((lines_left, width), f32), shape((lines_left, width), bf16)],
            lines_left * width,
        )
        kept, arrived = [keep], [trade(sent, mask)]
        columns = column_sum(pieces, keep)
        left = columns.shape[0] // 2
        own, far = columns[:left], columns[left:]
        pieces = [own, trade(far, mask)]
        if mask == rest[-1]:
            pieces += [swap(own), trade_across(far, mask)]

    triples, scores = call(
        finish_kernel,
        "finish",
        (affine_offset_vector.reshape(1, width), kept[0], arrived[0], *pieces),
        [shape((lines, width), f32), shape((1, rows), f32)],
        n * lines * width,
    )
    return (context, scores.reshape(rows), triples)


def solution(mesh):
    in_specs = (
        P(("grp", "seq"), "ten"),
        P(("grp", "seq"), "ten"),
        P(("grp", "seq"), "ten"),
        P(("grp", "seq"), None),
        P(),
        P(("grp", "seq")),
        P("grp"),
        P("seq", "ten"),
        P("ten"),
    )
    out_specs = (P(("grp", "seq"), "ten"), P(("grp", "seq")), P(("grp", "seq"), "ten"))
    return jax.shard_map(shards, mesh=mesh, in_specs=in_specs, out_specs=out_specs, check_vma=False)
```

```python
import functools
import math

import jax
import jax.numpy as jnp
from jax import lax
from jax.experimental import pallas as pl
from jax.experimental.pallas import tpu as pltpu
from jax.sharding import PartitionSpec as P

HEAD_SIZE = 128
QUERY_HEADS = 32
VMEM = pl.BlockSpec(memory_space=pltpu.VMEM)
ANY = pl.BlockSpec(memory_space=pl.ANY)
MIB = 1024 * 1024


def call(body, name, inputs, outputs, flops, limit=16, in_specs=None, scratch=(), remote=0):
    inputs = [pltpu.with_memory_space_constraint(x, pltpu.HBM) if i < remote else x for i, x in enumerate(inputs)]
    size = sum(math.prod(x.shape) * x.dtype.itemsize for x in list(inputs) + list(outputs))
    return pl.pallas_call(
        body,
        out_shape=list(outputs),
        in_specs=in_specs or [VMEM] * len(inputs),
        out_specs=[VMEM] * len(outputs),
        scratch_shapes=list(scratch),
        compiler_params=pltpu.CompilerParams(vmem_limit_bytes=limit * MIB),
        cost_estimate=pl.CostEstimate(flops=flops, bytes_accessed=size, transcendentals=0),
        name=name,
    )(*inputs)


def norm_select_kernel(n, hidden_in, gain_in, kept_in, keys_in, values_in, *refs):
    outs, (hidden, gain, kept, pair, sems) = refs[:n], refs[n:]
    rows, width = hidden.shape
    block = width // n
    half = block // 2
    pieces = 4
    piece = width // pieces
    key_width = keys_in.shape[1]
    loads = [
        pltpu.make_async_copy(
            hidden_in.at[:, i * piece : (i + 1) * piece], hidden.at[:, i * piece : (i + 1) * piece], sems.at[i]
        )
        for i in range(pieces)
    ]
    loads += [
        pltpu.make_async_copy(gain_in, gain, sems.at[pieces]),
        pltpu.make_async_copy(kept_in, kept, sems.at[pieces + 1]),
        pltpu.make_async_copy(keys_in, pair.at[:, :key_width], sems.at[pieces + 2]),
        pltpu.make_async_copy(values_in, pair.at[:, key_width:], sems.at[pieces + 3]),
    ]
    for load in loads:
        load.start()
    s, t = lax.axis_index("seq"), lax.axis_index("ten")
    step = min(piece, 1024)
    total = jnp.zeros((rows, step), jnp.float32)
    for i in range(pieces):
        loads[i].wait()
        for j in range(i * piece, (i + 1) * piece, step):
            part = hidden[:, j : j + step].astype(jnp.float32)
            total += part * part
    scale = lax.rsqrt(jnp.sum(total, axis=1, keepdims=True) / width + 1e-06)
    for load in loads[pieces:]:
        load.wait()
    selector = (kept[...] == lax.broadcasted_iota(jnp.int32, (rows, rows), 0)).astype(jnp.bfloat16)
    for k in range(n):
        start = pl.multiple_of(lax.bitwise_xor(s, k) * block + t * half, half)
        columns = pl.ds(start, half)
        normed = (hidden[:, columns].astype(jnp.float32) * scale * gain[:, columns]).astype(jnp.bfloat16)
        if outs[k].shape[1] > half:
            outs[k][:, half:] = pair[...]
        outs[k][:, :half] = lax.dot_general(
            selector, normed, (((0,), (0,)), ((), ())), preferred_element_type=jnp.float32
        ).astype(jnp.bfloat16)


def gather_kernel(near, far, after, out):
    rows = near.shape[0] + far.shape[0] - out.shape[0]
    out[: near.shape[0] - rows] = near[rows:]
    out[near.shape[0] - rows :] = far[...]


def relay_kernel(count, *refs):
    blocks, outs = refs[:count], refs[len(refs) - count :]
    for block, out in zip(blocks, outs):
        out[...] = block[...]


def stage_kernel(n, counts_in, matrix_in, queries_in, *refs):
    matrix, queries, target, counts, sems = refs[-5:]
    loads = [
        pltpu.make_async_copy(counts_in, counts, sems.at[0]),
        pltpu.make_async_copy(matrix_in, matrix, sems.at[1]),
        pltpu.make_async_copy(queries_in, queries, sems.at[2]),
    ]
    for load in loads:
        load.start()
    rows = target.shape[1] // n
    s = lax.axis_index("seq")
    loads[0].wait()
    slot_all = lax.broadcasted_iota(jnp.int32, (1, n * rows), 1)
    found = jnp.full((1, n * rows), -1, jnp.int32)
    for k in range(n):
        source = lax.bitwise_xor(s, k)
        begin = jnp.int32(0)
        for i in range(n):
            begin += jnp.where(i < source, counts[i], 0)
        slot = slot_all - k * rows
        inside = (slot >= 0) & (slot < counts[source])
        found = jnp.where(inside, begin + slot, found)
    target[...] = found
    for load in loads[1:]:
        load.wait()


def compact_kernel(n, target, *refs):
    blocks, (out, even, pair) = refs[:n], refs[n:]
    pair[...] = blocks[1][:, out.shape[1] :]
    rows, half = blocks[0].shape[0], out.shape[1]
    for i in range(n // 4):
        even[i * rows : (i + 1) * rows] = blocks[2 * i][:, half:]
    lines = out.shape[0] // n
    s = lax.axis_index("seq")
    received = jnp.concatenate([b[:, :half] for b in blocks], axis=0)
    line = lax.broadcasted_iota(jnp.int32, (lines, received.shape[0]), 0)
    pick = jnp.concatenate(
        [(line + lax.bitwise_xor(s, k) * lines == target[...]).astype(jnp.float32) for k in range(n)], axis=0
    ).astype(jnp.bfloat16)
    out[...] = jnp.dot(pick, received, preferred_element_type=jnp.float32).astype(jnp.bfloat16)


def halving_order(n, masks):
    return sorted(range(n), key=lambda k: [k & mask for mask in masks])


def project_own_kernel(own, matrix, out):
    half = own.shape[1]
    mine = pl.ds(pl.multiple_of(lax.axis_index("ten") * half, half), half)
    tile = out.shape[1] // 4 if out.shape[1] % 512 == 0 else out.shape[1]
    for j in range(0, out.shape[1], tile):
        out[:, j : j + tile] = jnp.dot(own[...], matrix[mine, j : j + tile], preferred_element_type=jnp.float32)


def project_kernel(first, order, product, other, matrix, near, far):
    survivors, half = other.shape
    lines = survivors // len(order)
    width = near.shape[1]
    t = lax.axis_index("ten")
    others = pl.ds(pl.multiple_of((1 - t) * half, half), half)
    tile = width // 2 if width % 256 == 0 else width
    for j in range(0, width, tile):
        lanes = slice(first + j, first + j + tile)
        part = product[:, lanes]
        part += jnp.dot(other[...], matrix[others, lanes], preferred_element_type=jnp.float32)
        for i, k in enumerate(order):
            block = part[k * lines : (k + 1) * lines]
            if i < len(order) // 2:
                near[i * lines : (i + 1) * lines, j : j + tile] = block
            else:
                i -= len(order) // 2
                far[i * lines : (i + 1) * lines, j : j + tile] = block.astype(jnp.bfloat16)


def hop_sum_kernel(kept, received, after, keep, sent):
    rows = keep.shape[0]
    total = kept[...] + received[...].astype(jnp.float32)
    keep[...] = total[:rows]
    sent[...] = total[rows:].astype(jnp.bfloat16)


def hop_sum_both_kernel(*refs):
    *parts, keep, sent = refs
    count = len(parts) // 2
    rows = keep.shape[0]
    first = 0
    for c in range(count):
        lanes = slice(first, first + parts[c].shape[1])
        first = lanes.stop
        total = parts[c][...] + parts[count + c][...].astype(jnp.float32)
        keep[:, lanes] = total[:rows]
        sent[:, lanes] = total[rows:].astype(jnp.bfloat16)


def column_sum_kernel(scale, after, *refs):
    *parts, out = refs
    total = parts[0][...]
    for part in parts[1:]:
        total += part[...]
    out[...] = total * scale


def attention_kernel(n, kv_heads, masks, queries, near, far, pair, odd, after, context, columns):
    rows = queries.shape[0]
    group = queries.shape[1] // (HEAD_SIZE * kv_heads)
    s = lax.axis_index("seq")
    keys_total = n * rows
    column = lax.broadcasted_iota(jnp.int32, (1, keys_total), 1)
    position = column
    order = list(range(0, n, 2)) + list(range(1, n, 2))
    for at, k in enumerate(order):
        inside = (column >= at * rows) & (column < (at + 1) * rows)
        position = jnp.where(inside, column + (lax.bitwise_xor(s, k) - s - at) * rows, position)
    row = lax.rem(lax.broadcasted_iota(jnp.int32, (group * rows, keys_total), 0), rows)
    allowed = position <= row
    sums = jnp.zeros((1, keys_total), jnp.float32)
    for g in range(kv_heads):
        key_lanes = slice(g * HEAD_SIZE, (g + 1) * HEAD_SIZE)
        value_lanes = slice((kv_heads + g) * HEAD_SIZE, (kv_heads + g + 1) * HEAD_SIZE)
        key, value = [
            jnp.concatenate([block[:, x] for block in (near, far, pair, odd)], axis=0)
            for x in (key_lanes, value_lanes)
        ]
        heads = range(g * group, (g + 1) * group)
        stacked = jnp.concatenate([queries[:, h * HEAD_SIZE : (h + 1) * HEAD_SIZE] for h in heads], axis=0)
        scores = lax.dot_general(
            stacked, key, (((1,), (1,)), ((), ())), preferred_element_type=jnp.float32
        ) * HEAD_SIZE ** (-0.5)
        scores = jnp.where(allowed, scores, -1e30)
        weights = jnp.exp(scores - jnp.max(scores, axis=1, keepdims=True))
        inverse = 1.0 / jnp.sum(weights, axis=1, keepdims=True)
        mixed = jnp.dot(weights.astype(jnp.bfloat16), value, preferred_element_type=jnp.float32) * inverse
        for i, h in enumerate(heads):
            context[:, h * HEAD_SIZE : (h + 1) * HEAD_SIZE] = mixed[i * rows : (i + 1) * rows]
        sums += jnp.sum(weights * inverse, axis=0, keepdims=True)
    for i, k in enumerate(halving_order(n, masks)):
        at = order.index(k)
        columns[i : i + 1, :] = sums[:, at * rows : (at + 1) * rows]


def finish_kernel(bias, kept, received, *refs):
    *parts, out, scores = refs
    out[...] = kept[...] + received[...].astype(jnp.float32) + bias[...]
    total = parts[0][...]
    for part in parts[1:]:
        total += part[...]
    scores[...] = total / QUERY_HEADS


def shards(queries, keys, values, hidden, norm_gain, retained_lists, counts, affine_matrix, affine_offset_vector):
    n = lax.axis_size("seq")
    rows, model = hidden.shape
    kv_heads = keys.shape[1] // HEAD_SIZE
    half = affine_matrix.shape[0] // 2
    width = affine_matrix.shape[1]
    survivors = n * rows // 2
    lines = survivors // n
    cut = width * 11 // 20 // HEAD_SIZE * HEAD_SIZE
    chunks = [cut, width - cut]
    near = survivors // 2
    f32, bf16, i32 = jnp.float32, jnp.bfloat16, jnp.int32
    shape = jax.ShapeDtypeStruct
    dma = pltpu.SemaphoreType.DMA

    def trade(x, k):
        return lax.ppermute(x, "seq", [(i, i ^ k) for i in range(n)])

    def give_later(x, k):
        return lax.ppermute(x, "seq", [(i, i ^ k) for i in range(n) if i < i ^ k])

    def trade_across(x, k):
        return lax.ppermute(x, ("seq", "ten"), [(2 * i + t, 2 * (i ^ k) + 1 - t) for i in range(n) for t in range(2)])

    def swap(x):
        return lax.ppermute(x, "ten", [(0, 1), (1, 0)])

    chosen = call(
        functools.partial(norm_select_kernel, n),
        "norm_select",
        (hidden, norm_gain.reshape(1, model), retained_lists.reshape(1, rows), keys, values),
        [shape((rows, half + (2 * keys.shape[1] if k == 1 or k in range(0, n // 2, 2) else 0)), bf16) for k in range(n)],
        4 * rows * model,
        limit=16,
        in_specs=[ANY] * 5,
        remote=5,
        scratch=[pltpu.VMEM((rows, model), bf16), pltpu.VMEM((1, model), f32), pltpu.VMEM((1, rows), i32), pltpu.VMEM((rows, 2 * keys.shape[1]), bf16), dma((8,))],
    )
    received = {0: chosen[0]}
    received.update({k: trade(chosen[k], k) for k in [1, *range(n // 2, n)]})
    relayed = call(
        functools.partial(relay_kernel, n // 2 - 2),
        "relay",
        (*chosen[2 : n // 2], received[1]),
        [shape(x.shape, bf16) for x in chosen[2 : n // 2]],
        0,
        in_specs=[VMEM] * (n // 2 - 2) + [ANY],
    )
    received.update({k: trade(x, k) for k, x in zip(range(2, n // 2), relayed)})
    received = [received[k] for k in range(n)]
    matrix, queries, target = call(
        functools.partial(stage_kernel, n),
        "stage",
        (counts, affine_matrix, queries, *received[n // 2 : n // 2 + 2]),
        [shape(affine_matrix.shape, bf16), shape(queries.shape, bf16), shape((1, n * rows), i32)],
        1500 * affine_matrix.size,
        in_specs=[ANY] * 5,
        remote=3,
        scratch=[pltpu.SMEM(counts.shape, i32), dma((3,))],
    )
    own, even, pair = call(
        functools.partial(compact_kernel, n),
        "compact",
        (target, *received),
        [shape((survivors, half), bf16)] + [shape((x * rows, 2 * keys.shape[1]), bf16) for x in (n // 4, 1)],
        2 * survivors * n * rows * half,
    )
    other = swap(own)
    rest = [1 << i for i in range(2, n.bit_length() - 1)]
    masks = [[1, 2] + rest, [2, 1] + rest]
    (product,) = call(
        project_own_kernel,
        "project_own",
        (own, matrix),
        [shape((survivors, width), f32)],
        2 * survivors * half * width,
    )
    products = [
        call(
            functools.partial(project_kernel, c * cut, halving_order(n, masks[c])),
            "project",
            (product, other, matrix),
            [shape((near, chunk), f32), shape((near, chunk), bf16)],
            2 * survivors * half * chunk,
        )
        for c, chunk in enumerate(chunks)
    ]
    far = give_later(even, n // 2)
    (gathered,) = call(
        gather_kernel,
        "gather",
        (even, far, products[1][1]),
        [shape((n // 2 * rows - rows, even.shape[1]), bf16)],
        1500 * affine_matrix.size,
        in_specs=[VMEM] * 2 + [ANY],
    )
    odd = trade(gathered, 1)
    kept = [product[0] for product in products]
    arrived = [trade(product[1], masks[c][0]) for c, product in enumerate(products)]
    lines_left = near // 2
    for c, chunk in enumerate(chunks):
        keep, sent = call(
            hop_sum_kernel,
            "hop_sum",
            (kept[c], arrived[c], kept[0] if c else products[1][1]),
            [shape((lines_left, chunk), f32), shape((lines_left, chunk), bf16)],
            near * chunk,
            in_specs=[VMEM] * 2 + [ANY],
        )
        kept[c], arrived[c] = keep, trade(sent, masks[c][1])

    context, columns = call(
        functools.partial(attention_kernel, n, kv_heads, masks[0]),
        "attention",
        (queries, even, far, pair, odd, kept[0]),
        [shape(queries.shape, f32), shape((n, rows), f32)],
        4 * rows * n * rows * queries.shape[1],
        limit=32,
        in_specs=[VMEM] * 5 + [ANY],
    )

    def column_sum(pieces, after, scale=1.0, remote=0):
        (total,) = call(
            functools.partial(column_sum_kernel, scale),
            "column_sum",
            (after, *pieces),
            [shape(pieces[0].shape, f32)],
            0,
            in_specs=[ANY] + [VMEM] * len(pieces),
            remote=remote,
        )
        return total

    pieces = [columns[i * (n // 4) : (i + 1) * (n // 4)] for i in range(4)]
    pieces = pieces[:1] + [trade(x, mask) for x, mask in zip(pieces[1:], (2, 1, 3))]
    for mask in rest:
        lines_left //= 2
        keep, sent = call(
            hop_sum_both_kernel,
            "hop_sum_both",
            (*kept, *arrived),
            [shape((lines_left, width), f32), shape((lines_left, width), bf16)],
            lines_left * width,
        )
        kept, arrived = [keep], [trade(sent, mask)]
        columns = column_sum(pieces, keep)
        left = columns.shape[0] // 2
        own, far = columns[:left], columns[left:]
        pieces = [own, trade(far, mask)]
        if mask == rest[-1]:
            pieces += [swap(own), trade_across(far, mask)]

    triples, scores = call(
        finish_kernel,
        "finish",
        (affine_offset_vector.reshape(1, width), kept[0], arrived[0], *pieces),
        [shape((lines, width), f32), shape((1, rows), f32)],
        n * lines * width,
    )
    return (context, scores.reshape(rows), triples)


def solution(mesh):
    in_specs = (
        P(("grp", "seq"), "ten"),
        P(("grp", "seq"), "ten"),
        P(("grp", "seq"), "ten"),
        P(("grp", "seq"), None),
        P(),
        P(("grp", "seq")),
        P("grp"),
        P("seq", "ten"),
        P("ten"),
    )
    out_specs = (P(("grp", "seq"), "ten"), P(("grp", "seq")), P(("grp", "seq"), "ten"))
    return jax.shard_map(shards, mesh=mesh, in_specs=in_specs, out_specs=out_specs, check_vma=False)
```

```python
import functools
import math

import jax
import jax.numpy as jnp
from jax import lax
from jax.experimental import pallas as pl
from jax.experimental.pallas import tpu as pltpu
from jax.sharding import PartitionSpec as P

HEAD_SIZE = 128
QUERY_HEADS = 32
VMEM = pl.BlockSpec(memory_space=pltpu.VMEM)
ANY = pl.BlockSpec(memory_space=pl.ANY)
MIB = 1024 * 1024


def call(body, name, inputs, outputs, flops, limit=16, in_specs=None, scratch=(), remote=0):
    inputs = [pltpu.with_memory_space_constraint(x, pltpu.HBM) if i < remote else x for i, x in enumerate(inputs)]
    size = sum(math.prod(x.shape) * x.dtype.itemsize for x in list(inputs) + list(outputs))
    return pl.pallas_call(
        body,
        out_shape=list(outputs),
        in_specs=in_specs or [VMEM] * len(inputs),
        out_specs=[VMEM] * len(outputs),
        scratch_shapes=list(scratch),
        compiler_params=pltpu.CompilerParams(vmem_limit_bytes=limit * MIB),
        cost_estimate=pl.CostEstimate(flops=flops, bytes_accessed=size, transcendentals=0),
        name=name,
    )(*inputs)


def norm_select_kernel(n, hidden_in, gain_in, kept_in, keys_in, values_in, *refs):
    outs, (hidden, gain, kept, pair, sems) = refs[:n], refs[n:]
    rows, width = hidden.shape
    block = width // n
    half = block // 2
    pieces = 4
    piece = width // pieces
    key_width = keys_in.shape[1]
    loads = [
        pltpu.make_async_copy(
            hidden_in.at[:, i * piece : (i + 1) * piece], hidden.at[:, i * piece : (i + 1) * piece], sems.at[i]
        )
        for i in range(pieces)
    ]
    loads += [
        pltpu.make_async_copy(gain_in, gain, sems.at[pieces]),
        pltpu.make_async_copy(kept_in, kept, sems.at[pieces + 1]),
        pltpu.make_async_copy(keys_in, pair.at[:, :key_width], sems.at[pieces + 2]),
        pltpu.make_async_copy(values_in, pair.at[:, key_width:], sems.at[pieces + 3]),
    ]
    for load in loads:
        load.start()
    s, t = lax.axis_index("seq"), lax.axis_index("ten")
    step = min(piece, 1024)
    total = jnp.zeros((rows, step), jnp.float32)
    for i in range(pieces):
        loads[i].wait()
        for j in range(i * piece, (i + 1) * piece, step):
            part = hidden[:, j : j + step].astype(jnp.float32)
            total += part * part
    scale = lax.rsqrt(jnp.sum(total, axis=1, keepdims=True) / width + 1e-06)
    for load in loads[pieces:]:
        load.wait()
    selector = (kept[...] == lax.broadcasted_iota(jnp.int32, (rows, rows), 0)).astype(jnp.bfloat16)
    for k in range(n):
        start = pl.multiple_of(lax.bitwise_xor(s, k) * block + t * half, half)
        columns = pl.ds(start, half)
        normed = (hidden[:, columns].astype(jnp.float32) * scale * gain[:, columns]).astype(jnp.bfloat16)
        if outs[k].shape[1] > half:
            outs[k][:, half:] = pair[...]
        outs[k][:, :half] = lax.dot_general(
            selector, normed, (((0,), (0,)), ((), ())), preferred_element_type=jnp.float32
        ).astype(jnp.bfloat16)


def gather_kernel(near, far, after, out):
    rows = near.shape[0] + far.shape[0] - out.shape[0]
    out[: near.shape[0] - rows] = near[rows:]
    out[near.shape[0] - rows :] = far[...]


def relay_kernel(count, *refs):
    blocks, outs = refs[:count], refs[len(refs) - count :]
    for block, out in zip(blocks, outs):
        out[...] = block[...]


def stage_kernel(n, counts_in, matrix_in, queries_in, *refs):
    matrix, queries, target, counts, sems = refs[-5:]
    loads = [
        pltpu.make_async_copy(counts_in, counts, sems.at[0]),
        pltpu.make_async_copy(matrix_in, matrix, sems.at[1]),
        pltpu.make_async_copy(queries_in, queries, sems.at[2]),
    ]
    for load in loads:
        load.start()
    rows = target.shape[1] // n
    s = lax.axis_index("seq")
    loads[0].wait()
    slot_all = lax.broadcasted_iota(jnp.int32, (1, n * rows), 1)
    found = jnp.full((1, n * rows), -1, jnp.int32)
    for k in range(n):
        source = lax.bitwise_xor(s, k)
        begin = jnp.int32(0)
        for i in range(n):
            begin += jnp.where(i < source, counts[i], 0)
        slot = slot_all - k * rows
        inside = (slot >= 0) & (slot < counts[source])
        found = jnp.where(inside, begin + slot, found)
    target[...] = found
    for load in loads[1:]:
        load.wait()


def compact_kernel(n, target, *refs):
    blocks, (out, even, pair) = refs[:n], refs[n:]
    pair[...] = blocks[1][:, out.shape[1] :]
    rows, half = blocks[0].shape[0], out.shape[1]
    for i in range(n // 4):
        even[i * rows : (i + 1) * rows] = blocks[2 * i][:, half:]
    lines = out.shape[0] // n
    s = lax.axis_index("seq")
    received = jnp.concatenate([b[:, :half] for b in blocks], axis=0)
    line = lax.broadcasted_iota(jnp.int32, (lines, received.shape[0]), 0)
    pick = jnp.concatenate(
        [(line + lax.bitwise_xor(s, k) * lines == target[...]).astype(jnp.float32) for k in range(n)], axis=0
    ).astype(jnp.bfloat16)
    out[...] = jnp.dot(pick, received, preferred_element_type=jnp.float32).astype(jnp.bfloat16)


def halving_order(n, masks):
    return sorted(range(n), key=lambda k: [k & mask for mask in masks])


def project_own_kernel(own, matrix, even_in, out, even):
    even[...] = even_in[...]
    half = own.shape[1]
    mine = pl.ds(pl.multiple_of(lax.axis_index("ten") * half, half), half)
    tile = out.shape[1] // 4 if out.shape[1] % 512 == 0 else out.shape[1]
    for j in range(0, out.shape[1], tile):
        out[:, j : j + tile] = jnp.dot(own[...], matrix[mine, j : j + tile], preferred_element_type=jnp.float32)


def project_kernel(first, order, product, other, matrix, near, far):
    survivors, half = other.shape
    lines = survivors // len(order)
    width = near.shape[1]
    t = lax.axis_index("ten")
    others = pl.ds(pl.multiple_of((1 - t) * half, half), half)
    tile = width // 2 if width % 256 == 0 else width
    for j in range(0, width, tile):
        lanes = slice(first + j, first + j + tile)
        part = product[:, lanes]
        part += jnp.dot(other[...], matrix[others, lanes], preferred_element_type=jnp.float32)
        for i, k in enumerate(order):
            block = part[k * lines : (k + 1) * lines]
            if i < len(order) // 2:
                near[i * lines : (i + 1) * lines, j : j + tile] = block
            else:
                i -= len(order) // 2
                far[i * lines : (i + 1) * lines, j : j + tile] = block.astype(jnp.bfloat16)


def hop_sum_kernel(kept, received, after, keep, sent):
    rows = keep.shape[0]
    total = kept[...] + received[...].astype(jnp.float32)
    keep[...] = total[:rows]
    sent[...] = total[rows:].astype(jnp.bfloat16)


def hop_sum_both_kernel(*refs):
    *parts, keep, sent = refs
    count = len(parts) // 2
    rows = keep.shape[0]
    first = 0
    for c in range(count):
        lanes = slice(first, first + parts[c].shape[1])
        first = lanes.stop
        total = parts[c][...] + parts[count + c][...].astype(jnp.float32)
        keep[:, lanes] = total[:rows]
        sent[:, lanes] = total[rows:].astype(jnp.bfloat16)


def column_sum_kernel(scale, after, *refs):
    *parts, out = refs
    total = parts[0][...]
    for part in parts[1:]:
        total += part[...]
    out[...] = total * scale


def attention_kernel(n, kv_heads, masks, queries, near, far, pair, odd, after, context, columns):
    rows = queries.shape[0]
    group = queries.shape[1] // (HEAD_SIZE * kv_heads)
    s = lax.axis_index("seq")
    keys_total = n * rows
    column = lax.broadcasted_iota(jnp.int32, (1, keys_total), 1)
    position = column
    order = list(range(0, n, 2)) + list(range(1, n, 2))
    for at, k in enumerate(order):
        inside = (column >= at * rows) & (column < (at + 1) * rows)
        position = jnp.where(inside, column + (lax.bitwise_xor(s, k) - s - at) * rows, position)
    row = lax.rem(lax.broadcasted_iota(jnp.int32, (group * rows, keys_total), 0), rows)
    allowed = position <= row
    sums = jnp.zeros((1, keys_total), jnp.float32)
    for g in range(kv_heads):
        key_lanes = slice(g * HEAD_SIZE, (g + 1) * HEAD_SIZE)
        value_lanes = slice((kv_heads + g) * HEAD_SIZE, (kv_heads + g + 1) * HEAD_SIZE)
        key, value = [
            jnp.concatenate([block[:, x] for block in (near, far, pair, odd)], axis=0)
            for x in (key_lanes, value_lanes)
        ]
        heads = range(g * group, (g + 1) * group)
        stacked = jnp.concatenate([queries[:, h * HEAD_SIZE : (h + 1) * HEAD_SIZE] for h in heads], axis=0)
        scores = lax.dot_general(
            stacked, key, (((1,), (1,)), ((), ())), preferred_element_type=jnp.float32
        ) * HEAD_SIZE ** (-0.5)
        scores = jnp.where(allowed, scores, -1e30)
        weights = jnp.exp(scores - jnp.max(scores, axis=1, keepdims=True))
        inverse = 1.0 / jnp.sum(weights, axis=1, keepdims=True)
        mixed = jnp.dot(weights.astype(jnp.bfloat16), value, preferred_element_type=jnp.float32) * inverse
        for i, h in enumerate(heads):
            context[:, h * HEAD_SIZE : (h + 1) * HEAD_SIZE] = mixed[i * rows : (i + 1) * rows]
        sums += jnp.sum(weights * inverse, axis=0, keepdims=True)
    for i, k in enumerate(halving_order(n, masks)):
        at = order.index(k)
        columns[i : i + 1, :] = sums[:, at * rows : (at + 1) * rows]


def finish_kernel(bias, kept, received, *refs):
    *parts, out, scores = refs
    out[...] = kept[...] + received[...].astype(jnp.float32) + bias[...]
    total = parts[0][...]
    for part in parts[1:]:
        total += part[...]
    scores[...] = total / QUERY_HEADS


def shards(queries, keys, values, hidden, norm_gain, retained_lists, counts, affine_matrix, affine_offset_vector):
    n = lax.axis_size("seq")
    rows, model = hidden.shape
    kv_heads = keys.shape[1] // HEAD_SIZE
    half = affine_matrix.shape[0] // 2
    width = affine_matrix.shape[1]
    survivors = n * rows // 2
    lines = survivors // n
    cut = width // 2
    chunks = [cut, width - cut]
    near = survivors // 2
    f32, bf16, i32 = jnp.float32, jnp.bfloat16, jnp.int32
    shape = jax.ShapeDtypeStruct
    dma = pltpu.SemaphoreType.DMA

    def trade(x, k):
        return lax.ppermute(x, "seq", [(i, i ^ k) for i in range(n)])

    def trade_across(x, k):
        return lax.ppermute(x, ("seq", "ten"), [(2 * i + t, 2 * (i ^ k) + 1 - t) for i in range(n) for t in range(2)])

    def swap(x):
        return lax.ppermute(x, "ten", [(0, 1), (1, 0)])

    chosen = call(
        functools.partial(norm_select_kernel, n),
        "norm_select",
        (hidden, norm_gain.reshape(1, model), retained_lists.reshape(1, rows), keys, values),
        [shape((rows, half + (2 * keys.shape[1] if k == 1 or k in range(0, n // 2, 2) else 0)), bf16) for k in range(n)],
        4 * rows * model,
        limit=16,
        in_specs=[ANY] * 5,
        remote=5,
        scratch=[pltpu.VMEM((rows, model), bf16), pltpu.VMEM((1, model), f32), pltpu.VMEM((1, rows), i32), pltpu.VMEM((rows, 2 * keys.shape[1]), bf16), dma((8,))],
    )
    received = {0: chosen[0]}
    received.update({k: trade(chosen[k], k) for k in [1, *range(n // 2, n)]})
    relayed = call(
        functools.partial(relay_kernel, n // 2 - 2),
        "relay",
        (*chosen[2 : n // 2], received[1]),
        [shape(x.shape, bf16) for x in chosen[2 : n // 2]],
        0,
        in_specs=[VMEM] * (n // 2 - 2) + [ANY],
    )
    received.update({k: trade(x, k) for k, x in zip(range(2, n // 2), relayed)})
    received = [received[k] for k in range(n)]
    matrix, queries, target = call(
        functools.partial(stage_kernel, n),
        "stage",
        (counts, affine_matrix, queries, *received[n // 2 : n // 2 + 2]),
        [shape(affine_matrix.shape, bf16), shape(queries.shape, bf16), shape((1, n * rows), i32)],
        1500 * affine_matrix.size,
        in_specs=[ANY] * 5,
        remote=3,
        scratch=[pltpu.SMEM(counts.shape, i32), dma((3,))],
    )
    own, even, pair = call(
        functools.partial(compact_kernel, n),
        "compact",
        (target, *received),
        [shape((survivors, half), bf16)] + [shape((x * rows, 2 * keys.shape[1]), bf16) for x in (n // 4, 1)],
        2 * survivors * n * rows * half,
    )
    other = swap(own)
    rest = [1 << i for i in range(2, n.bit_length() - 1)]
    masks = [[1, 2] + rest, [2, 1] + rest]
    product, even = call(
        project_own_kernel,
        "project_own",
        (own, matrix, even),
        [shape((survivors, width), f32), shape(even.shape, bf16)],
        2 * survivors * half * width,
    )
    products = [
        call(
            functools.partial(project_kernel, c * cut, halving_order(n, masks[c])),
            "project",
            (product, other, matrix),
            [shape((near, chunk), f32), shape((near, chunk), bf16)],
            2 * survivors * half * chunk,
        )
        for c, chunk in enumerate(chunks)
    ]
    far = trade(even, n // 2)
    (gathered,) = call(
        gather_kernel,
        "gather",
        (even, far, products[1][1]),
        [shape((n // 2 * rows - rows, even.shape[1]), bf16)],
        1500 * affine_matrix.size,
        in_specs=[VMEM] * 2 + [ANY],
    )
    odd = trade(gathered, 1)
    kept = [product[0] for product in products]
    arrived = [trade(product[1], masks[c][0]) for c, product in enumerate(products)]
    lines_left = near // 2
    for c, chunk in enumerate(chunks):
        keep, sent = call(
            hop_sum_kernel,
            "hop_sum",
            (kept[c], arrived[c], kept[0] if c else products[1][1]),
            [shape((lines_left, chunk), f32), shape((lines_left, chunk), bf16)],
            near * chunk,
            in_specs=[VMEM] * 2 + [ANY],
        )
        kept[c], arrived[c] = keep, trade(sent, masks[c][1])

    context, columns = call(
        functools.partial(attention_kernel, n, kv_heads, masks[0]),
        "attention",
        (queries, even, far, pair, odd, kept[0]),
        [shape(queries.shape, f32), shape((n, rows), f32)],
        4 * rows * n * rows * queries.shape[1],
        limit=32,
        in_specs=[VMEM] * 5 + [ANY],
    )

    def column_sum(pieces, after, scale=1.0, remote=0):
        (total,) = call(
            functools.partial(column_sum_kernel, scale),
            "column_sum",
            (after, *pieces),
            [shape(pieces[0].shape, f32)],
            0,
            in_specs=[ANY] + [VMEM] * len(pieces),
            remote=remote,
        )
        return total

    pieces = [columns[i * (n // 4) : (i + 1) * (n // 4)] for i in range(4)]
    pieces = pieces[:1] + [trade(x, mask) for x, mask in zip(pieces[1:], (2, 1, 3))]
    for mask in rest:
        lines_left //= 2
        keep, sent = call(
            hop_sum_both_kernel,
            "hop_sum_both",
            (*kept, *arrived),
            [shape((lines_left, width), f32), shape((lines_left, width), bf16)],
            lines_left * width,
        )
        kept, arrived = [keep], [trade(sent, mask)]
        columns = column_sum(pieces, keep)
        left = columns.shape[0] // 2
        own, far = columns[:left], columns[left:]
        pieces = [own, trade(far, mask)]
        if mask == rest[-1]:
            pieces += [swap(own), trade_across(far, mask)]

    triples, scores = call(
        finish_kernel,
        "finish",
        (affine_offset_vector.reshape(1, width), kept[0], arrived[0], *pieces),
        [shape((lines, width), f32), shape((1, rows), f32)],
        n * lines * width,
    )
    return (context, scores.reshape(rows), triples)


def solution(mesh):
    in_specs = (
        P(("grp", "seq"), "ten"),
        P(("grp", "seq"), "ten"),
        P(("grp", "seq"), "ten"),
        P(("grp", "seq"), None),
        P(),
        P(("grp", "seq")),
        P("grp"),
        P("seq", "ten"),
        P("ten"),
    )
    out_specs = (P(("grp", "seq"), "ten"), P(("grp", "seq")), P(("grp", "seq"), "ten"))
    return jax.shard_map(shards, mesh=mesh, in_specs=in_specs, out_specs=out_specs, check_vma=False)
```

```python
import functools
import math

import jax
import jax.numpy as jnp
from jax import lax
from jax.experimental import pallas as pl
from jax.experimental.pallas import tpu as pltpu
from jax.sharding import PartitionSpec as P

HEAD_SIZE = 128
QUERY_HEADS = 32
VMEM = pl.BlockSpec(memory_space=pltpu.VMEM)
ANY = pl.BlockSpec(memory_space=pl.ANY)
MIB = 1024 * 1024


def call(body, name, inputs, outputs, flops, limit=16, in_specs=None, scratch=(), remote=0, out_specs=None):
    inputs = [pltpu.with_memory_space_constraint(x, pltpu.HBM) if i < remote else x for i, x in enumerate(inputs)]
    size = sum(math.prod(x.shape) * x.dtype.itemsize for x in list(inputs) + list(outputs))
    return pl.pallas_call(
        body,
        out_shape=list(outputs),
        in_specs=in_specs or [VMEM] * len(inputs),
        out_specs=out_specs or [VMEM] * len(outputs),
        scratch_shapes=list(scratch),
        compiler_params=pltpu.CompilerParams(vmem_limit_bytes=limit * MIB),
        cost_estimate=pl.CostEstimate(flops=flops, bytes_accessed=size, transcendentals=0),
        name=name,
    )(*inputs)


def norm_select_kernel(n, hidden_in, gain_in, kept_in, keys_in, values_in, *refs):
    outs, (hidden, gain, kept, pair, sems) = refs[:n], refs[n:]
    rows, width = hidden.shape
    block = width // n
    half = block // 2
    pieces = 4
    piece = width // pieces
    key_width = keys_in.shape[1]
    loads = [
        pltpu.make_async_copy(
            hidden_in.at[:, i * piece : (i + 1) * piece], hidden.at[:, i * piece : (i + 1) * piece], sems.at[i]
        )
        for i in range(pieces)
    ]
    loads += [
        pltpu.make_async_copy(gain_in, gain, sems.at[pieces]),
        pltpu.make_async_copy(kept_in, kept, sems.at[pieces + 1]),
        pltpu.make_async_copy(keys_in, pair.at[:, :key_width], sems.at[pieces + 2]),
        pltpu.make_async_copy(values_in, pair.at[:, key_width:], sems.at[pieces + 3]),
    ]
    for load in loads:
        load.start()
    s, t = lax.axis_index("seq"), lax.axis_index("ten")
    step = min(piece, 1024)
    total = jnp.zeros((rows, step), jnp.float32)
    for i in range(pieces):
        loads[i].wait()
        for j in range(i * piece, (i + 1) * piece, step):
            part = hidden[:, j : j + step].astype(jnp.float32)
            total += part * part
    scale = lax.rsqrt(jnp.sum(total, axis=1, keepdims=True) / width + 1e-06)
    for load in loads[pieces:]:
        load.wait()
    selector = (kept[...] == lax.broadcasted_iota(jnp.int32, (rows, rows), 0)).astype(jnp.bfloat16)
    for k in range(n):
        start = pl.multiple_of(lax.bitwise_xor(s, k) * block + t * half, half)
        columns = pl.ds(start, half)
        normed = (hidden[:, columns].astype(jnp.float32) * scale * gain[:, columns]).astype(jnp.bfloat16)
        if outs[k].shape[1] > half:
            outs[k][:, half:] = pair[...]
        outs[k][:, :half] = lax.dot_general(
            selector, normed, (((0,), (0,)), ((), ())), preferred_element_type=jnp.float32
        ).astype(jnp.bfloat16)


def gather_kernel(near, far, after, out):
    rows = near.shape[0] + far.shape[0] - out.shape[0]
    out[: near.shape[0] - rows] = near[rows:]
    out[near.shape[0] - rows :] = far[...]


def relay_kernel(count, *refs):
    blocks, outs = refs[:count], refs[len(refs) - count :]
    for block, out in zip(blocks, outs):
        out[...] = block[...]


def stage_kernel(n, counts_in, matrix_in, queries_in, *refs):
    matrix, queries, target, counts, sems = refs[-5:]
    loads = [
        pltpu.make_async_copy(counts_in, counts, sems.at[0]),
        pltpu.make_async_copy(matrix_in, matrix, sems.at[1]),
        pltpu.make_async_copy(queries_in, queries, sems.at[2]),
    ]
    for load in loads:
        load.start()
    rows = target.shape[1] // n
    s = lax.axis_index("seq")
    loads[0].wait()
    slot_all = lax.broadcasted_iota(jnp.int32, (1, n * rows), 1)
    found = jnp.full((1, n * rows), -1, jnp.int32)
    for k in range(n):
        source = lax.bitwise_xor(s, k)
        begin = jnp.int32(0)
        for i in range(n):
            begin += jnp.where(i < source, counts[i], 0)
        slot = slot_all - k * rows
        inside = (slot >= 0) & (slot < counts[source])
        found = jnp.where(inside, begin + slot, found)
    target[...] = found
    for load in loads[1:]:
        load.wait()


def compact_kernel(n, target, *refs):
    blocks, (out, even, pair) = refs[:n], refs[n:]
    pair[...] = blocks[1][:, out.shape[1] :]
    rows, half = blocks[0].shape[0], out.shape[1]
    for i in range(n // 4):
        even[i * rows : (i + 1) * rows] = blocks[2 * i][:, half:]
    lines = out.shape[0] // n
    s = lax.axis_index("seq")
    received = jnp.concatenate([b[:, :half] for b in blocks], axis=0)
    line = lax.broadcasted_iota(jnp.int32, (lines, received.shape[0]), 0)
    pick = jnp.concatenate(
        [(line + lax.bitwise_xor(s, k) * lines == target[...]).astype(jnp.float32) for k in range(n)], axis=0
    ).astype(jnp.bfloat16)
    out[...] = jnp.dot(pick, received, preferred_element_type=jnp.float32).astype(jnp.bfloat16)


def halving_order(n, masks):
    return sorted(range(n), key=lambda k: [k & mask for mask in masks])


def project_own_kernel(own, matrix, out):
    half = own.shape[1]
    mine = pl.ds(pl.multiple_of(lax.axis_index("ten") * half, half), half)
    tile = out.shape[1] // 4 if out.shape[1] % 512 == 0 else out.shape[1]
    for j in range(0, out.shape[1], tile):
        out[:, j : j + tile] = jnp.dot(own[...], matrix[mine, j : j + tile], preferred_element_type=jnp.float32)


def project_kernel(first, order, product, other, matrix, near, far):
    survivors, half = other.shape
    lines = survivors // len(order)
    width = near.shape[1]
    t = lax.axis_index("ten")
    others = pl.ds(pl.multiple_of((1 - t) * half, half), half)
    tile = width // 2 if width % 256 == 0 else width
    for j in range(0, width, tile):
        lanes = slice(first + j, first + j + tile)
        part = product[:, lanes]
        part += jnp.dot(other[...], matrix[others, lanes], preferred_element_type=jnp.float32)
        for i, k in enumerate(order):
            block = part[k * lines : (k + 1) * lines]
            if i < len(order) // 2:
                near[i * lines : (i + 1) * lines, j : j + tile] = block
            else:
                i -= len(order) // 2
                far[i * lines : (i + 1) * lines, j : j + tile] = block.astype(jnp.bfloat16)


def hop_sum_kernel(kept, received, after, keep, sent):
    rows = keep.shape[0]
    total = kept[...] + received[...].astype(jnp.float32)
    keep[...] = total[:rows]
    sent[...] = total[rows:].astype(jnp.bfloat16)


def hop_sum_both_kernel(*refs):
    *parts, keep, sent = refs
    count = len(parts) // 2
    rows = keep.shape[0]
    first = 0
    for c in range(count):
        lanes = slice(first, first + parts[c].shape[1])
        first = lanes.stop
        total = parts[c][...] + parts[count + c][...].astype(jnp.float32)
        keep[:, lanes] = total[:rows]
        sent[:, lanes] = total[rows:].astype(jnp.bfloat16)


def column_sum_kernel(scale, after, *refs):
    *parts, out = refs
    total = parts[0][...]
    for part in parts[1:]:
        total += part[...]
    out[...] = total * scale


def attention_kernel(n, kv_heads, masks, queries, near, far, pair, odd, after, context, columns):
    rows = queries.shape[0]
    group = queries.shape[1] // (HEAD_SIZE * kv_heads)
    s = lax.axis_index("seq")
    keys_total = n * rows
    column = lax.broadcasted_iota(jnp.int32, (1, keys_total), 1)
    position = column
    order = list(range(0, n, 2)) + list(range(1, n, 2))
    for at, k in enumerate(order):
        inside = (column >= at * rows) & (column < (at + 1) * rows)
        position = jnp.where(inside, column + (lax.bitwise_xor(s, k) - s - at) * rows, position)
    row = lax.rem(lax.broadcasted_iota(jnp.int32, (group * rows, keys_total), 0), rows)
    allowed = position <= row
    sums = jnp.zeros((1, keys_total), jnp.float32)
    for g in range(kv_heads):
        key_lanes = slice(g * HEAD_SIZE, (g + 1) * HEAD_SIZE)
        value_lanes = slice((kv_heads + g) * HEAD_SIZE, (kv_heads + g + 1) * HEAD_SIZE)
        key, value = [
            jnp.concatenate([block[:, x] for block in (near, far, pair, odd)], axis=0)
            for x in (key_lanes, value_lanes)
        ]
        heads = range(g * group, (g + 1) * group)
        stacked = jnp.concatenate([queries[:, h * HEAD_SIZE : (h + 1) * HEAD_SIZE] for h in heads], axis=0)
        scores = lax.dot_general(
            stacked, key, (((1,), (1,)), ((), ())), preferred_element_type=jnp.float32
        ) * HEAD_SIZE ** (-0.5)
        scores = jnp.where(allowed, scores, -1e30)
        weights = jnp.exp(scores - jnp.max(scores, axis=1, keepdims=True))
        inverse = 1.0 / jnp.sum(weights, axis=1, keepdims=True)
        mixed = jnp.dot(weights.astype(jnp.bfloat16), value, preferred_element_type=jnp.float32) * inverse
        for i, h in enumerate(heads):
            context[:, h * HEAD_SIZE : (h + 1) * HEAD_SIZE] = mixed[i * rows : (i + 1) * rows]
        sums += jnp.sum(weights * inverse, axis=0, keepdims=True)
    for i, k in enumerate(halving_order(n, masks)):
        at = order.index(k)
        columns[i : i + 1, :] = sums[:, at * rows : (at + 1) * rows]


def finish_kernel(bias, kept, received, *refs):
    *parts, out, scores, total, sems = refs
    pieces = sems.shape[0]
    width = total.shape[1] // pieces
    stores = []
    for i in range(pieces):
        lanes = slice(i * width, (i + 1) * width)
        total[:, lanes] = kept[:, lanes] + received[:, lanes].astype(jnp.float32) + bias[:, lanes]
        stores.append(pltpu.make_async_copy(total.at[:, lanes], out.at[:, lanes], sems.at[i]))
        stores[i].start()
    columns = parts[0][...]
    for part in parts[1:]:
        columns += part[...]
    scores[...] = columns / QUERY_HEADS
    for store in stores:
        store.wait()


def shards(queries, keys, values, hidden, norm_gain, retained_lists, counts, affine_matrix, affine_offset_vector):
    n = lax.axis_size("seq")
    rows, model = hidden.shape
    kv_heads = keys.shape[1] // HEAD_SIZE
    half = affine_matrix.shape[0] // 2
    width = affine_matrix.shape[1]
    survivors = n * rows // 2
    lines = survivors // n
    cut = width // 2
    chunks = [cut, width - cut]
    near = survivors // 2
    f32, bf16, i32 = jnp.float32, jnp.bfloat16, jnp.int32
    shape = jax.ShapeDtypeStruct
    dma = pltpu.SemaphoreType.DMA

    def trade(x, k):
        return lax.ppermute(x, "seq", [(i, i ^ k) for i in range(n)])

    def trade_across(x, k):
        return lax.ppermute(x, ("seq", "ten"), [(2 * i + t, 2 * (i ^ k) + 1 - t) for i in range(n) for t in range(2)])

    def swap(x):
        return lax.ppermute(x, "ten", [(0, 1), (1, 0)])

    chosen = call(
        functools.partial(norm_select_kernel, n),
        "norm_select",
        (hidden, norm_gain.reshape(1, model), retained_lists.reshape(1, rows), keys, values),
        [shape((rows, half + (2 * keys.shape[1] if k == 1 or k in range(0, n // 2, 2) else 0)), bf16) for k in range(n)],
        4 * rows * model,
        limit=16,
        in_specs=[ANY] * 5,
        remote=5,
        scratch=[pltpu.VMEM((rows, model), bf16), pltpu.VMEM((1, model), f32), pltpu.VMEM((1, rows), i32), pltpu.VMEM((rows, 2 * keys.shape[1]), bf16), dma((8,))],
    )
    received = {0: chosen[0]}
    received.update({k: trade(chosen[k], k) for k in [1, *range(n // 2, n)]})
    relayed = call(
        functools.partial(relay_kernel, n // 2 - 2),
        "relay",
        (*chosen[2 : n // 2], received[1]),
        [shape(x.shape, bf16) for x in chosen[2 : n // 2]],
        0,
        in_specs=[VMEM] * (n // 2 - 2) + [ANY],
    )
    received.update({k: trade(x, k) for k, x in zip(range(2, n // 2), relayed)})
    received = [received[k] for k in range(n)]
    matrix, queries, target = call(
        functools.partial(stage_kernel, n),
        "stage",
        (counts, affine_matrix, queries, *received[n // 2 : n // 2 + 2]),
        [shape(affine_matrix.shape, bf16), shape(queries.shape, bf16), shape((1, n * rows), i32)],
        1500 * affine_matrix.size,
        in_specs=[ANY] * 5,
        remote=3,
        scratch=[pltpu.SMEM(counts.shape, i32), dma((3,))],
    )
    own, even, pair = call(
        functools.partial(compact_kernel, n),
        "compact",
        (target, *received),
        [shape((survivors, half), bf16)] + [shape((x * rows, 2 * keys.shape[1]), bf16) for x in (n // 4, 1)],
        2 * survivors * n * rows * half,
    )
    other = swap(own)
    rest = [1 << i for i in range(2, n.bit_length() - 1)]
    masks = [[1, 2] + rest, [2, 1] + rest]
    (product,) = call(
        project_own_kernel,
        "project_own",
        (own, matrix),
        [shape((survivors, width), f32)],
        2 * survivors * half * width,
    )
    products = [
        call(
            functools.partial(project_kernel, c * cut, halving_order(n, masks[c])),
            "project",
            (product, other, matrix),
            [shape((near, chunk), f32), shape((near, chunk), bf16)],
            2 * survivors * half * chunk,
        )
        for c, chunk in enumerate(chunks)
    ]
    far = trade(even, n // 2)
    (gathered,) = call(
        gather_kernel,
        "gather",
        (even, far, products[1][1]),
        [shape((n // 2 * rows - rows, even.shape[1]), bf16)],
        1500 * affine_matrix.size,
        in_specs=[VMEM] * 2 + [ANY],
    )
    odd = trade(gathered, 1)
    kept = [product[0] for product in products]
    arrived = [trade(product[1], masks[c][0]) for c, product in enumerate(products)]
    lines_left = near // 2
    for c, chunk in enumerate(chunks):
        keep, sent = call(
            hop_sum_kernel,
            "hop_sum",
            (kept[c], arrived[c], kept[0] if c else products[1][1]),
            [shape((lines_left, chunk), f32), shape((lines_left, chunk), bf16)],
            near * chunk,
            in_specs=[VMEM] * 2 + [ANY],
        )
        kept[c], arrived[c] = keep, trade(sent, masks[c][1])

    context, columns = call(
        functools.partial(attention_kernel, n, kv_heads, masks[0]),
        "attention",
        (queries, even, far, pair, odd, kept[0]),
        [shape(queries.shape, f32), shape((n, rows), f32)],
        4 * rows * n * rows * queries.shape[1],
        limit=32,
        in_specs=[VMEM] * 5 + [ANY],
    )

    def column_sum(pieces, after, scale=1.0, remote=0):
        (total,) = call(
            functools.partial(column_sum_kernel, scale),
            "column_sum",
            (after, *pieces),
            [shape(pieces[0].shape, f32)],
            0,
            in_specs=[ANY] + [VMEM] * len(pieces),
            remote=remote,
        )
        return total

    pieces = [columns[i * (n // 4) : (i + 1) * (n // 4)] for i in range(4)]
    pieces = pieces[:1] + [trade(x, mask) for x, mask in zip(pieces[1:], (2, 1, 3))]
    for mask in rest:
        lines_left //= 2
        keep, sent = call(
            hop_sum_both_kernel,
            "hop_sum_both",
            (*kept, *arrived),
            [shape((lines_left, width), f32), shape((lines_left, width), bf16)],
            lines_left * width,
        )
        kept, arrived = [keep], [trade(sent, mask)]
        columns = column_sum(pieces, keep)
        left = columns.shape[0] // 2
        own, far = columns[:left], columns[left:]
        pieces = [own, trade(far, mask)]
        if mask == rest[-1]:
            pieces += [swap(own), trade_across(far, mask)]

    triples, scores = call(
        finish_kernel,
        "finish",
        (affine_offset_vector.reshape(1, width), kept[0], arrived[0], *pieces),
        [shape((lines, width), f32), shape((1, rows), f32)],
        n * lines * width,
        scratch=[pltpu.VMEM((lines, width), f32), dma((4 if width % 512 == 0 else 1,))],
        out_specs=[ANY, VMEM],
    )
    return (context, scores.reshape(rows), triples)


def solution(mesh):
    in_specs = (
        P(("grp", "seq"), "ten"),
        P(("grp", "seq"), "ten"),
        P(("grp", "seq"), "ten"),
        P(("grp", "seq"), None),
        P(),
        P(("grp", "seq")),
        P("grp"),
        P("seq", "ten"),
        P("ten"),
    )
    out_specs = (P(("grp", "seq"), "ten"), P(("grp", "seq")), P(("grp", "seq"), "ten"))
    return jax.shard_map(shards, mesh=mesh, in_specs=in_specs, out_specs=out_specs, check_vma=False)
```
